32 devices in a mesh: ctx: 8 (over y, x, core), fsdp: 4 (over z).
Axes of the slice: x: 2, y: 2, z: 4, core: 2. Of those that a mesh axis runs over, the one named last changes fastest.
Arguments:
- tokens: bfloat16 [4, 1024, 2048], P('fsdp', 'ctx'), may hold values from -6 to 6
- gain_attn: bfloat16 [2048], P(('ctx', 'fsdp')), may hold values from 0.5 to 1.5
- w_qkv: bfloat16 [2048, 6144], P(('ctx', 'fsdp')), may hold values from -0.1875 to 0.1875
- w_out: bfloat16 [2048, 2048], P(('ctx', 'fsdp')), may hold values from -0.5 to 0.5
- gain_ffn: bfloat16 [2048], P(('ctx', 'fsdp')), may hold values from 0.5 to 1.5
- w_router: bfloat16 [2048, 64], P(('ctx', 'fsdp')), may hold values from -0.0625 to 0.0625
- w_shared_in: bfloat16 [2048, 5632], P(('ctx', 'fsdp')), may hold values from -0.125 to 0.125
- w_shared_down: bfloat16 [2816, 2048], P(('ctx', 'fsdp')), may hold values from -0.109375 to 0.109375
- w_expert_in: bfloat16 [128, 2048, 1408], P(('ctx', 'fsdp')), may hold values from -0.125 to 0.125
- w_expert_down: bfloat16 [128, 704, 2048], P(('ctx', 'fsdp')), may hold values from -0.15625 to 0.15625
- routes: int32 [4, 1024, 6], P('fsdp', 'ctx'), may hold values from 0 to 63, all different within a row; in each aligned block of 128 rows (0 to 127, 128 to 255, ..., all dimensions but the last counted through in order) at most 20 rows name the same one
- plan: int32 [16], replicated, may hold values from 0 to 15, each once
- cotangent: bfloat16 [4, 1024, 2048], P('fsdp', 'ctx'), may hold values from -6 to 6
Outputs:
- result: bfloat16 [4, 1024, 2048], P('fsdp', 'ctx')
- tokens_grad: float32 [4, 1024, 2048], P('fsdp', 'ctx')
- gain_attn_grad: float32 [2048], P(('ctx', 'fsdp'))
- qkv_grad: float32 [2048, 6144], P(('ctx', 'fsdp'))
- out_grad: float32 [2048, 2048], P(('ctx', 'fsdp'))
- gain_ffn_grad: float32 [2048], P(('ctx', 'fsdp'))
- router_grad: float32 [2048, 64], P(('ctx', 'fsdp'))
- shared_in_grad: float32 [2048, 5632], P(('ctx', 'fsdp'))
- shared_down_grad: float32 [2816, 2048], P(('ctx', 'fsdp'))
- expert_in_grad: float32 [128, 2048, 1408], P(('ctx', 'fsdp'))
- expert_down_grad: float32 [128, 704, 2048], P(('ctx', 'fsdp'))
The draws below stay inside these ranges and needn't reach their ends.
Inputs may be any that keep to these rules, and one draw needn't show every extreme that they name: `routes`: each token names 6 different experts; among the rows of one device (aligned blocks of 128 tokens) no expert is named more than 20 times, a bound that some block reaches. `plan`: each half-block of positions once.
All inputs are finite; a program needn't handle non-finite values.
Results may differ from the reference program's by a relative error of at most 0.022.
Values may be sent and summed in bfloat16 or wider, within the bound.
No kernel may reach another device: no remote copies, remote signals or barrier semaphores. Data moves between devices by JAX's collectives and lax.ppermute only.
A program may use at most 512 MiB of HBM per device.

```python
import math
import jax
import jax.numpy as jnp
import numpy as np
from jax import lax

D = 2048
HEADS = 16
HEAD = 128
FFE = 1408
EXPERTS = 64
TOP = 6
TOK_DEV = 128
CAP = 20
SH = 2816
HALF = 704
LENGTH = 1024
SEQS = 4
N_CTX = 8


def shard_levels(own_key, extent, split, low, largest):
    level = 1.0
    for position, blocks in split:
        draws = jax.random.uniform(jax.random.fold_in(jax.random.fold_in(own_key, 6), position), (blocks,), jnp.float32, low / len(split), largest / len(split))
        level = level * jnp.repeat(jnp.exp(draws), extent[position] // blocks).reshape((-1,) + (1,) * (len(extent) - 1 - position))
    return level


def assign_block(rng, own, number, rows, number_of, top, bound, skew):
    sequence = jax.random.permutation(rng, number_of)
    crowded, common = load_shares(number_of, rows * top, bound, skew, True), load_shares(number_of, rows * top, bound, skew, False)
    places = jnp.arange(number_of)

    def named(sizes, rotation):
        used = int((sizes > 0).sum())
        fixed = max(1, used // 4)
        passed = fixed + (places - fixed + rotation * (used - fixed)) % max(1, number_of - fixed)
        return jnp.zeros((number_of,), jnp.int32).at[sequence[jnp.where(places < fixed, places, passed)]].set(jnp.asarray(sizes, jnp.int32))

    sizes = jnp.where(number % 4 == 0, named(crowded, number // 4), named(common, number - number // 4 - 1))
    mixed = jax.random.permutation(jax.random.fold_in(own, 3), number_of)
    donor, sink = mixed[0:number_of // 2 * 2:2], mixed[1:number_of // 2 * 2:2]
    room = jnp.minimum(sizes[donor] - 1, bound - sizes[sink]) // 2
    room = jnp.where((donor == sequence[0]) | (sink == sequence[0]) | (sizes[sink] == 0), 0, jnp.maximum(room, 0))
    passed = jax.random.randint(jax.random.fold_in(own, 4), (number_of // 2,), 0, 1 << 20) % (room + 1)
    sizes = sizes.at[donor].add(-passed).at[sink].add(passed)
    items = jnp.searchsorted(jnp.cumsum(sizes), jnp.arange(rows * top), side="right").astype(jnp.int32)
    listing = items.reshape(top, rows).T
    listing = listing[jax.random.permutation(jax.random.fold_in(own, 1), rows)]
    rotation = jax.random.randint(jax.random.fold_in(own, 2), (rows, 1), 0, top)
    return jnp.take_along_axis(listing, (jnp.arange(top)[None, :] + rotation) % top, axis=1)


def load_shares(count, total, limit, slope, full):
    weights = [(1 << 20) // math.isqrt(standing ** slope) + 1 for standing in range(1, count + 1)]
    largest = limit if full else min(limit, max(-(-total // count), total * weights[0] // sum(weights)))
    least = 1 if total - largest >= count - 1 else 0
    given, rest = [largest] + [least] * (count - 1), total - largest - least * (count - 1)
    while rest > 0:
        free = [i for i in range(1, count) if given[i] < largest] or [i for i in range(1, count) if given[i] < limit]
        pool, budget = sum([weights[i] for i in free]), rest
        for i in free:
            extra = min(limit - given[i], max(1, budget * weights[i] // pool), rest)
            given[i] = given[i] + extra
            rest = rest - extra
    return np.array(given)


def centred(key, shape, deviation, reach, cuts=(), kind=jnp.bfloat16):
    array = jax.random.normal(key, shape, jnp.float32) * deviation
    if len(cuts) > 0:
        array = shard_levels(key, shape, cuts, -0.22, 0.18) * array
    return jnp.clip(array, min=-reach, max=reach).astype(kind)


def setup_inputs(seed: int = 0) -> dict:
    arg_keys = jax.random.split(jax.random.key(seed), 14)
    tokens = centred(arg_keys[0], (SEQS, LENGTH, D), 1.0, 6.0, ((0, 4), (1, 8)))
    gain_attn = jnp.clip(1.0 + 0.1 * jax.random.normal(arg_keys[1], (D,), jnp.float32), 0.5, 1.5).astype(jnp.bfloat16)
    w_qkv = centred(arg_keys[2], (D, 3 * D), (D // 2) ** -0.5, 0.1875, ((0, 32),))
    w_out = centred(arg_keys[3], (D, D), (D // 16) ** -0.5, 0.5, ((0, 32),))
    gain_ffn = jnp.clip(1.0 + 0.1 * jax.random.normal(arg_keys[4], (D,), jnp.float32), 0.5, 1.5).astype(jnp.bfloat16)
    w_router = centred(arg_keys[5], (D, EXPERTS), (4 * D) ** -0.5, 0.0625, ((0, 32),))
    w_shared_in = centred(arg_keys[6], (D, 2 * SH), D ** -0.5, 0.125, ((0, 32),))
    w_shared_down = centred(arg_keys[7], (SH, D), SH ** -0.5, 0.109375, ((0, 32),))
    w_expert_in = centred(arg_keys[8], (2 * EXPERTS, D, 2 * HALF), D ** -0.5, 0.125, ((0, 32),))
    w_expert_down = centred(arg_keys[9], (2 * EXPERTS, HALF, D), FFE ** -0.5, 0.15625, ((0, 32),))
    routes_keys = jax.random.split(jax.random.fold_in(arg_keys[10], 1), SEQS * LENGTH // TOK_DEV)
    routes_turns = jax.random.permutation(jax.random.fold_in(arg_keys[10], 3), SEQS * LENGTH // TOK_DEV)
    routes = jax.vmap(lambda own, number: assign_block(jax.random.fold_in(arg_keys[10], 2), own, number, TOK_DEV, EXPERTS, TOP, CAP, 0))(routes_keys, routes_turns).reshape((SEQS, LENGTH, TOP))
    plan = jax.random.permutation(arg_keys[11], 2 * N_CTX).astype(jnp.int32)
    cotangent = centred(arg_keys[12], (SEQS, LENGTH, D), 1.0, 6.0, ((0, 4), (1, 8)))
    return dict(tokens=tokens, gain_attn=gain_attn, w_qkv=w_qkv, w_out=w_out, gain_ffn=gain_ffn, w_router=w_router, w_shared_in=w_shared_in, w_shared_down=w_shared_down, w_expert_in=w_expert_in, w_expert_down=w_expert_down, routes=routes, plan=plan, cotangent=cotangent)


EPSILON = 1e-06
ROPE_BASE = 10000.0
NEGATIVE = -1e+30

@jax.custom_vjp
def low(v):
    return lax.optimization_barrier(v.astype(jnp.bfloat16)).astype(jnp.float32)

@jax.custom_vjp
def low_back(v):
    return v

def low_keep(v):
    return (low(v), None)

def low_pass(kept, grad):
    return (grad,)

def back_keep(v):
    return (v, None)

def back_low(kept, grad):
    return (low(grad),)
low.defvjp(low_keep, low_pass)
low_back.defvjp(back_keep, back_low)

def product(left, right):
    return jnp.dot(left, right, precision=lax.Precision.HIGHEST, preferred_element_type=jnp.float32)

def rms_scale(values, gain):
    inverse = lax.rsqrt(lax.optimization_barrier(jnp.mean(values * values, axis=-1, keepdims=True)) + EPSILON)
    return values * inverse * gain

def gating(joined):
    half_size = joined.shape[-1] // 2
    return jax.nn.silu(joined[..., :half_size]) * joined[..., half_size:]

def rotate(values, places, head_count):
    amount, model_width = values.shape
    head_size = model_width // head_count
    half_size = head_size // 2
    frequency = ROPE_BASE ** (-2.0 * jnp.arange(half_size, dtype=jnp.float32) / head_size)
    angles = places.astype(jnp.float32)[:, None] * frequency[None, :]
    cosine = jnp.cos(angles)[:, None, :]
    sine_part = jnp.sin(angles)[:, None, :]
    split_heads = values.reshape(amount, head_count, head_size)
    first_part = split_heads[..., :half_size]
    second = split_heads[..., half_size:]
    turned = jnp.concatenate([first_part * cosine - second * sine_part, second * cosine + first_part * sine_part], axis=-1)
    return turned.reshape(amount, model_width)

def half_expert(row_block, weight_in, weight_down):
    row_block = low_back(row_block)
    joined = low_back(product(row_block, weight_in))
    return low(product(low(gating(joined)), weight_down))

def expert_pair(packed):
    row_block, in_first, in_second, down_first, down_second = packed
    return low(half_expert(row_block, in_first, down_first) + half_expert(row_block, in_second, down_second))

def reference(tokens, gain_attn, w_qkv, w_out, gain_ffn, w_router, w_shared_in, w_shared_down, w_expert_in, w_expert_down, routes, plan, cotangent):
    amount = SEQS * LENGTH
    half_block = TOK_DEV // 2
    row_ids = jnp.arange(LENGTH, dtype=jnp.int32)
    places = plan[row_ids // half_block] * half_block + row_ids % half_block
    visible = places[None, :] <= places[:, None]
    seq_places = jnp.tile(places, SEQS)
    blocks = amount // TOK_DEV
    per_block = routes.reshape(blocks, TOK_DEV * TOP)
    matches = (per_block[:, :, None] == jnp.arange(EXPERTS, dtype=jnp.int32)[None, None, :]).astype(jnp.int32)
    ranking = lax.optimization_barrier(jnp.sum((jnp.cumsum(matches, axis=1) - matches) * matches, axis=2))
    slot_index = per_block * (blocks * CAP) + jnp.arange(blocks, dtype=jnp.int32)[:, None] * CAP + ranking
    token_ids = jnp.repeat(jnp.arange(amount, dtype=jnp.int32), TOP)
    slot_token = jnp.full((EXPERTS * blocks * CAP,), amount, dtype=jnp.int32).at[slot_index.reshape(-1)].set(token_ids).reshape(EXPERTS, blocks * CAP)
    route_slot = slot_index.reshape(amount, TOP)
    chosen_mask = (routes.reshape(amount, TOP)[:, :, None] == jnp.arange(EXPERTS, dtype=jnp.int32)[None, None, :]).astype(jnp.float32)

    def one_head(packed):
        query, key, value = packed
        scores = low_back(product(query, key.T) * HEAD ** (-0.5))
        scores = jnp.where(visible, scores, NEGATIVE)
        row_top = lax.optimization_barrier(jnp.max(scores, axis=1, keepdims=True))
        weights_exp = jnp.where(visible, jnp.exp(scores - row_top), 0.0)
        row_total = lax.optimization_barrier(jnp.sum(weights_exp, axis=1, keepdims=True))
        return low_back(product(low(weights_exp), value)) / row_total

    def one_sequence(packed):
        return lax.map(jax.checkpoint(one_head), packed)

    def split_heads(values):
        return values.reshape(SEQS, LENGTH, HEADS, HEAD).transpose(0, 2, 1, 3)

    def layer(inputs, gain_one, weight_qkv, weight_out, gain_two, weight_router, shared_in, shared_down, expert_in, expert_down):
        flattened = inputs.reshape(amount, D)
        normed = low(rms_scale(flattened, gain_one))
        projected = low_back(product(normed, weight_qkv))
        query = low(rotate(projected[:, :D], seq_places, HEADS))
        key = low(rotate(projected[:, D:2 * D], seq_places, HEADS))
        value = low(projected[:, 2 * D:])
        head_out = lax.map(one_sequence, (split_heads(query), split_heads(key), split_heads(value)))
        mixed_out = head_out.transpose(0, 2, 1, 3).reshape(amount, D)
        mixed_out = low_back(low(mixed_out))
        residual = flattened + low_back(product(mixed_out, weight_out))
        ffn_in = low(rms_scale(residual, gain_two))
        logits = low_back(product(ffn_in, weight_router))
        chosen = lax.optimization_barrier(jnp.sum(chosen_mask * logits[:, None, :], axis=2))
        gate_weights = jax.nn.softmax(chosen, axis=1)
        shared = product(low(gating(low_back(product(ffn_in, shared_in)))), shared_down)
        padded = jnp.concatenate([ffn_in, jnp.zeros((1, D), jnp.float32)], axis=0)
        gathered = low_back(padded[slot_token])
        expert_outs = lax.map(jax.checkpoint(expert_pair), (gathered, expert_in[:EXPERTS], expert_in[EXPERTS:], expert_down[:EXPERTS], expert_down[EXPERTS:]))
        expert_outs = low_back(expert_outs)
        picked = expert_outs.reshape(-1, D)[route_slot]
        routed = lax.optimization_barrier(jnp.sum(gate_weights[:, :, None] * picked, axis=1))
        return (residual + shared + routed).reshape(SEQS, LENGTH, D)
    floats = (tokens.astype(jnp.float32), gain_attn.astype(jnp.float32), w_qkv.astype(jnp.float32), w_out.astype(jnp.float32), gain_ffn.astype(jnp.float32), w_router.astype(jnp.float32), w_shared_in.astype(jnp.float32), w_shared_down.astype(jnp.float32), w_expert_in.astype(jnp.float32), w_expert_down.astype(jnp.float32))
    output, pullback = jax.vjp(layer, *floats)
    grads = pullback(cotangent.astype(jnp.float32))
    return (output.astype(jnp.bfloat16), grads[0], grads[1], grads[2], grads[3], grads[4], grads[5], grads[6], grads[7], grads[8], grads[9])
```

```python
import functools

import jax
import jax.numpy as jnp
from jax import lax
from jax.experimental import pallas as pl
from jax.experimental.pallas import tpu as pltpu
from jax.sharding import PartitionSpec as P

HEADS = 16
EXPERTS = 64
CAP = 20
BLOCK = 128
GROUP = 4
VMEM = 60 * 1024 * 1024

EPSILON = 1e-06
ROPE_BASE = 10000.0
NEGATIVE = -1e30
BOTH = ("ctx", "fsdp")


def rms_scale(values, gain):
    inverse = lax.rsqrt(jnp.mean(values * values, axis=-1, keepdims=True) + EPSILON)
    return values * inverse * gain


def rotate(values, places, head_count):
    amount, width = values.shape
    head_size = width // head_count
    half_size = head_size // 2
    frequency = ROPE_BASE ** (-2.0 * jnp.arange(half_size, dtype=jnp.float32) / head_size)
    angles = places.astype(jnp.float32)[:, None] * frequency[None, :]
    cosine = jnp.cos(angles)
    sine = jnp.sin(angles)
    turned = []
    for head in range(head_count):
        first = values[:, head * head_size : head * head_size + half_size]
        second = values[:, head * head_size + half_size : (head + 1) * head_size]
        turned += [first * cosine - second * sine, second * cosine + first * sine]
    return jnp.concatenate(turned, axis=-1)


def dot(left, right):
    return jnp.dot(left, right, preferred_element_type=jnp.float32)


def contract_rows(left, right):
    return lax.dot_general(
        left, right, (((0,), (0,)), ((), ())), preferred_element_type=jnp.float32
    )


def contract_cols(left, right):
    return lax.dot_general(
        left, right, (((1,), (1,)), ((), ())), preferred_element_type=jnp.float32
    )


def plane_order():
    count = lax.axis_size("ctx")
    return list(range(0, count, 2)) + list(range(1, count, 2))


def ctx_bits():
    count = lax.axis_size("ctx")
    return [1 << i for i in range(1, count.bit_length() - 1)]


def swap(values, bit):
    count = lax.axis_size("ctx")
    return lax.ppermute(values, "ctx", [(i, i ^ bit) for i in range(count)])


def turn(values):
    count = lax.axis_size("fsdp")
    return lax.ppermute(values, "fsdp", [(i, (i + 1) % count) for i in range(count)])


def ring(block):
    held = [block]
    for _ in range(lax.axis_size("fsdp") - 1):
        held.append(turn(held[-1]))
    return held


def ring_sum(pieces):
    if len(pieces) == 1:
        return pieces[0]
    total = pieces[1]
    for piece in pieces[2:]:
        total = add(piece, turn(total))
    return add(pieces[0], turn(total))


def gather_small(block):
    held = jnp.stack(ring(block))[:, None]
    for bit in ctx_bits() + [1]:
        held = jnp.concatenate([held, swap(held, bit)], axis=1)
    return held


def gather_plane(block):
    bits = ctx_bits()
    half = block.shape[0] // 2
    if len(bits) == 2:
        x_bit, y_bit = bits
        over_x = swap(block, x_bit)
        over_y = swap(block, y_bit)
        corner_a = swap(over_x[:half], y_bit)
        corner_b = swap(over_y[half:], x_bit)
        near = jnp.concatenate([block, over_x, over_y, corner_a, corner_b], axis=0)
    else:
        near = block
        for bit in bits:
            near = jnp.concatenate([near, swap(near, bit)], axis=0)
    return near, swap(near, 1)


def add(left, right):
    return (left.astype(jnp.float32) + right.astype(jnp.float32)).astype(left.dtype)


def scatter_plane(near, far):
    bits = ctx_bits()
    near_too = swap(far, 1)
    size = near.shape[0] >> len(bits)
    if len(bits) == 2:
        x_bit, y_bit = bits
        half = size // 2
        own, part_x, part_y, corner = (
            add(near[i * size : (i + 1) * size], near_too[i * size : (i + 1) * size])
            for i in range(4)
        )
        for_y, for_x = swap(corner[:half], x_bit), swap(corner[half:], y_bit)
        back_x = swap(jnp.concatenate([part_x[:half], add(part_x[half:], for_x)], axis=0), x_bit)
        back_y = swap(jnp.concatenate([add(part_y[:half], for_y), part_y[half:]], axis=0), y_bit)
        return add(add(own, back_x), back_y)
    held = add(near, near_too)
    for bit in reversed(bits):
        middle = held.shape[0] // 2
        held = add(held[:middle], swap(held[middle:], bit))
    return held


def by_plane(pieces, axis):
    count, me = lax.axis_size("fsdp"), lax.axis_index("fsdp")
    shape = list(pieces[0].shape)
    shape.insert(axis, count)
    whole = jnp.zeros(shape, pieces[0].dtype)
    for k, piece in enumerate(pieces):
        place = lax.rem(me - k + count, count)
        whole = lax.dynamic_update_slice_in_dim(whole, jnp.expand_dims(piece, axis), place, axis)
    return whole


def from_plane(whole, axis):
    count, me = lax.axis_size("fsdp"), lax.axis_index("fsdp")
    return [
        jnp.squeeze(
            lax.dynamic_slice_in_dim(whole, lax.rem(me - k + count, count), 1, axis), axis
        )
        for k in range(count)
    ]


def gate_parts(first, second):
    sigmoid = 1.0 / (1.0 + jnp.exp(-first))
    return sigmoid, first * sigmoid * second


def gate_back(first, second, sigmoid, upstream):
    silu = first * sigmoid
    return upstream * second * (sigmoid + silu * (1.0 - sigmoid)), upstream * silu


def pick(slot_ref, owner, span):
    tokens = GROUP * BLOCK
    slots = slot_ref[pl.ds(owner, 1), span * tokens : (span + 1) * tokens]
    ids = lax.broadcasted_iota(jnp.int32, (GROUP * CAP, tokens), 0).astype(jnp.float32)
    return ids == slots


def pick_all(slot_ref, span):
    chosen = [pick(slot_ref, owner, span).astype(jnp.bfloat16) for owner in range(slot_ref.shape[0])]
    return jnp.concatenate(chosen, axis=0)


def spans_of(first_ref, second_ref):
    tokens = GROUP * BLOCK
    per_side = first_ref.shape[0] // tokens
    return [
        (ref, slice(n * tokens, (n + 1) * tokens))
        for ref in (first_ref, second_ref)
        for n in range(per_side)
    ]


def slots_at(span):
    return slice(span * GROUP * CAP, (span + 1) * GROUP * CAP)


def tokens_at(span):
    return slice(span * GROUP * BLOCK, (span + 1) * GROUP * BLOCK)


def early_kernel(*refs, carried):
    ga_ref, gb_ref, slot_ref, down_ref, s_down_ref = refs[:5]
    rows_ref, dh_ref, dhs_ref, kept_ref = refs[5 + carried :]
    owners = slot_ref.shape[0]
    step = pl.program_id(0)

    @pl.when(step == 0)
    def _():
        for span, (ref, at) in enumerate(spans_of(ga_ref, gb_ref)):
            values = ref[at, :]
            taken = dot(pick_all(slot_ref, span), values).astype(jnp.bfloat16)
            for owner in range(owners):
                kept_ref[owner, slots_at(span), :] = taken[slots_at(owner)]
            dhs_ref[tokens_at(span), :] = contract_cols(values, s_down_ref[...])

    rows = kept_ref[step]
    rows_ref[0] = rows
    dh_ref[0] = contract_cols(rows, down_ref[0])


def middle_kernel(*refs, carried):
    (first_ref, xa_ref, xb_ref, router_ref, mask_ref, slot_ref, in_ref, s_in_ref, dh_ref, dhs_ref) = refs[:10]
    (rows_ref, hidden_ref, dj_ref, da_ref, db_ref, gates_ref, sh_ref, ds_ref, r_ref, z_ref, gate_ref) = refs[10 + carried :]
    bf16 = jnp.bfloat16
    owners = slot_ref.shape[0]
    step = pl.program_id(0)
    spans = spans_of(xa_ref, xb_ref)

    @pl.when(step == 0)
    def _():
        for span, (ref, at) in enumerate(spans):
            x = ref[at, :]
            lanes = tokens_at(span)
            mask = mask_ref[:, lanes] > 0
            logits = jnp.where(mask, contract_cols(router_ref[...], x), NEGATIVE)
            gates = jnp.where(mask, jnp.exp(logits - jnp.max(logits, axis=0, keepdims=True)), 0.0)
            gates = gates / jnp.sum(gates, axis=0, keepdims=True)
            gates_ref[:, lanes] = gates
            expert = lax.broadcasted_iota(jnp.int32, gates.shape, 0)
            for owner in range(owners):
                own = jnp.sum(jnp.where(expert == first_ref[0] + owner, gates, 0.0), axis=0, keepdims=True)
                gate_ref[owner, slots_at(span), :] = jnp.sum(
                    jnp.where(pick(slot_ref, owner, span), own, 0.0), axis=1, keepdims=True
                )
            taken = dot(pick_all(slot_ref, span), x).astype(bf16)
            for owner in range(owners):
                r_ref[owner, slots_at(span), :] = taken[slots_at(owner)]
            joined = dot(x, s_in_ref[...])
            units = joined.shape[1] // 2
            first, second = joined[:, :units], joined[:, units:]
            sigmoid, hidden = gate_parts(first, second)
            sh_ref[lanes, :] = hidden.astype(bf16)
            back = gate_back(first, second, sigmoid, dhs_ref[lanes, :])
            ds_ref[lanes, :] = jnp.concatenate(back, axis=1).astype(bf16)

    rows = r_ref[step]
    joined = dot(rows, in_ref[0])
    units = joined.shape[1] // 2
    first, second = joined[:, :units], joined[:, units:]
    sigmoid, hidden = gate_parts(first, second)
    back = gate_back(first, second, sigmoid, gate_ref[step] * dh_ref[0])
    d_joined = jnp.concatenate(back, axis=1).astype(bf16)
    z_ref[step] = contract_cols(d_joined, in_ref[0]).astype(bf16)
    rows_ref[0] = rows
    hidden_ref[0] = hidden.astype(bf16)
    dj_ref[0] = d_joined

    @pl.when(step == owners - 1)
    def _():
        for span, (ref, at) in enumerate(spans_of(da_ref, db_ref)):
            made = jnp.concatenate([z_ref[owner, slots_at(span), :] for owner in range(owners)], axis=0)
            total = contract_rows(pick_all(slot_ref, span), made)
            total = total + contract_cols(ds_ref[tokens_at(span), :], s_in_ref[...])
            ref[at, :] = total.astype(bf16)


def late_kernel(*refs, carried):
    (first_ref, hidden_ref, rows_ref, slot_ref, gates_ref, sh_ref, down_ref, s_down_ref) = refs[:8]
    (oa_ref, ob_ref, dgate_ref, dy_ref, y_ref) = refs[8 + carried :]
    bf16 = jnp.bfloat16
    owners = slot_ref.shape[0]
    step = pl.program_id(0)
    spans = spans_of(oa_ref, ob_ref)
    partial = dot(hidden_ref[0], down_ref[0])
    rows = rows_ref[0].astype(jnp.float32)
    d_gate = jnp.sum(rows * partial, axis=1, keepdims=True)
    gates = []
    for span in range(len(spans)):
        chosen = pick(slot_ref, step, span)
        lanes = tokens_at(span)
        own = gates_ref[pl.ds(first_ref[0] + step, 1), lanes]
        gates.append(jnp.sum(jnp.where(chosen, own, 0.0), axis=1, keepdims=True))
        dgate_ref[pl.ds(step, 1), lanes] = jnp.sum(
            jnp.where(chosen, d_gate[slots_at(span)], 0.0), axis=0, keepdims=True
        )
    gate = jnp.concatenate(gates, axis=0)
    y_ref[step] = (gate * partial).astype(bf16)
    dy_ref[0] = (gate * rows).astype(bf16)

    @pl.when(step == owners - 1)
    def _():
        for span, (ref, at) in enumerate(spans):
            made = jnp.concatenate([y_ref[owner, slots_at(span), :] for owner in range(owners)], axis=0)
            total = contract_rows(pick_all(slot_ref, span), made)
            total = total + dot(sh_ref[tokens_at(span), :], s_down_ref[...])
            ref[at, :] = total.astype(bf16)


def held_whole(*shape):
    return pl.BlockSpec(shape, lambda j: (0,) * len(shape), pipeline_mode=pl.Buffered(1))


def expert_call(kernel, owners, operands, specs, outs, out_specs, kept, scratch, flops, moved):
    return pl.pallas_call(
        functools.partial(kernel, carried=len(kept)),
        grid=(owners,),
        in_specs=specs + [pl.BlockSpec(memory_space=pl.ANY)] * len(kept),
        out_specs=out_specs,
        out_shape=[jax.ShapeDtypeStruct(shape, kind) for shape, kind in outs],
        scratch_shapes=scratch,
        input_output_aliases={len(operands) + i: i for i in range(len(kept))},
        compiler_params=pltpu.CompilerParams(vmem_limit_bytes=VMEM),
        cost_estimate=pl.CostEstimate(flops=flops, bytes_accessed=moved, transcendentals=0),
    )(*operands, *kept)


def growing(k, rows, columns):
    return pl.BlockSpec((1, rows, columns), lambda j: (j, k, 0))


def weights_of(array):
    depth = 2 if array.shape[0] > 1 else 1
    return pl.BlockSpec(
        (1,) + array.shape[1:], lambda j: (j, 0, 0), pipeline_mode=pl.Buffered(depth)
    )


def early(k, planes, grads, slots, w_down, s_down, kept):
    bf16, f32 = jnp.bfloat16, jnp.float32
    owners, units, width = w_down.shape
    half = grads[0].shape[0]
    rows, lane = 2 * half // BLOCK * CAP, s_down.shape[0]
    outs = [
        ((owners, planes * rows, width), bf16),
        ((owners, planes * rows, units), f32),
        ((2 * half, lane), f32),
    ]
    taken, dh, dhs = expert_call(
        early_kernel,
        owners,
        [*grads, slots, w_down, s_down],
        [held_whole(half, width)] * 2
        + [held_whole(*slots.shape), weights_of(w_down), held_whole(*s_down.shape)],
        outs,
        [growing(k, rows, width), growing(k, rows, units), held_whole(2 * half, lane)],
        kept,
        [pltpu.VMEM((owners, rows, width), bf16)],
        2 * owners * rows * width * (units + GROUP * BLOCK) + 4 * half * width * lane,
        2 * owners * width * (units + 2 * rows) + 4 * half * width,
    )
    return [taken, dh], dhs


def middle(k, planes, first, rows_x, router_t, mask, slots, w_in, s_in, dh, dhs, kept):
    bf16, f32 = jnp.bfloat16, jnp.float32
    owners, width, joined = w_in.shape
    half = rows_x[0].shape[0]
    rows, lane = 2 * half // BLOCK * CAP, dhs.shape[1]
    outs = [
        ((owners, planes * rows, width), bf16),
        ((owners, planes * rows, joined // 2), bf16),
        ((owners, planes * rows, joined), bf16),
        ((half, width), bf16),
        ((half, width), bf16),
        ((EXPERTS, 2 * half), f32),
        ((2 * half, lane), bf16),
        ((2 * half, 2 * lane), bf16),
    ]
    made = expert_call(
        middle_kernel,
        owners,
        [first, *rows_x, router_t, mask, slots, w_in, s_in, dh, dhs],
        [pl.BlockSpec(memory_space=pltpu.SMEM)]
        + [held_whole(half, width)] * 2
        + [held_whole(*a.shape) for a in (router_t, mask, slots)]
        + [weights_of(w_in), held_whole(*s_in.shape), growing(k, rows, joined // 2)]
        + [held_whole(*dhs.shape)],
        outs,
        [growing(k, rows, width), growing(k, rows, joined // 2), growing(k, rows, joined)]
        + [held_whole(*shape) for shape, _ in outs[3:]],
        kept,
        [
            pltpu.VMEM((owners, rows, width), bf16),
            pltpu.VMEM((owners, rows, width), bf16),
            pltpu.VMEM((owners, rows, 1), f32),
        ],
        4 * owners * rows * width * (joined + GROUP * BLOCK) + 16 * half * width * lane,
        2 * owners * width * (joined + 2 * rows) + 8 * half * width,
    )
    return list(made[:3]), made[3:5], made[5], made[6], made[7]


def late(k, planes, first, hidden, taken, slots, gates, shared, w_down, s_down, kept):
    bf16, f32 = jnp.bfloat16, jnp.float32
    owners, units, width = w_down.shape
    half = shared.shape[0] // 2
    rows = 2 * half // BLOCK * CAP
    outs = [
        ((half, width), bf16),
        ((half, width), bf16),
        ((owners, 2 * half), f32),
        ((owners, rows, width), bf16),
    ]
    made = expert_call(
        late_kernel,
        owners,
        [first, hidden, taken, slots, gates, shared, w_down, s_down],
        [pl.BlockSpec(memory_space=pltpu.SMEM), growing(k, rows, units), growing(k, rows, width)]
        + [held_whole(*a.shape) for a in (slots, gates, shared)]
        + [weights_of(w_down), held_whole(*s_down.shape)],
        outs,
        [held_whole(*shape) for shape, _ in outs[:3]] + [growing(0, rows, width)],
        [],
        [pltpu.VMEM((owners, rows, width), bf16)],
        2 * owners * rows * width * (units + GROUP * BLOCK) + 4 * half * width * s_down.shape[0],
        2 * owners * width * (units + 2 * rows) + 4 * half * width,
    )
    return made[:2], made[2], made[3]


def local(
    tokens,
    gain_attn,
    w_qkv,
    w_out,
    gain_ffn,
    w_router,
    w_shared_in,
    w_shared_down,
    w_expert_in,
    w_expert_down,
    routes,
    plan,
    cotangent,
):
    n_ctx, planes = lax.axis_size("ctx"), lax.axis_size("fsdp")
    devices = n_ctx * planes
    ctx, plane = lax.axis_index("ctx"), lax.axis_index("fsdp")
    device = ctx * planes + plane
    amount, width = tokens.shape[1:]
    head_size = width // HEADS
    heads = HEADS // n_ctx
    part = heads * head_size
    scale = head_size ** (-0.5)
    rows = width // devices
    per_owner = w_expert_in.shape[0]
    units = w_shared_down.shape[0]
    bf16, f32 = jnp.bfloat16, jnp.float32
    order = jnp.array(plane_order(), jnp.int32)
    places = order ^ ctx

    def to_all(values):
        return lax.all_to_all(values, BOTH, split_axis=0, concat_axis=0, tiled=True)

    qkv_part = w_qkv.reshape(rows, 3, n_ctx, part).transpose(2, 0, 1, 3).reshape(n_ctx, rows, 3 * part)
    qkv_part = lax.all_to_all(qkv_part, "ctx", split_axis=0, concat_axis=0, tiled=True)
    seq_rows = jnp.concatenate(gather_plane(tokens[0]), axis=0)

    expert_ids = jnp.arange(EXPERTS, dtype=jnp.int32)
    own_mask = jnp.sum((expert_ids[:, None, None] == routes[0].T[None]).astype(f32), axis=1)
    small = jnp.concatenate([w_router, gain_attn[:, None], gain_ffn[:, None]], axis=1)
    small = jnp.pad(small, ((0, 0), (0, amount - EXPERTS - 2)))
    small = gather_small(jnp.concatenate([own_mask.astype(bf16), small], axis=0))
    masks = small[:, :, :EXPERTS].transpose(0, 2, 1, 3).reshape(planes, EXPERTS, n_ctx * amount)
    masks = masks.astype(f32)
    sources = jnp.arange(n_ctx, dtype=jnp.int32) ^ ctx
    sources = sources // 2 + (sources % 2) * (n_ctx // 2)
    back = lax.rem(plane - jnp.arange(planes, dtype=jnp.int32) + planes, planes)
    sources = (back[None, :] * n_ctx + sources[:, None]).reshape(-1)
    small = small[:, :, EXPERTS:].reshape(devices, rows, amount)
    small = jnp.take(small, sources, axis=0).reshape(width, amount)
    router_full = small[:, :EXPERTS]
    router_t = router_full.T
    gain_one = small[:, EXPERTS].astype(f32)
    gain_two = small[:, EXPERTS + 1].astype(f32)

    qkv_w = by_plane(ring(qkv_part), 1).reshape(width, 3 * part)
    out_w = by_plane(ring(w_out), 0).reshape(part, width)
    shared_in = w_shared_in.reshape(rows, 2, devices, units).transpose(2, 0, 1, 3)
    shared_in = to_all(shared_in.reshape(devices, rows, 2 * units)).reshape(width, 2, units)
    lane = -(-units // BLOCK) * BLOCK
    s_in = jnp.pad(shared_in, ((0, 0), (0, 0), (0, lane - units))).reshape(width, 2 * lane)
    s_down = jnp.pad(w_shared_down, ((0, lane - units), (0, 0)))

    first_expert = lax.rem(device * per_owner, EXPERTS)
    mask_own = lax.dynamic_slice_in_dim(masks, first_expert, per_owner, 1)
    mask_own = mask_own.reshape(planes, per_owner, n_ctx, amount)
    ranking = jnp.cumsum(mask_own, axis=3) - mask_own
    slots = ranking + (CAP * (jnp.arange(n_ctx) % GROUP)).astype(f32)[:, None]
    slots = jnp.where(mask_own > 0, slots, -1.0).reshape(planes, per_owner, n_ctx * amount)
    first = first_expert.reshape(1).astype(jnp.int32)

    grads = [gather_plane(block) for block in ring(cotangent[0])]
    kept, dhs = [], []
    for k in range(planes):
        kept, made = early(k, planes, grads[k], slots[k], w_expert_down, s_down, kept)
        dhs.append(made)
    taken, dh = kept

    half_block = amount // 2
    half_ids = (places[:, None] * 2 + jnp.arange(2, dtype=jnp.int32)[None, :]).reshape(-1)
    placed = jnp.sum(
        jnp.where(half_ids[:, None] == jnp.arange(plan.shape[0])[None, :], plan[None, :], 0), axis=1
    )
    pos = (placed[:, None] * half_block + jnp.arange(half_block)[None, :]).reshape(-1)
    visible = pos[None, :] <= pos[:, None]

    own_rows = tokens[0].astype(f32)
    normed = rms_scale(seq_rows.astype(f32), gain_one).astype(bf16)
    projected = dot(normed, qkv_w)
    query = rotate(projected[:, :part], pos, heads).astype(bf16)
    key = rotate(projected[:, part : 2 * part], pos, heads).astype(bf16)
    value = projected[:, 2 * part :].astype(bf16)

    def head_of(values, head):
        return values[:, head * head_size : (head + 1) * head_size]

    expos, totals, mixes = [], [], []
    for head in range(heads):
        scores = contract_cols(head_of(query, head), head_of(key, head)) * scale
        scores = jnp.where(visible, scores, NEGATIVE)
        top = jnp.max(scores, axis=1, keepdims=True)
        expo = jnp.where(visible, jnp.exp(scores - top), 0.0)
        total = jnp.sum(expo, axis=1, keepdims=True)
        expos.append(expo)
        totals.append(total)
        mixes.append(dot(expo.astype(bf16), head_of(value, head)) / total)
    mixed_b = jnp.concatenate(mixes, axis=1).astype(bf16)
    middle_row = n_ctx * amount // 2
    attended = [dot(side, out_w).astype(bf16) for side in (mixed_b[:middle_row], mixed_b[middle_row:])]
    residual = own_rows + scatter_plane(*attended).astype(f32)
    ffn_own = rms_scale(residual, gain_two).astype(bf16)

    ffn = [gather_plane(block) for block in ring(ffn_own)]
    kept, d_parts, gates, hidden_s, d_joined_s = [], [], [], [], []
    for k in range(planes):
        kept, pair, *made = middle(
            k, planes, first, ffn[k], router_t, masks[k], slots[k], w_expert_in, s_in, dh, dhs[k], kept
        )
        d_parts.append(scatter_plane(*pair))
        for some, one in zip((gates, hidden_s, d_joined_s), made, strict=True):
            some.append(one)
    rows_in, hidden, d_joined = kept
    d_ffn = ring_sum(d_parts)
    out_pairs, dgates, dys = [], [], []
    for k in range(planes):
        pair, dgate, dy = late(
            k, planes, first, hidden, taken, slots[k], gates[k], hidden_s[k], w_expert_down, s_down, []
        )
        out_pairs.append(pair)
        dgates.append(dgate)
        dys.append(dy)

    dgate = jnp.stack(dgates).reshape(planes, per_owner, n_ctx, amount).transpose(0, 2, 1, 3)
    dgate = jnp.take(dgate.reshape(devices, per_owner * amount), sources, axis=0)
    dgate = to_all(dgate).reshape(2, EXPERTS, amount)
    dgate = dgate[0] + dgate[1]
    gates_own = gates[0][:, :amount]
    dlogits = gates_own * (dgate - jnp.sum(gates_own * dgate, axis=0, keepdims=True))
    dlogits_b = dlogits.astype(bf16).T

    def small_sum(values):
        flat = to_all(values.reshape(devices, -1))
        return jnp.sum(flat, axis=0).reshape(values.shape[1:])

    d_ffn = d_ffn.astype(f32) + contract_cols(dlogits_b, router_full)
    router_grad = small_sum(contract_rows(ffn_own, dlogits_b).reshape(devices, rows, EXPERTS))
    second_back = jax.vjp(rms_scale, residual, gain_two)[1](d_ffn)
    d_residual = cotangent[0].astype(f32) + second_back[0]
    gain_ffn_grad = small_sum(second_back[1].reshape(devices, rows))

    out_parts = [scatter_plane(*pair) for pair in out_pairs]
    result = (residual + ring_sum(out_parts).astype(f32)).astype(bf16)

    d_attn = jnp.concatenate(gather_plane(d_residual.astype(bf16)), axis=0)
    out_grad = contract_rows(mixed_b, d_attn).astype(bf16).reshape(planes, rows, width)
    out_grad = ring_sum(from_plane(out_grad, 0)).astype(f32)
    d_mixed = contract_cols(d_attn, out_w).astype(bf16).astype(f32)
    d_query, d_key, d_value = [], [], []
    for head in range(heads):
        d_head = head_of(d_mixed, head)
        total, expo = totals[head], expos[head]
        grad_num = (d_head / total).astype(bf16)
        shift = jnp.sum(d_head * mixes[head], axis=1, keepdims=True) / total
        d_prob = contract_cols(grad_num, head_of(value, head))
        d_score = (expo * (d_prob - shift)).astype(bf16)
        d_value.append(contract_rows(expo.astype(bf16), grad_num))
        d_query.append(dot(d_score, head_of(key, head)) * scale)
        d_key.append(contract_rows(d_score, head_of(query, head)) * scale)
    d_query = rotate(jnp.concatenate(d_query, axis=1), -pos, heads)
    d_key = rotate(jnp.concatenate(d_key, axis=1), -pos, heads)
    d_projected = jnp.concatenate([d_query, d_key] + d_value, axis=1).astype(bf16)
    qkv_grad = contract_rows(normed, d_projected).astype(bf16)
    qkv_grad = qkv_grad.reshape(n_ctx, planes, rows, 3 * part)
    qkv_grad = ring_sum(from_plane(qkv_grad, 1))
    qkv_grad = lax.all_to_all(qkv_grad, "ctx", split_axis=0, concat_axis=0, tiled=True)
    qkv_grad = qkv_grad.reshape(n_ctx, rows, 3, part).transpose(1, 2, 0, 3)
    qkv_grad = qkv_grad.reshape(rows, 3 * width).astype(f32)
    d_normed = [
        contract_cols(side, qkv_w).astype(bf16)
        for side in (d_projected[:middle_row], d_projected[middle_row:])
    ]
    d_normed = scatter_plane(*d_normed).astype(f32)
    first_back = jax.vjp(rms_scale, own_rows, gain_one)[1](d_normed)
    tokens_grad = d_residual + first_back[0]
    gain_attn_grad = small_sum(first_back[1].reshape(devices, rows))

    dy = jnp.concatenate(dys, axis=1)
    expert_in_grad = jnp.einsum("jcd,jcf->jdf", rows_in, d_joined, preferred_element_type=f32)
    expert_down_grad = jnp.einsum("jcf,jcd->jfd", hidden, dy, preferred_element_type=f32)
    shared_down_grad, shared_in_grad = 0.0, 0.0
    for k in range(planes):
        at = 0
        for rows_x, rows_g in zip(ffn[k], grads[k], strict=True):
            span = slice(at, at + rows_x.shape[0])
            at += rows_x.shape[0]
            shared_down_grad += contract_rows(hidden_s[k][span], rows_g)
            shared_in_grad += contract_rows(d_joined_s[k][span], rows_x)
    shared_down_grad = shared_down_grad[:units]
    shared_in_grad = shared_in_grad.reshape(2, lane, width)[:, :units].reshape(2 * units, width)
    shared_in_grad = shared_in_grad.T.astype(bf16).reshape(devices, rows, 2 * units)
    shared_in_grad = to_all(shared_in_grad).reshape(devices, rows, 2, units).transpose(1, 2, 0, 3)
    shared_in_grad = shared_in_grad.reshape(rows, 2 * devices * units).astype(f32)
    return (
        result[None],
        tokens_grad[None],
        gain_attn_grad,
        qkv_grad,
        out_grad,
        gain_ffn_grad,
        router_grad,
        shared_in_grad,
        shared_down_grad,
        expert_in_grad,
        expert_down_grad,
    )


def solution(mesh):
    split = P(BOTH)
    matrix = P(BOTH, None)
    cube = P(BOTH, None, None)
    batch = P("fsdp", "ctx", None)
    return jax.shard_map(
        local,
        mesh=mesh,
        in_specs=(
            batch,
            split,
            matrix,
            matrix,
            split,
            matrix,
            matrix,
            matrix,
            cube,
            cube,
            batch,
            P(),
            batch,
        ),
        out_specs=(
            batch,
            batch,
            split,
            matrix,
            matrix,
            split,
            matrix,
            matrix,
            matrix,
            cube,
            cube,
        ),
        check_vma=False,
    )
```

```python
import functools

import jax
import jax.numpy as jnp
from jax import lax
from jax.experimental import pallas as pl
from jax.experimental.pallas import tpu as pltpu
from jax.sharding import PartitionSpec as P

HEADS = 16
EXPERTS = 64
CAP = 20
BLOCK = 128
EXTRA = 16
GROUP = 4
VMEM = 60 * 1024 * 1024

EPSILON = 1e-06
ROPE_BASE = 10000.0
NEGATIVE = -1e30
BOTH = ("ctx", "fsdp")


def rms_scale(values, gain):
    inverse = lax.rsqrt(jnp.mean(values * values, axis=-1, keepdims=True) + EPSILON)
    return values * inverse * gain


def dot(left, right):
    return jnp.dot(left, right, preferred_element_type=jnp.float32)


def contract_rows(left, right):
    return lax.dot_general(
        left, right, (((0,), (0,)), ((), ())), preferred_element_type=jnp.float32
    )


def contract_cols(left, right):
    return lax.dot_general(
        left, right, (((1,), (1,)), ((), ())), preferred_element_type=jnp.float32
    )


def plane_order():
    count = lax.axis_size("ctx")
    return list(range(0, count, 2)) + list(range(1, count, 2))


def ctx_bits():
    count = lax.axis_size("ctx")
    return [1 << i for i in range(1, count.bit_length() - 1)]


def swap(values, bit):
    count = lax.axis_size("ctx")
    return lax.ppermute(values, "ctx", [(i, i ^ bit) for i in range(count)])


def turn(values, step=1):
    count = lax.axis_size("fsdp")
    return lax.ppermute(values, "fsdp", [(i, (i + step) % count) for i in range(count)])


def add(left, right):
    return (left.astype(jnp.float32) + right.astype(jnp.float32)).astype(left.dtype)


class Step:
    def __init__(self, sent, make=None, beside=(), outs=()):
        self.sent, self.make, self.beside, self.outs = sent, make, list(beside), list(outs)


class Transfer:
    def __init__(self, steps):
        self.steps, self.step, self.done, self.result = steps, None, False, None
        self.advance(None)

    def advance(self, arrived):
        try:
            self.step = self.steps.send(arrived)
        except StopIteration as stop:
            self.step, self.done, self.result = None, True, stop.value


class Clock:
    def __init__(self):
        self.token = jnp.zeros((8, 128), jnp.float32)

    def now(self, values):
        return values + self.token[0, 0].astype(values.dtype)


def stage(clock, transfers, beside=()):
    active = [t for t in transfers if not t.done]
    making = [t.step for t in active if t.step.make is not None]
    passed = [clock.token, *beside]
    waited = [a for t in active if t.step.make is None for a in t.step.sent]
    taken = [a for step in making for a in step.sent + step.beside]
    outs = [jax.ShapeDtypeStruct(o, step.sent[0].dtype) for step in making for o in step.outs]
    first = len(passed) + len(waited)

    def kernel(*refs):
        inputs, made = refs[first : first + len(taken)], refs[first + len(taken) + len(passed) :]
        for step in making:
            count = len(step.sent) + len(step.beside)
            step.make(inputs[:count], made[: len(step.outs)])
            inputs, made = inputs[count:], made[len(step.outs) :]

    far, near = pl.BlockSpec(memory_space=pltpu.HBM), pl.BlockSpec(memory_space=pltpu.VMEM)
    arrays = pl.pallas_call(
        kernel,
        in_specs=[far] * first + [near] * len(taken),
        out_specs=[far] * len(passed) + [near] * len(outs),
        out_shape=[jax.ShapeDtypeStruct(a.shape, a.dtype) for a in passed] + outs,
        input_output_aliases={i: i for i in range(len(passed))},
        compiler_params=pltpu.CompilerParams(vmem_limit_bytes=VMEM),
    )(*passed, *waited, *taken)
    clock.token, given, arrays = arrays[0], arrays[1 : len(passed)], arrays[len(passed) :]
    for t in active:
        if t.step.make is None:
            t.advance(t.step.sent)
        else:
            count = len(t.step.outs)
            made, arrays = arrays[:count], arrays[count:]
            t.advance(made)
    return given


def finish(clock, *transfers):
    while not all(t.done for t in transfers):
        stage(clock, transfers)
    return [t.result for t in transfers]


CHUNK = 16


def chunks(amount, body):
    @pl.loop(0, amount // CHUNK)
    def _(i):
        body(pl.multiple_of(i * CHUNK, CHUNK))


def put(source, target, at=0, start=0, amount=None):
    def body(row):
        target[pl.ds(at + row, CHUNK), :] = source[pl.ds(start + row, CHUNK), :]

    chunks(amount or target.shape[0] - at, body)


def put_sum(target, sources, starts=None, at=0, amount=None):
    starts = starts or [0] * len(sources)

    def body(row):
        total = 0.0
        for source, start in zip(sources, starts, strict=True):
            total = total + source[pl.ds(start + row, CHUNK), :].astype(jnp.float32)
        target[pl.ds(at + row, CHUNK), :] = total.astype(target.dtype)

    chunks(amount or target.shape[0] - at, body)


def put_blocks_sum(taken, made):
    for i in range(made[0].shape[0]):
        put_sum(made[0].at[i], [ref.at[i] for ref in taken])


def put_joined(order):
    def make(taken, made):
        at = 0
        for i in order:
            put(taken[i], made[0], at, 0, taken[i].shape[0])
            at += taken[i].shape[0]

    return make


def turned(block, step=1):
    (block,) = yield Step([turn(block, step)])
    return block


def ring(block):
    held = [block]
    for _ in range(lax.axis_size("fsdp") - 1):
        (block,) = yield Step([turn(block)])
        held.append(block)
    return held


def ring_sum(pieces):
    total = pieces[min(1, len(pieces) - 1)]
    for piece in pieces[2:] + (pieces[:1] if len(pieces) > 1 else []):
        (total,) = yield Step([turn(total)], put_blocks_sum, [piece], [piece.shape])
    return total


def staged_sum(parts):
    total = parts[0].result
    for part in parts[1:]:
        (total,) = yield Step([turn(total)])
        while not part.done:
            (total,) = yield Step([total])
        total = add(part.result, total)
    return total


def to_all(values):
    return lax.all_to_all(values, BOTH, split_axis=0, concat_axis=0, tiled=True)


def exchanged(values):
    (values,) = yield Step([to_all(values)])
    return values


def gather_plane(block, direct=True):
    bits = ctx_bits()
    amount, width = block.shape
    half = -(-amount // 2 // CHUNK) * CHUNK
    if len(bits) == 2 and direct:
        others = [swap(block, place) for place in (bits[0], bits[1], bits[0] | bits[1])]
        (near,) = yield Step(others, put_joined([3, 0, 1, 2]), [block], [(4 * amount, width)])
    elif len(bits) == 2:
        x_bit, y_bit = bits
        over_x, over_y = swap(block, x_bit), swap(block, y_bit)

        def halves(taken, made):
            put(taken[0], made[0], 0, 0, half)
            put(taken[1], made[1], 0, half, amount - half)

        parts = [(half, width), (amount - half, width)]
        first, second = yield Step([over_x, over_y], halves, [], parts)
        corner = [swap(first, y_bit), swap(second, x_bit)]
        (near,) = yield Step(
            corner, put_joined([2, 3, 4, 0, 1]), [block, over_x, over_y], [(4 * amount, width)]
        )
    else:
        near = block
        for bit in bits:
            shape = (2 * near.shape[0], width)
            (near,) = yield Step([swap(near, bit)], put_joined([1, 0]), [near], [shape])
    (far,) = yield Step([swap(near, 1)])
    return near, far


def scatter_plane(near, far, direct=True):
    bits = ctx_bits()
    size, width = near.shape[0] >> len(bits), near.shape[1]
    half = size // 2
    whole, part = (size, width), (half, width)
    if len(bits) != 2:
        (held,) = yield Step([swap(far, 1)], lambda t, m: put_sum(m[0], t), [near], [near.shape])
        for bit in reversed(bits):
            middle = held.shape[0] // 2

            def fold(taken, made, middle=middle):
                put_sum(made[0], taken)

            (held,) = yield Step([swap(held[middle:], bit)], fold, [held[:middle]], [(middle, width)])
        return held
    x_bit, y_bit = bits
    if direct:

        def spread(taken, made):
            for i in range(4):
                put_sum(made[i], taken, [i * size, i * size])

        own, part_x, part_y, corner = yield Step([swap(far, 1)], spread, [near], [whole] * 4)
        back = [swap(part_x, x_bit), swap(part_y, y_bit), swap(corner, x_bit | y_bit)]
        (total,) = yield Step(back, lambda t, m: put_sum(m[0], t), [own], [whole])
        return total

    def split(taken, made):
        for i, at in enumerate((0, size, 2 * size, 3 * size, 3 * size + half)):
            put_sum(made[i], taken, [at, at])

    def join(taken, made):
        for_y, for_x, part_x, part_y = taken
        put(part_x, made[0], 0, 0, half)
        put_sum(made[0], [part_x, for_x], [half, 0], half, half)
        put_sum(made[1], [part_y, for_y], [0, 0], 0, half)
        put(part_y, made[1], half, half, half)

    own, part_x, part_y, corner_a, corner_b = yield Step(
        [swap(far, 1)], split, [near], [whole] * 3 + [part] * 2
    )
    part_x, part_y = yield Step(
        [swap(corner_a, x_bit), swap(corner_b, y_bit)], join, [part_x, part_y], [whole] * 2
    )
    (total,) = yield Step(
        [swap(part_x, x_bit), swap(part_y, y_bit)], lambda t, m: put_sum(m[0], t), [own], [whole]
    )
    return total


def gate_parts(first, second):
    sigmoid = 1.0 / (1.0 + jnp.exp(-first))
    return sigmoid, first * sigmoid * second


def gate_back(first, second, sigmoid, upstream):
    silu = first * sigmoid
    return upstream * second * (sigmoid + silu * (1.0 - sigmoid)), upstream * silu


def pick(slot_ref, owner, span):
    tokens = GROUP * BLOCK
    slots = slot_ref[pl.ds(owner, 1), span * tokens : (span + 1) * tokens]
    ids = lax.broadcasted_iota(jnp.int32, (GROUP * CAP, tokens), 0).astype(jnp.float32)
    return ids == slots


def pick_all(slot_ref, span):
    chosen = [pick(slot_ref, owner, span).astype(jnp.bfloat16) for owner in range(slot_ref.shape[0])]
    return jnp.concatenate(chosen, axis=0)


def spans_of(first_ref, second_ref, stride=BLOCK):
    per_side = first_ref.shape[0] // (GROUP * stride)
    return [
        (ref, [(n * GROUP + i) * stride for i in range(GROUP)])
        for ref in (first_ref, second_ref)
        for n in range(per_side)
    ]


def read_span(ref, starts):
    if starts[1] == starts[0] + BLOCK:
        return ref[starts[0] : starts[0] + GROUP * BLOCK, :]
    return jnp.concatenate([ref[at : at + BLOCK, :] for at in starts], axis=0)


def write_span(ref, starts, values):
    for i, at in enumerate(starts):
        ref[at : at + BLOCK, :] = values[i * BLOCK : (i + 1) * BLOCK].astype(ref.dtype)


def slots_at(span):
    return slice(span * GROUP * CAP, (span + 1) * GROUP * CAP)


def tokens_at(span):
    return slice(span * GROUP * BLOCK, (span + 1) * GROUP * BLOCK)


def early_kernel(*refs, carried):
    ga_ref, gb_ref, slot_ref, down_ref, s_down_ref = refs[:5]
    rows_ref, dh_ref, dhs_ref, kept_ref = refs[5 + carried :]
    owners = slot_ref.shape[0]
    step = pl.program_id(0)

    @pl.when(step == 0)
    def _():
        for span, place in enumerate(spans_of(ga_ref, gb_ref, BLOCK + EXTRA)):
            values = read_span(*place)
            taken = dot(pick_all(slot_ref, span), values).astype(jnp.bfloat16)
            for owner in range(owners):
                kept_ref[owner, slots_at(span), :] = taken[slots_at(owner)]
            dhs_ref[tokens_at(span), :] = contract_cols(values, s_down_ref[...])

    rows = kept_ref[step]
    rows_ref[0] = rows
    dh_ref[0] = contract_cols(rows, down_ref[0])


def gate_rows(first_ref, values, width):
    per_row = width // BLOCK
    rows = lax.broadcasted_iota(jnp.int32, (EXTRA, width), 0)
    groups = lax.broadcasted_iota(jnp.int32, (EXTRA, width), 1) // BLOCK
    leading = values.astype(jnp.bfloat16).astype(jnp.float32)
    total = jnp.zeros((EXTRA, width), jnp.float32)
    for owner in range(values.shape[0]):
        expert = first_ref[0] + owner
        for i, one in enumerate((leading, values - leading)):
            wide = jnp.concatenate([one[owner : owner + 1]] * per_row, axis=1)
            row = (2 * first_ref[1] + i) * (EXPERTS // per_row) + expert // per_row
            here = (rows == row) & (groups == expert % per_row)
            total = total + jnp.where(here, wide, 0.0)
    return total.astype(jnp.bfloat16)


def middle_kernel(*refs, carried):
    (first_ref, xa_ref, xb_ref, router_ref, mask_ref, slot_ref, in_ref, s_in_ref, dh_ref, dhs_ref) = refs[:10]
    (rows_ref, hidden_ref, dj_ref, da_ref, db_ref, gates_ref, dgate_ref, sh_ref, ds_ref, r_ref, z_ref, gate_ref) = refs[10 + carried :]
    bf16 = jnp.bfloat16
    owners = slot_ref.shape[0]
    step = pl.program_id(0)
    spans = spans_of(xa_ref, xb_ref)

    @pl.when(step == 0)
    def _():
        for span, place in enumerate(spans):
            x = read_span(*place)
            lanes = tokens_at(span)
            mask = jnp.concatenate(
                [mask_ref[span * GROUP + i].astype(jnp.float32) for i in range(GROUP)], axis=1
            )
            mask = mask >= 0
            logits = jnp.where(mask, contract_cols(router_ref[...], x), NEGATIVE)
            gates = jnp.where(mask, jnp.exp(logits - jnp.max(logits, axis=0, keepdims=True)), 0.0)
            gates = gates / jnp.sum(gates, axis=0, keepdims=True)
            gates_ref[:, lanes] = gates
            expert = lax.broadcasted_iota(jnp.int32, gates.shape, 0)
            for owner in range(owners):
                own = jnp.sum(jnp.where(expert == first_ref[0] + owner, gates, 0.0), axis=0, keepdims=True)
                gate_ref[owner, slots_at(span), :] = jnp.sum(
                    jnp.where(pick(slot_ref, owner, span), own, 0.0), axis=1, keepdims=True
                )
            taken = dot(pick_all(slot_ref, span), x).astype(bf16)
            for owner in range(owners):
                r_ref[owner, slots_at(span), :] = taken[slots_at(owner)]
            joined = dot(x, s_in_ref[...])
            units = joined.shape[1] // 2
            first, second = joined[:, :units], joined[:, units:]
            sigmoid, hidden = gate_parts(first, second)
            sh_ref[lanes, :] = hidden.astype(bf16)
            back = gate_back(first, second, sigmoid, dhs_ref[lanes, :])
            ds_ref[lanes, :] = jnp.concatenate(back, axis=1).astype(bf16)

    rows = r_ref[step]
    joined = dot(rows, in_ref[0])
    units = joined.shape[1] // 2
    first, second = joined[:, :units], joined[:, units:]
    sigmoid, hidden = gate_parts(first, second)
    back = gate_back(first, second, sigmoid, gate_ref[step] * dh_ref[0])
    d_gate = jnp.sum(hidden * dh_ref[0], axis=1, keepdims=True)
    for span in range(len(spans)):
        spread = jnp.where(pick(slot_ref, step, span), d_gate[slots_at(span)], 0.0)
        dgate_ref[pl.ds(step, 1), tokens_at(span)] = jnp.sum(spread, axis=0, keepdims=True)
    d_joined = jnp.concatenate(back, axis=1).astype(bf16)
    z_ref[step] = contract_cols(d_joined, in_ref[0]).astype(bf16)
    rows_ref[0] = rows
    hidden_ref[0] = hidden.astype(bf16)
    dj_ref[0] = d_joined

    @pl.when(step == owners - 1)
    def _():
        for span, place in enumerate(spans_of(da_ref, db_ref, BLOCK + EXTRA)):
            made = jnp.concatenate([z_ref[owner, slots_at(span), :] for owner in range(owners)], axis=0)
            total = contract_rows(pick_all(slot_ref, span), made)
            total = total + contract_cols(ds_ref[tokens_at(span), :], s_in_ref[...])
            write_span(*place, total)
            for i, at in enumerate(place[1]):
                block = span * GROUP + i
                place[0][at + BLOCK : at + BLOCK + EXTRA, :] = gate_rows(
                    first_ref, dgate_ref[:, block * BLOCK : (block + 1) * BLOCK], made.shape[1]
                )


def late_kernel(*refs, carried):
    (first_ref, hidden_ref, rows_ref, slot_ref, gates_ref, sh_ref, down_ref, s_down_ref) = refs[:8]
    (dy_ref, oa_ref, ob_ref, y_ref) = refs[8 + carried :]
    bf16 = jnp.bfloat16
    owners = slot_ref.shape[0]
    step = pl.program_id(0)
    spans = spans_of(oa_ref, ob_ref)
    partial = dot(hidden_ref[0], down_ref[0])
    rows = rows_ref[0].astype(jnp.float32)
    gates = []
    for span in range(len(spans)):
        chosen = pick(slot_ref, step, span)
        lanes = tokens_at(span)
        own = gates_ref[pl.ds(first_ref[0] + step, 1), lanes]
        gates.append(jnp.sum(jnp.where(chosen, own, 0.0), axis=1, keepdims=True))
    gate = jnp.concatenate(gates, axis=0)
    y_ref[step] = (gate * partial).astype(bf16)
    dy_ref[0] = (gate * rows).astype(bf16)

    @pl.when(step == owners - 1)
    def _():
        for span, place in enumerate(spans):
            made = jnp.concatenate([y_ref[owner, slots_at(span), :] for owner in range(owners)], axis=0)
            total = contract_rows(pick_all(slot_ref, span), made)
            total = total + dot(sh_ref[tokens_at(span), :], s_down_ref[...])
            write_span(*place, total)


ROWS = 256


def row_chunks(amount, body):
    @pl.loop(0, amount // ROWS)
    def _(i):
        body(pl.multiple_of(i * ROWS, ROWS))


def plane_copies(plane, pieces, target, sems):
    count = len(pieces)
    return [
        pltpu.make_async_copy(
            piece, target(lax.rem(plane - k + count, count)), sems.at[k]
        )
        for k, piece in enumerate(pieces)
    ]


def turn_head(values, cosine, sine):
    return values * cosine + pltpu.roll(values, values.shape[1] // 2, 1) * sine


def attend_kernel(*refs, planes, heads):
    (plane_ref, near_ref, far_ref, gain_ref, cos_ref, sin_ref, column_ref, row_ref) = refs[:8]
    w_pieces = refs[8 : 8 + planes]
    (oa_ref, ob_ref, normed_ref, q_ref, k_ref, v_ref, mixed_ref, top_ref, total_ref) = refs[
        9 + planes : 18 + planes
    ]
    w_ref, sems = refs[18 + planes :]
    bf16, f32 = jnp.bfloat16, jnp.float32
    plane = plane_ref[0]
    width = near_ref.shape[1]
    blocks, part = w_ref.shape[0], w_ref.shape[3] // 4
    size = part // heads
    half = near_ref.shape[0]
    amount = 2 * half
    copies = plane_copies(plane, w_pieces, lambda at: w_ref.at[:, at], sems.at[0])
    for copy in copies:
        copy.start()
    for copy in copies:
        copy.wait()

    for base, ref in ((0, near_ref), (half, far_ref)):

        def project(row, base=base, ref=ref):
            at = pl.ds(base + row, ROWS)
            x = ref[pl.ds(row, ROWS), :].astype(f32)
            normed = rms_scale(x, gain_ref[...]).astype(bf16)
            normed_ref[at, :] = normed
            projected = dot(normed, w_ref[:, :, :, : 3 * part].reshape(width, 3 * part))
            cosine, sine = cos_ref[at, :], sin_ref[at, :]
            for head in range(heads):
                mine = slice(head * size, (head + 1) * size)
                for target, start in ((q_ref, 0), (k_ref, part)):
                    values = projected[:, start + head * size : start + (head + 1) * size]
                    target[at, mine] = turn_head(values, cosine, sine).astype(bf16)
            v_ref[at, :] = projected[:, 2 * part :].astype(bf16)

        row_chunks(half, project)

    for head in range(heads):
        mine = slice(head * size, (head + 1) * size)

        def attend(row, mine=mine, head=head):
            at = pl.ds(row, ROWS)
            scores = contract_cols(q_ref[at, mine], k_ref[:, mine]) * size**-0.5
            visible = row_ref[...] <= column_ref[at, :]
            scores = jnp.where(visible, scores, NEGATIVE)
            top = jnp.max(scores, axis=1, keepdims=True)
            expo = jnp.where(visible, jnp.exp(scores - top), 0.0)
            total = jnp.sum(expo, axis=1, keepdims=True)
            top_ref[head, at, :] = top
            total_ref[head, at, :] = total
            mixed_ref[at, mine] = dot(expo.astype(bf16), v_ref[:, mine]) / total

        row_chunks(amount, attend)

    for base, ref in ((0, oa_ref), (half, ob_ref)):

        def project_out(row, base=base, ref=ref):
            mixed = mixed_ref[pl.ds(base + row, ROWS), :].astype(bf16)
            for i in range(blocks):
                weights = w_ref[i, :, :, 3 * part :].reshape(part, width // blocks)
                into = slice(i * width // blocks, (i + 1) * width // blocks)
                ref[pl.ds(row, ROWS), into] = dot(mixed, weights).astype(bf16)

        row_chunks(half, project_out)


def attend_back_kernel(*refs, planes, heads):
    (plane_ref, near_ref, far_ref, normed_ref, q_ref, k_ref, v_ref, mixed_ref, top_ref, total_ref) = refs[:10]
    (cos_ref, sin_ref, column_ref, row_ref) = refs[10:14]
    w_pieces = refs[14 : 14 + planes]
    rest = refs[15 + planes :]
    (da_ref, db_ref), w_grads = rest[:2], rest[2 : 2 + planes]
    (w_ref, gw_ref, dm_ref, dp_ref, dk_ref, dv_ref, sems) = rest[2 + planes :]
    bf16, f32 = jnp.bfloat16, jnp.float32
    plane = plane_ref[0]
    width = near_ref.shape[1]
    blocks, part = w_ref.shape[0], w_ref.shape[3] // 4
    size = part // heads
    half = near_ref.shape[0]
    amount = 2 * half
    w_copies = plane_copies(plane, w_pieces, lambda at: w_ref.at[:, at], sems.at[0])
    for copy in w_copies:
        copy.start()
    for copy in w_copies:
        copy.wait()

    for base, ref in ((0, near_ref), (half, far_ref)):

        def back_out(row, base=base, ref=ref):
            values = 0.0
            for i in range(blocks):
                weights = w_ref[i, :, :, 3 * part :].reshape(part, width // blocks)
                into = slice(i * width // blocks, (i + 1) * width // blocks)
                values = values + contract_cols(ref[pl.ds(row, ROWS), into], weights)
            dm_ref[pl.ds(base + row, ROWS), :] = values.astype(bf16).astype(f32)

        row_chunks(half, back_out)
    sides = [(mixed_ref[:half, :].astype(bf16), near_ref), (mixed_ref[half:, :].astype(bf16), far_ref)]
    for i in range(blocks):
        into = slice(i * width // blocks, (i + 1) * width // blocks)
        grad = sum(contract_rows(mixed, ref[:, into]) for mixed, ref in sides)
        grad = grad.astype(bf16).reshape(planes, part // planes, width // blocks)
        gw_ref[i, :, :, 3 * part :] = grad

    for head in range(heads):
        mine = slice(head * size, (head + 1) * size)
        dk_ref[...] = jnp.zeros_like(dk_ref)
        dv_ref[...] = jnp.zeros_like(dv_ref)

        def attend_back(row, mine=mine, head=head):
            at = pl.ds(row, ROWS)
            query, key, value = q_ref[at, mine], k_ref[:, mine], v_ref[:, mine]
            d_mixed, total = dm_ref[at, mine], total_ref[head, at, :]
            grad_num = (d_mixed / total).astype(bf16)
            shift = jnp.sum(d_mixed * mixed_ref[at, mine], axis=1, keepdims=True) / total
            scores = contract_cols(query, key) * size**-0.5
            visible = row_ref[...] <= column_ref[at, :]
            scores = jnp.where(visible, scores, NEGATIVE)
            expo = jnp.where(visible, jnp.exp(scores - top_ref[head, at, :]), 0.0)
            d_score = (expo * (contract_cols(grad_num, value) - shift)).astype(bf16)
            d_query = dot(d_score, key) * size**-0.5
            dp_ref[at, mine] = turn_head(d_query, cos_ref[at, :], -sin_ref[at, :]).astype(bf16)
            dk_ref[...] += contract_rows(d_score, query)
            dv_ref[...] += contract_rows(expo.astype(bf16), grad_num)

        row_chunks(amount, attend_back)
        d_key = turn_head(dk_ref[...] * size**-0.5, cos_ref[...], -sin_ref[...])
        dp_ref[:, part + head * size : part + (head + 1) * size] = d_key.astype(bf16)
        dp_ref[:, 2 * part + head * size : 2 * part + (head + 1) * size] = dv_ref[...].astype(bf16)

    pieces = 4
    step, count = width // pieces, blocks // pieces
    for i in range(pieces):
        grad = contract_rows(normed_ref[:, i * step : (i + 1) * step], dp_ref[...]).astype(bf16)
        grad = grad.reshape(count, *gw_ref.shape[1:3], 3 * part)
        gw_ref[i * count : (i + 1) * count, :, :, : 3 * part] = grad
    w_back = [
        pltpu.make_async_copy(
            gw_ref.at[:, lax.rem(plane - k + planes, planes)], w_grads[k], sems.at[1, k]
        )
        for k in range(planes)
    ]
    for copy in w_back:
        copy.start()
    for base, ref in ((0, da_ref), (half, db_ref)):

        def back_project(row, base=base, ref=ref):
            values = contract_cols(
                dp_ref[pl.ds(base + row, ROWS), :], w_ref[:, :, :, : 3 * part].reshape(width, 3 * part)
            )
            ref[pl.ds(row, ROWS), :] = values.astype(bf16)

        row_chunks(half, back_project)
    for copy in w_back:
        copy.wait()


def attend_call(kernel, small, blocks, pieces, outs, piece_outs, scratch, after, flops):
    far, near = pl.BlockSpec(memory_space=pltpu.HBM), pl.BlockSpec(memory_space=pltpu.VMEM)
    return pl.pallas_call(
        kernel,
        in_specs=[pl.BlockSpec(memory_space=pltpu.SMEM)]
        + [near] * len(blocks)
        + [far] * (len(pieces) + 1),
        out_specs=[near] * len(outs) + [far] * len(piece_outs),
        out_shape=[jax.ShapeDtypeStruct(shape, kind) for shape, kind in outs + piece_outs],
        scratch_shapes=scratch,
        compiler_params=pltpu.CompilerParams(vmem_limit_bytes=VMEM),
        cost_estimate=pl.CostEstimate(flops=flops, bytes_accessed=30_000_000, transcendentals=0),
    )(small, *blocks, *pieces, after)


def attend(plane, rows, gain, tables, pieces, heads, after):
    bf16, f32 = jnp.bfloat16, jnp.float32
    half, width = rows[0].shape
    planes = len(pieces)
    n_ctx, depth, four = pieces[0].shape
    part = four // 4
    outs = [((half, width), bf16)] * 2 + [((2 * half, width), bf16)]
    outs += [((2 * half, part), bf16)] * 3 + [((2 * half, part), f32)]
    outs += [((heads, 2 * half, 1), f32)] * 2
    return attend_call(
        functools.partial(attend_kernel, planes=planes, heads=heads),
        plane,
        [*rows, gain, *tables],
        pieces,
        outs,
        [],
        [
            pltpu.VMEM((n_ctx, planes, depth, four), bf16),
            pltpu.SemaphoreType.DMA((1, planes)),
        ],
        after,
        4 * half * width * 4 * part + 16 * half * half * part,
    )


def attend_back(plane, rows, saved, tables, pieces, heads, after):
    bf16, f32 = jnp.bfloat16, jnp.float32
    half, width = rows[0].shape
    planes = len(pieces)
    n_ctx, depth, four = pieces[0].shape
    part = four // 4
    made = attend_call(
        functools.partial(attend_back_kernel, planes=planes, heads=heads),
        plane,
        [*rows, *saved, *tables],
        pieces,
        [((half, width), bf16)] * 2,
        [(pieces[0].shape, bf16)] * planes,
        [
            pltpu.VMEM((n_ctx, planes, depth, four), bf16),
            pltpu.VMEM((n_ctx, planes, depth, four), bf16),
            pltpu.VMEM((2 * half, part), f32),
            pltpu.VMEM((2 * half, 3 * part), bf16),
            pltpu.VMEM((2 * half, part // heads), f32),
            pltpu.VMEM((2 * half, part // heads), f32),
            pltpu.SemaphoreType.DMA((2, planes)),
        ],
        after,
        4 * half * width * 8 * part + 40 * half * half * part,
    )
    return made[:2], list(made[2:])


def rows_kernel(left_ref, right_ref, *refs):
    refs[-1][0] = contract_rows(left_ref[0], right_ref[0])


def shared_kernel(xa_ref, xb_ref, ga_ref, gb_ref, hidden_ref, joined_ref, *refs):
    into_ref, down_ref = refs[-2:]
    size = GROUP * BLOCK
    places = spans_of(ga_ref, gb_ref, BLOCK + EXTRA)
    for i, (x_place, g_place) in enumerate(zip(spans_of(xa_ref, xb_ref), places, strict=True)):
        at = slice(i * size, (i + 1) * size)
        into = contract_rows(joined_ref[at, :], read_span(*x_place))
        down = contract_rows(hidden_ref[at, :], read_span(*g_place))
        into_ref[...] = into if i == 0 else into_ref[...] + into
        down_ref[...] = down if i == 0 else down_ref[...] + down


def held_whole(*shape):
    return pl.BlockSpec(shape, lambda j: (0,) * len(shape), pipeline_mode=pl.Buffered(1))


def expert_call(
    kernel, owners, operands, specs, outs, out_specs, kept, after, scratch, flops, moved
):
    return pl.pallas_call(
        functools.partial(kernel, carried=len(kept) + 1),
        grid=(owners,),
        in_specs=specs + [pl.BlockSpec(memory_space=pl.ANY)] * (len(kept) + 1),
        out_specs=out_specs,
        out_shape=[jax.ShapeDtypeStruct(shape, kind) for shape, kind in outs],
        scratch_shapes=scratch,
        input_output_aliases={len(operands) + i: i for i in range(len(kept))},
        compiler_params=pltpu.CompilerParams(vmem_limit_bytes=VMEM),
        cost_estimate=pl.CostEstimate(flops=flops, bytes_accessed=moved, transcendentals=0),
    )(*operands, *kept, after)


def growing(k, rows, columns):
    return pl.BlockSpec((1, rows, columns), lambda j: (j, k, 0))


def weights_of(array):
    depth = 2 if array.shape[0] > 1 else 1
    return pl.BlockSpec(
        (1,) + array.shape[1:], lambda j: (j, 0, 0), pipeline_mode=pl.Buffered(depth)
    )


def early(k, planes, grads, slots, w_down, s_down, kept, after):
    bf16, f32 = jnp.bfloat16, jnp.float32
    owners, units, width = w_down.shape
    half = grads[0].shape[0] * BLOCK // (BLOCK + EXTRA)
    rows, lane = 2 * half // BLOCK * CAP, s_down.shape[0]
    outs = [
        ((owners, planes * rows, width), bf16),
        ((owners, planes * rows, units), f32),
        ((2 * half, lane), f32),
    ]
    taken, dh, dhs = expert_call(
        early_kernel,
        owners,
        [*grads, slots, w_down, s_down],
        [held_whole(*grads[0].shape)] * 2
        + [held_whole(*slots.shape), weights_of(w_down), held_whole(*s_down.shape)],
        outs,
        [growing(k, rows, width), growing(k, rows, units), held_whole(2 * half, lane)],
        kept,
        after,
        [pltpu.VMEM((owners, rows, width), bf16)],
        2 * owners * rows * width * (units + GROUP * BLOCK) + 4 * half * width * lane,
        2 * owners * width * (units + 2 * rows) + 4 * half * width,
    )
    return [taken, dh], dhs


def middle(
    k, planes, first, rows_x, router_t, mask, slots, w_in, s_in, dh, dhs, kept, after
):
    bf16, f32 = jnp.bfloat16, jnp.float32
    owners, width, joined = w_in.shape
    half = rows_x[0].shape[0]
    rows, lane = 2 * half // BLOCK * CAP, dhs.shape[1]
    outs = [
        ((owners, planes * rows, width), bf16),
        ((owners, planes * rows, joined // 2), bf16),
        ((owners, planes * rows, joined), bf16),
        ((half // BLOCK * (BLOCK + EXTRA), width), bf16),
        ((half // BLOCK * (BLOCK + EXTRA), width), bf16),
        ((EXPERTS, 2 * half), f32),
        ((owners, 2 * half), f32),
        ((2 * half, lane), bf16),
        ((2 * half, 2 * lane), bf16),
    ]
    made = expert_call(
        middle_kernel,
        owners,
        [first, *rows_x, router_t, mask, slots, w_in, s_in, dh, dhs],
        [pl.BlockSpec(memory_space=pltpu.SMEM)]
        + [held_whole(half, width)] * 2
        + [held_whole(*a.shape) for a in (router_t, mask, slots)]
        + [weights_of(w_in), held_whole(*s_in.shape), growing(k, rows, joined // 2)]
        + [held_whole(*dhs.shape)],
        outs,
        [growing(k, rows, width), growing(k, rows, joined // 2), growing(k, rows, joined)]
        + [held_whole(*shape) for shape, _ in outs[3:]],
        kept,
        after,
        [
            pltpu.VMEM((owners, rows, width), bf16),
            pltpu.VMEM((owners, rows, width), bf16),
            pltpu.VMEM((owners, rows, 1), f32),
        ],
        4 * owners * rows * width * (joined + GROUP * BLOCK) + 16 * half * width * lane,
        2 * owners * width * (joined + 2 * rows) + 8 * half * width,
    )
    return list(made[:3]), made[3:5], made[5:]


def late(k, planes, first, hidden, taken, slots, gates, shared, w_down, s_down, kept, after):
    bf16, f32 = jnp.bfloat16, jnp.float32
    owners, units, width = w_down.shape
    half = shared.shape[0] // 2
    rows = 2 * half // BLOCK * CAP
    outs = [
        ((owners, hidden.shape[1], width), bf16),
        ((half, width), bf16),
        ((half, width), bf16),
    ]
    made = expert_call(
        late_kernel,
        owners,
        [first, hidden, taken, slots, gates, shared, w_down, s_down],
        [pl.BlockSpec(memory_space=pltpu.SMEM), growing(k, rows, units), growing(k, rows, width)]
        + [held_whole(*a.shape) for a in (slots, gates, shared)]
        + [weights_of(w_down), held_whole(*s_down.shape)],
        outs,
        [growing(k, rows, width)] + [held_whole(*shape) for shape, _ in outs[1:]],
        kept,
        after,
        [pltpu.VMEM((owners, rows, width), bf16)],
        2 * owners * rows * width * (units + GROUP * BLOCK) + 4 * half * width * s_down.shape[0],
        2 * owners * width * (units + 2 * rows) + 4 * half * width,
    )
    return list(made[:1]), made[1:]


def rows_grad(left, right, owner, count, kept, after):
    owners, amount, wide = left.shape
    narrow = right.shape[2]
    depth = pl.Buffered(2 if count > 1 else 1)
    at = lambda j: (owner + j, 0, 0)
    return pl.pallas_call(
        rows_kernel,
        grid=(count,),
        in_specs=[
            pl.BlockSpec((1, amount, wide), at, pipeline_mode=depth),
            pl.BlockSpec((1, amount, narrow), at, pipeline_mode=depth),
        ]
        + [pl.BlockSpec(memory_space=pl.ANY)] * (len(kept) + 1),
        out_specs=pl.BlockSpec((1, wide, narrow), at, pipeline_mode=depth),
        out_shape=jax.ShapeDtypeStruct((owners, wide, narrow), jnp.float32),
        input_output_aliases={2: 0} if kept else {},
        compiler_params=pltpu.CompilerParams(vmem_limit_bytes=VMEM),
        cost_estimate=pl.CostEstimate(
            flops=2 * count * amount * wide * narrow,
            bytes_accessed=4 * count * wide * narrow,
            transcendentals=0,
        ),
    )(left, right, *kept, after)


def shared_grads(rows_x, rows_g, hidden, joined, after):
    half, width = rows_x[0].shape
    near = pl.BlockSpec(memory_space=pltpu.VMEM)
    outs = [(joined.shape[1], width), (hidden.shape[1], width)]
    return pl.pallas_call(
        shared_kernel,
        in_specs=[near] * 6 + [pl.BlockSpec(memory_space=pltpu.HBM)],
        out_specs=[near] * 2,
        out_shape=[jax.ShapeDtypeStruct(shape, jnp.float32) for shape in outs],
        compiler_params=pltpu.CompilerParams(vmem_limit_bytes=VMEM),
        cost_estimate=pl.CostEstimate(
            flops=4 * half * width * (joined.shape[1] + hidden.shape[1]),
            bytes_accessed=8 * half * width,
            transcendentals=0,
        ),
    )(*rows_x, *rows_g, hidden, joined, after)


def local(
    tokens,
    gain_attn,
    w_qkv,
    w_out,
    gain_ffn,
    w_router,
    w_shared_in,
    w_shared_down,
    w_expert_in,
    w_expert_down,
    routes,
    plan,
    cotangent,
):
    n_ctx, planes = lax.axis_size("ctx"), lax.axis_size("fsdp")
    devices = n_ctx * planes
    ctx, plane = lax.axis_index("ctx"), lax.axis_index("fsdp")
    device = ctx * planes + plane
    amount, width = tokens.shape[1:]
    head_size = width // HEADS
    heads = HEADS // n_ctx
    part = heads * head_size
    rows = width // devices
    per_owner = w_expert_in.shape[0]
    units = w_shared_down.shape[0]
    bf16, f32 = jnp.bfloat16, jnp.float32
    order = jnp.array(plane_order(), jnp.int32)
    places = order ^ ctx

    clock = Clock()

    expert_ids = jnp.arange(EXPERTS, dtype=jnp.int32)
    own_mask = jnp.sum((expert_ids[:, None, None] == routes[0].T[None]).astype(f32), axis=1)
    before = (jnp.arange(amount)[:, None] < jnp.arange(amount)[None, :]).astype(bf16)
    ranking = jnp.where(own_mask > 0, dot(own_mask.astype(bf16), before), -1.0)

    qkv_part = w_qkv.reshape(rows, 3, n_ctx, part).transpose(2, 0, 1, 3).reshape(n_ctx, rows, 3 * part)
    qkv_part = lax.all_to_all(qkv_part, "ctx", split_axis=0, concat_axis=0, tiled=True)
    sequence = Transfer(gather_plane(tokens[0], False))
    small = jnp.concatenate([ranking.astype(bf16), jnp.pad(w_router, ((0, 0), (0, amount - EXPERTS)))])
    small = small.reshape(-1, width)
    held = small.shape[0]
    small = jnp.pad(small, ((0, EXTRA - held), (0, 0)))
    own_grads = jnp.concatenate([cotangent[0], small], axis=0)
    grads = [Transfer(gather_plane(own_grads, False))]
    grad_blocks = [Transfer(turned(own_grads, k)) for k in range(1, min(3, planes))]
    (qkv_part,) = stage(clock, [sequence, *grads, *grad_blocks], [qkv_part])

    out_part = w_out.reshape(rows, n_ctx, part).transpose(1, 0, 2)
    ring_w = Transfer(ring(jnp.concatenate([qkv_part, out_part], axis=2)))
    gains = jnp.concatenate([gain_attn, gain_ffn])
    gains = Transfer(exchanged(clock.now(jnp.broadcast_to(gains[None], (devices, 2 * rows)))))
    shared_in = w_shared_in.reshape(rows, 2, devices, units).transpose(2, 0, 1, 3)
    shared_in = shared_in.reshape(devices, rows, 2 * units)

    half_block = amount // 2
    half_ids = (places[:, None] * 2 + jnp.arange(2, dtype=jnp.int32)[None, :]).reshape(-1)
    placed = jnp.sum(
        jnp.where(half_ids[:, None] == jnp.arange(plan.shape[0])[None, :], plan[None, :], 0), axis=1
    )
    pos = (placed[:, None] * half_block + jnp.arange(half_block)[None, :]).reshape(-1).astype(f32)
    frequency = ROPE_BASE ** (-2.0 * jnp.arange(head_size // 2, dtype=f32) / head_size)
    angles = pos[:, None] * frequency[None, :]
    cosine, sine = jnp.cos(angles), jnp.sin(angles)
    tables = [
        jnp.concatenate([cosine, cosine], axis=1),
        jnp.concatenate([-sine, sine], axis=1),
        pos[:, None],
        pos[None, :],
    ]
    shared_in, *tables = stage(clock, [ring_w, gains, sequence, *grads], [shared_in, *tables])
    if planes > 1:
        grads.append(Transfer(gather_plane(grad_blocks[0].result, False)))
    stage(clock, [ring_w, gains, sequence, *grads])
    gain_one, gain_two = (
        gains.result[:, at : at + rows].reshape(width).astype(f32) for at in (0, rows)
    )
    seq_rows = finish(clock, sequence)[0]

    first_expert = lax.rem(device * per_owner, EXPERTS)
    first = jnp.stack([first_expert, device * per_owner // EXPERTS]).astype(jnp.int32)
    back = lax.rem(plane - jnp.arange(planes, dtype=jnp.int32) + planes, planes)
    sources = jnp.arange(n_ctx, dtype=jnp.int32) ^ ctx
    sources = sources // 2 + (sources % 2) * (n_ctx // 2)
    sources = (back[None, :] * n_ctx + sources[:, None]).reshape(-1)
    ranks, slots, routers = [], [], []

    def small_of(k):
        sides = [side.reshape(-1, amount + EXTRA, width)[:, amount : amount + held] for side in grads[k].result]
        came = jnp.concatenate(sides, axis=0).reshape(n_ctx, EXPERTS + rows, amount)
        ranks.append(came[:, :EXPERTS])
        routers.append(came[:, EXPERTS:])
        mine = lax.dynamic_slice_in_dim(came, first_expert, per_owner, 1).astype(f32)
        offset = (CAP * (jnp.arange(n_ctx) % GROUP)).astype(f32)[:, None, None]
        mine = jnp.where(mine >= 0, mine + offset, -1.0)
        slots.append(mine.transpose(1, 0, 2).reshape(per_owner, n_ctx * amount))

    lane = -(-units // BLOCK) * BLOCK
    s_down = jnp.pad(w_shared_down, ((0, lane - units), (0, 0)))
    early_kept, dhs = [], []

    def grads_stage(transfers, beside=(), work=True):
        nonlocal early_kept
        k, made = len(dhs), []
        if work and k < planes and k < len(grads) and grads[k].done:
            small_of(k)
            early_kept, made = early(
                k, planes, grads[k].result, slots[k], w_expert_down, s_down, early_kept, clock.token
            )
            made = [made]
        arrays = stage(clock, [*transfers, *grads, *grad_blocks], [*beside, *made])
        dhs.extend(arrays[len(beside) :])
        k = len(grads)
        if 2 <= k < planes and grad_blocks[k - 1].done and grads[-1].step is not grads[-1].opening:
            grads.append(Transfer(gather_plane(grad_blocks[k - 1].result, False)))
            grads[-1].opening = grads[-1].step
            if len(grad_blocks) < planes - 1:
                ahead = len(grad_blocks) + 1
                source = own_grads if ahead == 3 else grad_blocks[-1].result
                grad_blocks.append(Transfer(turned(clock.now(source), ahead if ahead == 3 else 1)))
        return arrays[: len(beside)]

    grads[-1].opening = None
    while not ring_w.done:
        grads_stage([ring_w])
    pieces = ring_w.result
    shared_in = Transfer(exchanged(clock.now(shared_in)))
    own_rows = tokens[0].astype(f32)
    plane_id = plane.reshape(1).astype(jnp.int32)
    *attended, normed, query, key, value, mixed, tops, totals = attend(
        plane_id, seq_rows, gain_one[None, :], tables, pieces, heads, clock.token
    )
    saved = [normed, query, key, value, mixed, tops, totals]
    attended = grads_stage([shared_in], attended)
    attended = Transfer(scatter_plane(*attended))
    while not attended.done:
        grads_stage([attended])
    residual = own_rows + attended.result.astype(f32)
    ffn_own = rms_scale(residual, gain_two).astype(bf16)
    shared_in = shared_in.result.reshape(width, 2, units)
    s_in = jnp.pad(shared_in, ((0, 0), (0, 0), (0, lane - units))).reshape(width, 2 * lane)

    ffn, d_parts = [Transfer(gather_plane(ffn_own))], []
    block, d_sum = Transfer(turned(ffn_own)), None
    mid_kept, mids, late_kept, out_parts, out_sum, router_t = [], [], [], [], None, None

    def do_late():
        nonlocal late_kept
        if len(out_parts) == planes:
            return []
        k = (len(out_parts) + 1) % planes
        late_kept, pair = late(
            k, planes, first, mid_kept[1], early_kept[0], slots[k], mids[k][0], mids[k][2],
            w_expert_down, s_down, late_kept, clock.token,
        )
        return list(pair)

    def outs_stage(transfers, beside=(), moving=None):
        nonlocal out_sum
        pair = do_late() if not beside else []
        if out_sum is None and len(out_parts) == planes and out_parts[0].done:
            out_sum = Transfer(staged_sum(out_parts))
        going = [t for t in out_parts if not t.done]
        fresh = [t for t in going if t.step is t.opening]
        going = [t for t in going if t not in fresh]
        if moving is not None:
            going = going[:moving]
        arrays = stage(
            clock, [*transfers, *going, *fresh, *([out_sum] if out_sum else [])], [*beside, *pair]
        )
        if pair:
            out_parts.append(Transfer(scatter_plane(*arrays)))
            out_parts[-1].opening = out_parts[-1].step
            arrays = []
        return arrays

    while d_sum is None or not d_sum.done:
        going = [*ffn, *d_parts, block, *([d_sum] if d_sum else [])]
        k = len(mids)
        if router_t is None and len(routers) == planes:
            router_full = jnp.stack(routers).reshape(devices, rows, amount)
            router_full = jnp.take(router_full, sources, axis=0).reshape(width, amount)[:, :EXPERTS]
            router_t = router_full.T
        if k < planes and ffn[k].done and len(dhs) > k and router_t is not None:
            mid_kept, pair, made = middle(
                k, planes, first, ffn[k].result, router_t, ranks[k], slots[k], w_expert_in, s_in,
                early_kept[1], dhs[k], mid_kept, clock.token,
            )
            mids.append(made)
            pair = grads_stage(going, list(pair), work=False)
            d_parts.append(Transfer(scatter_plane(*pair)))
        elif k == planes:
            outs_stage(going, moving=1 if d_parts[-1].done else 0)
        else:
            grads_stage(going)
        if len(ffn) < planes and block.done:
            ffn.append(Transfer(gather_plane(block.result)))
            if len(ffn) < planes:
                block = Transfer(turned(block.result))
        if d_sum is None and len(d_parts) == planes and d_parts[min(1, planes - 1)].done:
            d_sum = Transfer(staged_sum(d_parts[1:] + d_parts[:1]))
    rows_in, hidden, d_joined = mid_kept
    gates = mids[0][0]

    dgate = d_sum.result[amount:].astype(f32).reshape(4, EXPERTS, amount)
    dgate = jnp.sum(dgate, axis=0)
    gates_own = gates[:, :amount]
    dlogits = gates_own * (dgate - jnp.sum(gates_own * dgate, axis=0, keepdims=True))
    dlogits_b = dlogits.astype(bf16).T
    d_ffn = d_sum.result[:amount].astype(f32) + contract_cols(dlogits_b, router_full)
    second_back = jax.vjp(rms_scale, residual, gain_two)[1](d_ffn)
    d_residual = cotangent[0].astype(f32) + second_back[0]

    d_attn = Transfer(gather_plane(d_residual.astype(bf16)))
    outs_stage([d_attn], moving=0)
    while len(out_parts) < planes:
        outs_stage([], moving=1)
    shared = None
    while not d_attn.done or shared is None:
        if shared is not None:
            outs_stage([d_attn], moving=1)
            continue
        parts = [
            shared_grads(ffn[k].result, grads[k].result, mids[k][2], mids[k][3], clock.token)
            for k in range(planes)
        ]
        into, shared_down_grad = (sum(one) for one in zip(*parts, strict=True))
        into = into.reshape(2, lane, width)[:, :units].reshape(2 * units, width).T
        small = contract_rows(ffn_own, clock.now(dlogits_b))
        shared = jnp.concatenate([into, small, second_back[1][:, None]], axis=1).astype(bf16)
        shared = jnp.pad(shared, ((0, 0), (0, -shared.shape[1] % BLOCK)))
        shared = shared.reshape(devices, rows, -1)
        shared, shared_down_grad = outs_stage([d_attn], [shared, shared_down_grad], moving=1)
    shared = Transfer(exchanged(shared))

    d_normed, ring_grad = attend_back(
        plane_id, d_attn.result, saved, tables, pieces, heads, clock.token
    )
    d_normed = outs_stage([shared], list(d_normed), moving=1)
    ring_grad = Transfer(ring_sum(ring_grad))
    d_normed = Transfer(scatter_plane(*d_normed))

    first_half = -(-per_owner // 2)
    (dy,) = late_kept
    work = [lambda kept: rows_grad(rows_in, d_joined, 0, first_half, kept, clock.token)]
    if first_half < per_owner:
        work.append(
            lambda kept: rows_grad(
                rows_in, d_joined, first_half, per_owner - first_half, kept, clock.token
            )
        )
    work.append(lambda kept: rows_grad(hidden, dy, 0, per_owner, [], clock.token))
    made = []
    while work or not (ring_grad.done and d_normed.done):
        if work:
            one = work.pop(0)(made)
            (one,) = outs_stage([ring_grad, d_normed], [one], moving=1)
            if work:
                made = [one]
            else:
                (expert_in_grad,), expert_down_grad = made, one
        else:
            outs_stage([ring_grad, d_normed], [], moving=1)
    ring_grad = ring_grad.result
    qkv_grad = lax.all_to_all(ring_grad[:, :, : 3 * part], "ctx", split_axis=0, concat_axis=0, tiled=True)
    out_grad = ring_grad[:, :, 3 * part :].transpose(1, 0, 2).reshape(rows, width).astype(f32)
    first_back = jax.vjp(lambda x: rms_scale(x, gain_one), own_rows)[1](d_normed.result.astype(f32))
    tokens_grad = d_residual + first_back[0]
    shared = clock.now(shared.result)
    shared_in_grad = shared[:, :, : 2 * units].reshape(devices, rows, 2, units)
    shared_in_grad = shared_in_grad.transpose(1, 2, 0, 3).reshape(rows, 2 * devices * units).astype(f32)
    small = jnp.sum(shared[:, :, 2 * units :].astype(f32), axis=0)
    router_grad, gain_ffn_grad = small[:, :EXPERTS], small[:, EXPERTS]
    shared_down_grad = shared_down_grad[:units]
    while out_sum is None or not out_sum.done:
        if out_sum is None and out_parts[0].done:
            out_sum = Transfer(staged_sum(out_parts))
        stage(clock, [*out_parts, *([out_sum] if out_sum else [])])
    result = (residual + out_sum.result.astype(f32)).astype(bf16)
    qkv_grad = qkv_grad.reshape(n_ctx, rows, 3, part).transpose(1, 2, 0, 3)
    qkv_grad = qkv_grad.reshape(rows, 3 * width).astype(f32)
    gain_attn_grad = jnp.sum(qkv_grad * w_qkv.astype(f32), axis=1) / gain_attn.astype(f32)
    return (
        result[None],
        tokens_grad[None],
        gain_attn_grad,
        qkv_grad,
        out_grad,
        gain_ffn_grad,
        router_grad,
        shared_in_grad,
        shared_down_grad,
        expert_in_grad,
        expert_down_grad,
    )


def solution(mesh):
    split = P(BOTH)
    matrix = P(BOTH, None)
    cube = P(BOTH, None, None)
    batch = P("fsdp", "ctx", None)
    return jax.shard_map(
        local,
        mesh=mesh,
        in_specs=(
            batch,
            split,
            matrix,
            matrix,
            split,
            matrix,
            matrix,
            matrix,
            cube,
            cube,
            batch,
            P(),
            batch,
        ),
        out_specs=(
            batch,
            batch,
            split,
            matrix,
            matrix,
            split,
            matrix,
            matrix,
            matrix,
            cube,
            cube,
        ),
        check_vma=False,
    )
```

```python
import functools

import jax
import jax.numpy as jnp
from jax import lax
from jax.experimental import pallas as pl
from jax.experimental.pallas import tpu as pltpu
from jax.sharding import PartitionSpec as P

HEADS = 16
EXPERTS = 64
CAP = 20
BLOCK = 128
EXTRA = 16
GROUP = 4
VMEM = 60 * 1024 * 1024

EPSILON = 1e-06
ROPE_BASE = 10000.0
NEGATIVE = -1e30
BOTH = ("ctx", "fsdp")


def rms_scale(values, gain):
    inverse = lax.rsqrt(jnp.mean(values * values, axis=-1, keepdims=True) + EPSILON)
    return values * inverse * gain


def dot(left, right):
    return jnp.dot(left, right, preferred_element_type=jnp.float32)


def contract_rows(left, right):
    return lax.dot_general(
        left, right, (((0,), (0,)), ((), ())), preferred_element_type=jnp.float32
    )


def contract_cols(left, right):
    return lax.dot_general(
        left, right, (((1,), (1,)), ((), ())), preferred_element_type=jnp.float32
    )


def plane_order():
    count = lax.axis_size("ctx")
    return list(range(0, count, 2)) + list(range(1, count, 2))


def ctx_bits():
    count = lax.axis_size("ctx")
    return [1 << i for i in range(1, count.bit_length() - 1)]


def swap(values, bit):
    count = lax.axis_size("ctx")
    return lax.ppermute(values, "ctx", [(i, i ^ bit) for i in range(count)])


def turn(values, step=1):
    count = lax.axis_size("fsdp")
    return lax.ppermute(values, "fsdp", [(i, (i + step) % count) for i in range(count)])


def add(left, right):
    return (left.astype(jnp.float32) + right.astype(jnp.float32)).astype(left.dtype)


class Step:
    def __init__(self, sent, outs=(), beside=()):
        self.sent, self.outs, self.beside = list(sent), list(outs), list(beside)


class Transfer:
    def __init__(self, steps):
        self.steps, self.step, self.done, self.result = steps, None, False, None
        self.advance(None)

    def advance(self, arrived):
        try:
            self.step = self.steps.send(arrived)
        except StopIteration as stop:
            self.step, self.done, self.result = None, True, stop.value


class Clock:
    def __init__(self):
        self.token = jnp.zeros((8, 128), jnp.float32)

    def now(self, values):
        return values + self.token[0, 0].astype(values.dtype)


CHUNK = 16


def add_rows(target, at, sources, rows):
    @pl.loop(0, rows // CHUNK)
    def _(i):
        row = pl.multiple_of(i * CHUNK, CHUNK)
        total = sum(ref[pl.ds(row, CHUNK), :].astype(jnp.float32) for ref in sources)
        target[pl.ds(at + row, CHUNK), :] = total.astype(target.dtype)


def make_outs(inputs, outs, plans, scratch):
    held, terms, (in_sems, out_sems) = scratch[: len(outs)], scratch[len(outs) : -2], scratch[-2:]
    parts, copies, used = [], 0, 0
    for buffer, out, plan in zip(held, outs, plans, strict=True):
        at = 0
        for rows, sources in plan:
            place = buffer.at[pl.ds(at, rows)]
            into = [place] if len(sources) == 1 else list(terms[used : used + len(sources)])
            used += 0 if len(sources) == 1 else len(sources)
            arriving = []
            for (i, start), target in zip(sources, into, strict=True):
                source = inputs[i].at[pl.ds(start, rows)]
                arriving.append(pltpu.make_async_copy(source, target, in_sems.at[copies]))
                arriving[-1].start()
                copies += 1
            leaving = pltpu.make_async_copy(place, out.at[pl.ds(at, rows)], out_sems.at[len(parts)])
            parts.append((arriving, buffer, at, into, rows, leaving))
            at += rows
    for arriving, buffer, at, into, rows, leaving in parts:
        for copy in arriving:
            copy.wait()
        if len(arriving) > 1:
            add_rows(buffer, at, into, rows)
        leaving.start()
    for *_, leaving in parts:
        leaving.wait()


def stage(clock, transfers, beside=()):
    active = [t for t in transfers if not t.done]
    making = [t for t in active if t.step.outs]
    waited = [a for t in active if not t.step.outs for a in t.step.sent]
    passed = [clock.token, *beside]
    taken, plans, kinds = [], [], []
    for t in making:
        base = len(taken)
        taken += t.step.sent + t.step.beside
        for plan in t.step.outs:
            plans.append([(rows, [(base + i, start) for i, start in terms]) for rows, terms in plan])
            like = t.step.sent[0]
            kinds.append((sum(rows for rows, _ in plan), like.shape[1], like.dtype))
    scratch = [pltpu.VMEM((rows, width), kind) for rows, width, kind in kinds]
    count = 0
    for (_, width, kind), plan in zip(kinds, plans, strict=True):
        for rows, terms in plan:
            count += len(terms)
            if len(terms) > 1:
                scratch += [pltpu.VMEM((rows, width), kind)] * len(terms)
    if making:
        scratch += [pltpu.SemaphoreType.DMA((count,)), pltpu.SemaphoreType.DMA((sum(map(len, plans)),))]
    first = len(passed) + len(waited)

    def kernel(*refs):
        outs = first + len(taken) + len(passed)
        if making:
            make_outs(
                refs[first : first + len(taken)],
                refs[outs : outs + len(kinds)],
                plans,
                refs[outs + len(kinds) :],
            )

    far = pl.BlockSpec(memory_space=pl.ANY)
    arrays = pl.pallas_call(
        kernel,
        in_specs=[far] * (first + len(taken)),
        out_specs=[far] * (len(passed) + len(kinds)),
        out_shape=[jax.ShapeDtypeStruct(a.shape, a.dtype) for a in passed]
        + [jax.ShapeDtypeStruct((rows, width), kind) for rows, width, kind in kinds],
        scratch_shapes=scratch,
        input_output_aliases={i: i for i in range(len(passed))},
        compiler_params=pltpu.CompilerParams(vmem_limit_bytes=VMEM),
    )(*passed, *waited, *taken)
    clock.token, given, arrays = arrays[0], arrays[1 : len(passed)], arrays[len(passed) :]
    results = {}
    for t in making:
        results[id(t)], arrays = arrays[: len(t.step.outs)], arrays[len(t.step.outs) :]
    for t in active:
        t.advance(results[id(t)] if id(t) in results else t.step.sent)
    return given


def finish(clock, *transfers):
    while not all(t.done for t in transfers):
        stage(clock, transfers)
    return [t.result for t in transfers]


def turned(block, step=1):
    (block,) = yield Step([turn(block, step)])
    return block


def ring(block):
    held = [block]
    for _ in range(lax.axis_size("fsdp") - 1):
        (block,) = yield Step([turn(block)])
        held.append(block)
    return held


def ring_sum(pieces):
    total = pieces[min(1, len(pieces) - 1)]
    for piece in pieces[2:] + (pieces[:1] if len(pieces) > 1 else []):
        rows = total.shape[0]
        (total,) = yield Step([turn(total)], [[(rows, [(0, 0), (1, 0)])]], [piece])
    return total


def staged_sum(parts):
    total = parts[0].result
    for part in parts[1:]:
        (total,) = yield Step([turn(total)])
        while not part.done:
            (total,) = yield Step([total])
        total = add(part.result, total)
    return total


def to_all(values):
    return lax.all_to_all(values, BOTH, split_axis=0, concat_axis=0, tiled=True)


def exchanged(values):
    (values,) = yield Step([to_all(values)])
    return values


def gather_plane(block, direct=True):
    bits = ctx_bits()
    amount = block.shape[0]
    half = -(-amount // 2 // CHUNK) * CHUNK
    rest = amount - half
    if len(bits) == 2 and direct:
        others = [swap(block, place) for place in (bits[0], bits[1], bits[0] | bits[1])]
        (near,) = yield Step(others, [[(amount, [(i, 0)]) for i in (3, 0, 1, 2)]], [block])
    elif len(bits) == 2:
        x_bit, y_bit = bits
        over = [swap(block, x_bit), swap(block, y_bit)]
        first, second = yield Step(over, [[(half, [(0, 0)])], [(rest, [(1, half)])]])
        corner = [swap(first, y_bit), swap(second, x_bit)]
        parts = [(amount, [(i, 0)]) for i in (2, 3, 4)] + [(half, [(0, 0)]), (rest, [(1, 0)])]
        (near,) = yield Step(corner, [parts], [block, *over])
    else:
        near = block
        for bit in bits:
            rows = near.shape[0]
            (near,) = yield Step([swap(near, bit)], [[(rows, [(1, 0)]), (rows, [(0, 0)])]], [near])
    (far,) = yield Step([swap(near, 1)])
    return near, far


def scatter_plane(near, far):
    bits = ctx_bits()
    size = near.shape[0] >> len(bits)
    if len(bits) == 2:
        parts = [[(size, [(0, i * size), (1, i * size)])] for i in range(4)]
        own, part_x, part_y, corner = yield Step([swap(far, 1)], parts, [near])
        back = [swap(part_x, bits[0]), swap(part_y, bits[1]), swap(corner, bits[0] | bits[1])]
        (total,) = yield Step(back, [[(size, [(i, 0) for i in range(4)])]], [own])
        return total
    rows = near.shape[0]
    (held,) = yield Step([swap(far, 1)], [[(rows, [(0, 0), (1, 0)])]], [near])
    for bit in reversed(bits):
        rows //= 2
        (held,) = yield Step([swap(held[rows:], bit)], [[(rows, [(0, 0), (1, 0)])]], [held])
    return held


def gate_parts(first, second):
    sigmoid = 1.0 / (1.0 + jnp.exp(-first))
    return sigmoid, first * sigmoid * second


def gate_back(first, second, sigmoid, upstream):
    silu = first * sigmoid
    return upstream * second * (sigmoid + silu * (1.0 - sigmoid)), upstream * silu


def pick(slot_ref, owner, span):
    tokens = GROUP * BLOCK
    slots = slot_ref[pl.ds(owner, 1), span * tokens : (span + 1) * tokens]
    ids = lax.broadcasted_iota(jnp.int32, (GROUP * CAP, tokens), 0).astype(jnp.float32)
    return ids == slots


def pick_all(slot_ref, span):
    chosen = [pick(slot_ref, owner, span).astype(jnp.bfloat16) for owner in range(slot_ref.shape[0])]
    return jnp.concatenate(chosen, axis=0)


def spans_of(first_ref, second_ref, stride=BLOCK):
    per_side = first_ref.shape[0] // (GROUP * stride)
    return [
        (ref, [(n * GROUP + i) * stride for i in range(GROUP)])
        for ref in (first_ref, second_ref)
        for n in range(per_side)
    ]


def read_span(ref, starts):
    if starts[1] == starts[0] + BLOCK:
        return ref[starts[0] : starts[0] + GROUP * BLOCK, :]
    return jnp.concatenate([ref[at : at + BLOCK, :] for at in starts], axis=0)


def write_span(ref, starts, values):
    for i, at in enumerate(starts):
        ref[at : at + BLOCK, :] = values[i * BLOCK : (i + 1) * BLOCK].astype(ref.dtype)


def slots_at(span):
    return slice(span * GROUP * CAP, (span + 1) * GROUP * CAP)


def tokens_at(span):
    return slice(span * GROUP * BLOCK, (span + 1) * GROUP * BLOCK)


def streamed(source, buffers, sems, step, count):
    def copy(owner):
        return pltpu.make_async_copy(source.at[owner], buffers.at[owner % 2], sems.at[owner % 2])

    @pl.when(step == 0)
    def _():
        copy(0).start()

    @pl.when(step + 1 < count)
    def _():
        copy(step + 1).start()

    def arrived():
        copy(step).wait()
        return buffers[step % 2]

    return arrived


def early_kernel(*refs, carried):
    first_ref, ga_ref, gb_ref, down_ref, s_down_ref = refs[:5]
    (rows_ref, dh_ref, router_out, dhs_ref, ranks_ref, slot_ref, kept_ref, router_ref, w_ref, w_sems, sem) = refs[
        5 + carried :
    ]
    owners = slot_ref.shape[0]
    step = pl.program_id(0)
    weights = streamed(down_ref, w_ref, w_sems, step, owners)

    @pl.when(step == 0)
    def _():
        places = spans_of(ga_ref, gb_ref, BLOCK + EXTRA)
        blocks, count = router_ref.shape[:2]
        for block, (ref, at) in enumerate((ref, at) for ref, starts in places for at in starts):
            place = 2 * block if 2 * block < blocks else 2 * block - blocks + 1
            came = ref[at + BLOCK : at + BLOCK + EXTRA, :]
            lanes = slice(block * BLOCK, (block + 1) * BLOCK)
            for i in range((EXPERTS + count) // EXTRA):
                tile, row = came[:, i * BLOCK : (i + 1) * BLOCK], i * EXTRA
                if row < EXPERTS:
                    ranks_ref[row : row + EXTRA, lanes] = tile.astype(jnp.float32)
                else:
                    router_ref[first_ref[2] ^ place, row - EXPERTS : row - EXPERTS + EXTRA, :] = tile
        router_copy = pltpu.make_async_copy(router_ref, router_out.at[:, first_ref[3]], sem)
        router_copy.start()
        lane = lax.broadcasted_iota(jnp.int32, (1, slot_ref.shape[1]), 1)
        offset = (CAP * (lane // BLOCK % GROUP)).astype(jnp.float32)
        for owner in range(owners):
            ranks = ranks_ref[pl.ds(first_ref[0] + owner, 1), :]
            slot_ref[owner : owner + 1, :] = jnp.where(ranks >= 0, ranks + offset, -1.0)
        for span, place in enumerate(places):
            values = read_span(*place)
            taken = dot(pick_all(slot_ref, span), values).astype(jnp.bfloat16)
            for owner in range(owners):
                kept_ref[owner, slots_at(span), :] = taken[slots_at(owner)]
            dhs_ref[tokens_at(span), :] = contract_cols(values, s_down_ref[...])
        router_copy.wait()

    rows = kept_ref[step]
    rows_ref[0] = rows
    dh_ref[0] = contract_cols(rows, weights())


def gate_rows(first_ref, values, width):
    per_row = width // BLOCK
    rows = lax.broadcasted_iota(jnp.int32, (EXTRA, width), 0)
    groups = lax.broadcasted_iota(jnp.int32, (EXTRA, width), 1) // BLOCK
    leading = values.astype(jnp.bfloat16).astype(jnp.float32)
    total = jnp.zeros((EXTRA, width), jnp.float32)
    for owner in range(values.shape[0]):
        expert = first_ref[0] + owner
        for i, one in enumerate((leading, values - leading)):
            wide = jnp.concatenate([one[owner : owner + 1]] * per_row, axis=1)
            row = (2 * first_ref[1] + i) * (EXPERTS // per_row) + expert // per_row
            here = (rows == row) & (groups == expert % per_row)
            total = total + jnp.where(here, wide, 0.0)
    return total.astype(jnp.bfloat16)


def middle_kernel(*refs, carried):
    (first_ref, xa_ref, xb_ref, router_ref, mask_ref, slot_ref, in_ref, s_in_ref, dh_ref, dhs_ref) = refs[:10]
    (rows_ref, hidden_ref, dj_ref, da_ref, db_ref, gates_ref, dgate_ref, sh_ref, ds_ref, r_ref, z_ref, gate_ref, w_ref, w_sems) = refs[10 + carried :]
    bf16 = jnp.bfloat16
    owners = slot_ref.shape[0]
    step = pl.program_id(0)
    spans = spans_of(xa_ref, xb_ref)
    weights = streamed(in_ref, w_ref, w_sems, step, owners)

    @pl.when(step == 0)
    def _():
        for span, place in enumerate(spans):
            x = read_span(*place)
            lanes = tokens_at(span)
            mask = mask_ref[:, lanes] >= 0
            logits = jnp.where(mask, contract_cols(router_ref[...], x), NEGATIVE)
            gates = jnp.where(mask, jnp.exp(logits - jnp.max(logits, axis=0, keepdims=True)), 0.0)
            gates = gates / jnp.sum(gates, axis=0, keepdims=True)
            gates_ref[:, lanes] = gates
            expert = lax.broadcasted_iota(jnp.int32, gates.shape, 0)
            for owner in range(owners):
                own = jnp.sum(jnp.where(expert == first_ref[0] + owner, gates, 0.0), axis=0, keepdims=True)
                gate_ref[owner, slots_at(span), :] = jnp.sum(
                    jnp.where(pick(slot_ref, owner, span), own, 0.0), axis=1, keepdims=True
                )
            taken = dot(pick_all(slot_ref, span), x).astype(bf16)
            for owner in range(owners):
                r_ref[owner, slots_at(span), :] = taken[slots_at(owner)]
            joined = dot(x, s_in_ref[...])
            units = joined.shape[1] // 2
            first, second = joined[:, :units], joined[:, units:]
            sigmoid, hidden = gate_parts(first, second)
            sh_ref[lanes, :] = hidden.astype(bf16)
            back = gate_back(first, second, sigmoid, dhs_ref[lanes, :])
            ds_ref[lanes, :] = jnp.concatenate(back, axis=1).astype(bf16)

    rows = r_ref[step]
    weights_in = weights()
    joined = dot(rows, weights_in)
    units = joined.shape[1] // 2
    first, second = joined[:, :units], joined[:, units:]
    sigmoid, hidden = gate_parts(first, second)
    back = gate_back(first, second, sigmoid, gate_ref[step] * dh_ref[0])
    d_gate = jnp.sum(hidden * dh_ref[0], axis=1, keepdims=True)
    for span in range(len(spans)):
        spread = jnp.where(pick(slot_ref, step, span), d_gate[slots_at(span)], 0.0)
        dgate_ref[pl.ds(step, 1), tokens_at(span)] = jnp.sum(spread, axis=0, keepdims=True)
    d_joined = jnp.concatenate(back, axis=1).astype(bf16)
    z_ref[step] = contract_cols(d_joined, weights_in).astype(bf16)
    rows_ref[0] = rows
    hidden_ref[0] = hidden.astype(bf16)
    dj_ref[0] = d_joined

    @pl.when(step == owners - 1)
    def _():
        for span, place in enumerate(spans_of(da_ref, db_ref, BLOCK + EXTRA)):
            made = jnp.concatenate([z_ref[owner, slots_at(span), :] for owner in range(owners)], axis=0)
            total = contract_rows(pick_all(slot_ref, span), made)
            total = total + contract_cols(ds_ref[tokens_at(span), :], s_in_ref[...])
            write_span(*place, total)
            for i, at in enumerate(place[1]):
                block = span * GROUP + i
                place[0][at + BLOCK : at + BLOCK + EXTRA, :] = gate_rows(
                    first_ref, dgate_ref[:, block * BLOCK : (block + 1) * BLOCK], made.shape[1]
                )


def late_kernel(*refs, carried):
    (first_ref, hidden_ref, rows_ref, slot_ref, gates_ref, sh_ref, down_ref, s_down_ref) = refs[:8]
    (dy_ref, oa_ref, ob_ref, y_ref) = refs[8 + carried :]
    bf16 = jnp.bfloat16
    owners = slot_ref.shape[0]
    step = pl.program_id(0)
    spans = spans_of(oa_ref, ob_ref)
    partial = dot(hidden_ref[0], down_ref[0])
    rows = rows_ref[0].astype(jnp.float32)
    gates = []
    for span in range(len(spans)):
        chosen = pick(slot_ref, step, span)
        lanes = tokens_at(span)
        own = gates_ref[pl.ds(first_ref[0] + step, 1), lanes]
        gates.append(jnp.sum(jnp.where(chosen, own, 0.0), axis=1, keepdims=True))
    gate = jnp.concatenate(gates, axis=0)
    y_ref[step] = (gate * partial).astype(bf16)
    dy_ref[0] = (gate * rows).astype(bf16)

    @pl.when(step == owners - 1)
    def _():
        for span, place in enumerate(spans):
            made = jnp.concatenate([y_ref[owner, slots_at(span), :] for owner in range(owners)], axis=0)
            total = contract_rows(pick_all(slot_ref, span), made)
            total = total + dot(sh_ref[tokens_at(span), :], s_down_ref[...])
            write_span(*place, total)


ROWS = 256


def row_chunks(amount, body):
    @pl.loop(0, amount // ROWS)
    def _(i):
        body(pl.multiple_of(i * ROWS, ROWS))


def plane_copies(plane, pieces, target, sems):
    count = len(pieces)
    return [
        pltpu.make_async_copy(
            piece, target(lax.rem(plane - k + count, count)), sems.at[k]
        )
        for k, piece in enumerate(pieces)
    ]


def turn_head(values, cosine, sine):
    return values * cosine + pltpu.roll(values, values.shape[1] // 2, 1) * sine


def attend_kernel(*refs, planes, heads):
    (plane_ref, gain_ref, cos_ref, sin_ref, column_ref, row_ref) = refs[:6]
    near_out, far_out, w_pieces = refs[6], refs[7], refs[8 : 8 + planes]
    outs = refs[9 + planes : 18 + planes]
    (w_ref, x_ref, o_ref, *kept, sems) = refs[18 + planes :]
    (normed_ref, q_ref, k_ref, v_ref, mixed_ref, top_ref, total_ref) = kept
    bf16, f32 = jnp.bfloat16, jnp.float32
    plane = plane_ref[0]
    width = near_out.shape[1]
    blocks, part = w_ref.shape[0], w_ref.shape[3] // 4
    size = part // heads
    half = near_out.shape[0]
    amount = 2 * half
    copies = plane_copies(plane, w_pieces, lambda at: w_ref.at[:, at], sems.at[0])
    sides = [
        pltpu.make_async_copy(ref, x_ref.at[side], sems.at[1, side])
        for side, ref in enumerate((near_out, far_out))
    ]
    leaving = [pltpu.make_async_copy(o_ref.at[side], outs[side], sems.at[2, side]) for side in range(2)]
    leaving += [
        pltpu.make_async_copy(ref, out, sems.at[3, i])
        for i, (ref, out) in enumerate(zip(kept, outs[2:], strict=True))
    ]
    for copy in copies + sides:
        copy.start()
    for copy in copies:
        copy.wait()

    for side, base in enumerate((0, half)):
        sides[side].wait()

        def project(row, base=base, side=side):
            at = pl.ds(base + row, ROWS)
            x = x_ref[side, pl.ds(row, ROWS), :].astype(f32)
            normed = rms_scale(x, gain_ref[...]).astype(bf16)
            normed_ref[at, :] = normed
            projected = dot(normed, w_ref[:, :, :, : 3 * part].reshape(width, 3 * part))
            cosine, sine = cos_ref[at, :], sin_ref[at, :]
            for head in range(heads):
                mine = slice(head * size, (head + 1) * size)
                for target, start in ((q_ref, 0), (k_ref, part)):
                    values = projected[:, start + head * size : start + (head + 1) * size]
                    target[at, mine] = turn_head(values, cosine, sine).astype(bf16)
            v_ref[at, :] = projected[:, 2 * part :].astype(bf16)

        row_chunks(half, project)
    for copy in leaving[2:6]:
        copy.start()

    for head in range(heads):
        mine = slice(head * size, (head + 1) * size)

        def attend(row, mine=mine, head=head):
            at = pl.ds(row, ROWS)
            scores = contract_cols(q_ref[at, mine], k_ref[:, mine]) * size**-0.5
            visible = row_ref[...] <= column_ref[at, :]
            scores = jnp.where(visible, scores, NEGATIVE)
            top = jnp.max(scores, axis=1, keepdims=True)
            expo = jnp.where(visible, jnp.exp(scores - top), 0.0)
            total = jnp.sum(expo, axis=1, keepdims=True)
            top_ref[head, at, :] = top
            total_ref[head, at, :] = total
            mixed_ref[at, mine] = dot(expo.astype(bf16), v_ref[:, mine]) / total

        row_chunks(amount, attend)
    for copy in leaving[6:]:
        copy.start()

    for side, base in enumerate((0, half)):

        def project_out(row, base=base, side=side):
            mixed = mixed_ref[pl.ds(base + row, ROWS), :].astype(bf16)
            for i in range(blocks):
                weights = w_ref[i, :, :, 3 * part :].reshape(part, width // blocks)
                into = slice(i * width // blocks, (i + 1) * width // blocks)
                o_ref[side, pl.ds(row, ROWS), into] = dot(mixed, weights).astype(bf16)

        row_chunks(half, project_out)
        leaving[side].start()
    for copy in leaving:
        copy.wait()


def attend_back_kernel(*refs, planes, heads):
    (plane_ref, cos_ref, sin_ref, column_ref, row_ref) = refs[:5]
    arriving, w_pieces = refs[5:14], refs[14 : 14 + planes]
    rest = refs[15 + planes :]
    d_outs, w_grads = rest[:2], rest[2 : 2 + planes]
    (w_ref, gw_ref, dm_ref, dp_ref, dk_ref, dv_ref, o_ref, *came, sems) = rest[2 + planes :]
    (near_ref, far_ref, normed_ref, q_ref, k_ref, v_ref, mixed_ref, top_ref, total_ref) = came
    bf16, f32 = jnp.bfloat16, jnp.float32
    plane = plane_ref[0]
    width = near_ref.shape[1]
    blocks, part = w_ref.shape[0], w_ref.shape[3] // 4
    size = part // heads
    half = near_ref.shape[0]
    amount = 2 * half
    w_copies = plane_copies(plane, w_pieces, lambda at: w_ref.at[:, at], sems.at[0])
    copies = [
        pltpu.make_async_copy(source, ref, sems.at[2, i])
        for i, (source, ref) in enumerate(zip(arriving, came, strict=True))
    ]
    d_copies = [pltpu.make_async_copy(o_ref.at[side], d_outs[side], sems.at[3, side]) for side in range(2)]
    for copy in w_copies + copies[:2] + copies[3:] + copies[2:3]:
        copy.start()
    for copy in w_copies:
        copy.wait()

    for side, (base, ref) in enumerate(((0, near_ref), (half, far_ref))):
        copies[side].wait()

        def back_out(row, base=base, ref=ref):
            values = 0.0
            for i in range(blocks):
                weights = w_ref[i, :, :, 3 * part :].reshape(part, width // blocks)
                into = slice(i * width // blocks, (i + 1) * width // blocks)
                values = values + contract_cols(ref[pl.ds(row, ROWS), into], weights)
            dm_ref[pl.ds(base + row, ROWS), :] = values.astype(bf16).astype(f32)

        row_chunks(half, back_out)
    for copy in copies[3:]:
        copy.wait()
    sides = [(mixed_ref[:half, :].astype(bf16), near_ref), (mixed_ref[half:, :].astype(bf16), far_ref)]
    for i in range(blocks):
        into = slice(i * width // blocks, (i + 1) * width // blocks)
        grad = sum(contract_rows(mixed, ref[:, into]) for mixed, ref in sides)
        grad = grad.astype(bf16).reshape(planes, part // planes, width // blocks)
        gw_ref[i, :, :, 3 * part :] = grad

    for head in range(heads):
        mine = slice(head * size, (head + 1) * size)
        dk_ref[...] = jnp.zeros_like(dk_ref)
        dv_ref[...] = jnp.zeros_like(dv_ref)

        def attend_back(row, mine=mine, head=head):
            at = pl.ds(row, ROWS)
            query, key, value = q_ref[at, mine], k_ref[:, mine], v_ref[:, mine]
            d_mixed, total = dm_ref[at, mine], total_ref[head, at, :]
            grad_num = (d_mixed / total).astype(bf16)
            shift = jnp.sum(d_mixed * mixed_ref[at, mine], axis=1, keepdims=True) / total
            scores = contract_cols(query, key) * size**-0.5
            visible = row_ref[...] <= column_ref[at, :]
            scores = jnp.where(visible, scores, NEGATIVE)
            expo = jnp.where(visible, jnp.exp(scores - top_ref[head, at, :]), 0.0)
            d_score = (expo * (contract_cols(grad_num, value) - shift)).astype(bf16)
            d_query = dot(d_score, key) * size**-0.5
            dp_ref[at, mine] = turn_head(d_query, cos_ref[at, :], -sin_ref[at, :]).astype(bf16)
            dk_ref[...] += contract_rows(d_score, query)
            dv_ref[...] += contract_rows(expo.astype(bf16), grad_num)

        row_chunks(amount, attend_back)
        d_key = turn_head(dk_ref[...] * size**-0.5, cos_ref[...], -sin_ref[...])
        dp_ref[:, part + head * size : part + (head + 1) * size] = d_key.astype(bf16)
        dp_ref[:, 2 * part + head * size : 2 * part + (head + 1) * size] = dv_ref[...].astype(bf16)

    copies[2].wait()
    pieces = 4
    step, count = width // pieces, blocks // pieces
    for i in range(pieces):
        grad = contract_rows(normed_ref[:, i * step : (i + 1) * step], dp_ref[...]).astype(bf16)
        grad = grad.reshape(count, *gw_ref.shape[1:3], 3 * part)
        gw_ref[i * count : (i + 1) * count, :, :, : 3 * part] = grad
    w_back = [
        pltpu.make_async_copy(
            gw_ref.at[:, lax.rem(plane - k + planes, planes)], w_grads[k], sems.at[1, k]
        )
        for k in range(planes)
    ]
    for copy in w_back:
        copy.start()
    for side, base in enumerate((0, half)):

        def back_project(row, base=base, side=side):
            values = contract_cols(
                dp_ref[pl.ds(base + row, ROWS), :], w_ref[:, :, :, : 3 * part].reshape(width, 3 * part)
            )
            o_ref[side, pl.ds(row, ROWS), :] = values.astype(bf16)

        row_chunks(half, back_project)
        d_copies[side].start()
    for copy in w_back + d_copies:
        copy.wait()


def attend_call(kernel, small, blocks, arrays, outs, scratch, after, flops):
    far, near = pl.BlockSpec(memory_space=pltpu.HBM), pl.BlockSpec(memory_space=pltpu.VMEM)
    return pl.pallas_call(
        kernel,
        in_specs=[pl.BlockSpec(memory_space=pltpu.SMEM)]
        + [near] * len(blocks)
        + [far] * (len(arrays) + 1),
        out_specs=[far] * len(outs),
        out_shape=[jax.ShapeDtypeStruct(shape, kind) for shape, kind in outs],
        scratch_shapes=scratch,
        compiler_params=pltpu.CompilerParams(vmem_limit_bytes=VMEM),
        cost_estimate=pl.CostEstimate(flops=flops, bytes_accessed=30_000_000, transcendentals=0),
    )(small, *blocks, *arrays, after)


def attend(plane, rows, gain, tables, pieces, heads, after):
    bf16, f32 = jnp.bfloat16, jnp.float32
    half, width = rows[0].shape
    planes = len(pieces)
    n_ctx, depth, four = pieces[0].shape
    part = four // 4
    kept = [((2 * half, width), bf16)] + [((2 * half, part), bf16)] * 3
    kept += [((2 * half, part), f32)] + [((heads, 2 * half, 1), f32)] * 2
    return attend_call(
        functools.partial(attend_kernel, planes=planes, heads=heads),
        plane,
        [gain, *tables],
        [*rows, *pieces],
        [((half, width), bf16)] * 2 + kept,
        [pltpu.VMEM((n_ctx, planes, depth, four), bf16)]
        + [pltpu.VMEM((2, half, width), bf16)] * 2
        + [pltpu.VMEM(shape, kind) for shape, kind in kept]
        + [pltpu.SemaphoreType.DMA((4, max(planes, 7)))],
        after,
        4 * half * width * 4 * part + 16 * half * half * part,
    )


def attend_back(plane, rows, saved, tables, pieces, heads, after):
    bf16, f32 = jnp.bfloat16, jnp.float32
    half, width = rows[0].shape
    planes = len(pieces)
    n_ctx, depth, four = pieces[0].shape
    part = four // 4
    made = attend_call(
        functools.partial(attend_back_kernel, planes=planes, heads=heads),
        plane,
        tables,
        [*rows, *saved, *pieces],
        [((half, width), bf16)] * 2 + [(pieces[0].shape, bf16)] * planes,
        [
            pltpu.VMEM((n_ctx, planes, depth, four), bf16),
            pltpu.VMEM((n_ctx, planes, depth, four), bf16),
            pltpu.VMEM((2 * half, part), f32),
            pltpu.VMEM((2 * half, 3 * part), bf16),
            pltpu.VMEM((2 * half, part // heads), f32),
            pltpu.VMEM((2 * half, part // heads), f32),
            pltpu.VMEM((2, half, width), bf16),
            *(pltpu.VMEM(a.shape, a.dtype) for a in (*rows, *saved)),
            pltpu.SemaphoreType.DMA((4, max(planes, 9))),
        ],
        after,
        4 * half * width * 8 * part + 40 * half * half * part,
    )
    return made[:2], list(made[2:])


def rows_kernel(left_ref, right_ref, *refs):
    refs[-1][0] = contract_rows(left_ref[0], right_ref[0])


def shared_kernel(*refs, count):
    xs, gs = refs[:count], refs[count : 2 * count]
    hidden_ref, joined_ref, _, into_ref, down_ref, x_ref, g_ref, sum_ref, sems = refs[2 * count :]
    size = GROUP * BLOCK
    places = []
    for x, g in zip(xs, gs, strict=True):
        for at, (_, starts) in enumerate(spans_of(g, g, BLOCK + EXTRA)[: x.shape[0] // size]):
            places.append((x, at * size, g, starts))

    def copies(i):
        x, at, g, starts = places[i]
        slot = i % 2
        made = [pltpu.make_async_copy(x.at[pl.ds(at, size)], x_ref.at[slot], sems.at[slot, 0])]
        for n, start in enumerate(starts):
            source, target = g.at[pl.ds(start, BLOCK)], g_ref.at[slot, pl.ds(n * BLOCK, BLOCK)]
            made.append(pltpu.make_async_copy(source, target, sems.at[slot, 1 + n]))
        return made

    for copy in copies(0):
        copy.start()
    for i in range(len(places)):
        if i + 1 < len(places):
            for copy in copies(i + 1):
                copy.start()
        for copy in copies(i):
            copy.wait()
        at = slice(i * size, (i + 1) * size)
        into = contract_rows(joined_ref[at, :], x_ref[i % 2])
        down = contract_rows(hidden_ref[at, :], g_ref[i % 2])
        sum_ref[...] = into if i == 0 else sum_ref[...] + into
        down_ref[...] = down if i == 0 else down_ref[...] + down
    for at in range(0, into_ref.shape[0], size):
        into_ref[at : at + size, :] = sum_ref[:, at : at + size].T.astype(into_ref.dtype)


def held_whole(*shape):
    return pl.BlockSpec(shape, lambda j: (0,) * len(shape), pipeline_mode=pl.Buffered(1))


def expert_call(
    kernel, owners, operands, specs, outs, out_specs, kept, after, scratch, flops, moved
):
    return pl.pallas_call(
        functools.partial(kernel, carried=len(kept) + 1),
        grid=(owners,),
        in_specs=specs + [pl.BlockSpec(memory_space=pl.ANY)] * (len(kept) + 1),
        out_specs=out_specs,
        out_shape=[jax.ShapeDtypeStruct(shape, kind) for shape, kind in outs],
        scratch_shapes=scratch,
        input_output_aliases={len(operands) + i: i for i in range(len(kept))},
        compiler_params=pltpu.CompilerParams(vmem_limit_bytes=VMEM),
        cost_estimate=pl.CostEstimate(flops=flops, bytes_accessed=moved, transcendentals=0),
    )(*operands, *kept, after)


def growing(k, rows, columns):
    return pl.BlockSpec((1, rows, columns), lambda j: (j, k, 0))


def weight_buffers(array):
    depth = min(2, array.shape[0])
    return [pltpu.VMEM((depth,) + array.shape[1:], array.dtype), pltpu.SemaphoreType.DMA((depth,))]


def early(k, planes, first, grads, count, w_down, s_down, kept, after):
    bf16, f32 = jnp.bfloat16, jnp.float32
    owners, units, width = w_down.shape
    half = grads[0].shape[0] * BLOCK // (BLOCK + EXTRA)
    rows, lane = 2 * half // BLOCK * CAP, s_down.shape[0]
    outs = [
        ((owners, planes * rows, width), bf16),
        ((owners, planes * rows, units), f32),
        ((2 * half // BLOCK, planes, count, BLOCK), bf16),
        ((2 * half, lane), f32),
        ((EXPERTS, 2 * half), f32),
        ((owners, 2 * half), f32),
    ]
    made = expert_call(
        early_kernel,
        owners,
        [first, *grads, w_down, s_down],
        [pl.BlockSpec(memory_space=pltpu.SMEM)]
        + [held_whole(*grads[0].shape)] * 2
        + [pl.BlockSpec(memory_space=pltpu.HBM), held_whole(*s_down.shape)],
        outs,
        [growing(k, rows, width), growing(k, rows, units), pl.BlockSpec(memory_space=pltpu.HBM)]
        + [held_whole(*shape) for shape, _ in outs[3:]],
        kept,
        after,
        [
            pltpu.VMEM((owners, rows, width), bf16),
            pltpu.VMEM((2 * half // BLOCK, count, BLOCK), bf16),
            *weight_buffers(w_down),
            pltpu.SemaphoreType.DMA(()),
        ],
        2 * owners * rows * width * (units + GROUP * BLOCK) + 4 * half * width * lane,
        2 * owners * width * (units + 2 * rows) + 4 * half * width,
    )
    return list(made[:3]), made[3:]


def middle(
    k, planes, first, rows_x, router_t, mask, slots, w_in, s_in, dh, dhs, kept, after
):
    bf16, f32 = jnp.bfloat16, jnp.float32
    owners, width, joined = w_in.shape
    half = rows_x[0].shape[0]
    rows, lane = 2 * half // BLOCK * CAP, dhs.shape[1]
    outs = [
        ((owners, planes * rows, width), bf16),
        ((owners, planes * rows, joined // 2), bf16),
        ((owners, planes * rows, joined), bf16),
        ((half // BLOCK * (BLOCK + EXTRA), width), bf16),
        ((half // BLOCK * (BLOCK + EXTRA), width), bf16),
        ((EXPERTS, 2 * half), f32),
        ((owners, 2 * half), f32),
        ((2 * half, lane), bf16),
        ((2 * half, 2 * lane), bf16),
    ]
    made = expert_call(
        middle_kernel,
        owners,
        [first, *rows_x, router_t, mask, slots, w_in, s_in, dh, dhs],
        [pl.BlockSpec(memory_space=pltpu.SMEM)]
        + [held_whole(half, width)] * 2
        + [held_whole(*a.shape) for a in (router_t, mask, slots)]
        + [pl.BlockSpec(memory_space=pltpu.HBM), held_whole(*s_in.shape), growing(k, rows, joined // 2)]
        + [held_whole(*dhs.shape)],
        outs,
        [growing(k, rows, width), growing(k, rows, joined // 2), growing(k, rows, joined)]
        + [held_whole(*shape) for shape, _ in outs[3:]],
        kept,
        after,
        [
            pltpu.VMEM((owners, rows, width), bf16),
            pltpu.VMEM((owners, rows, width), bf16),
            pltpu.VMEM((owners, rows, 1), f32),
            *weight_buffers(w_in),
        ],
        4 * owners * rows * width * (joined + GROUP * BLOCK) + 16 * half * width * lane,
        2 * owners * width * (joined + 2 * rows) + 8 * half * width,
    )
    return list(made[:3]), made[3:5], made[5:]


def late(k, planes, first, hidden, taken, slots, gates, shared, w_down, s_down, kept, after):
    bf16, f32 = jnp.bfloat16, jnp.float32
    owners, units, width = w_down.shape
    half = shared.shape[0] // 2
    rows = 2 * half // BLOCK * CAP
    outs = [
        ((owners, hidden.shape[1], width), bf16),
        ((half, width), bf16),
        ((half, width), bf16),
    ]
    made = expert_call(
        late_kernel,
        owners,
        [first, hidden, taken, slots, gates, shared, w_down, s_down],
        [pl.BlockSpec(memory_space=pltpu.SMEM), growing(k, rows, units), growing(k, rows, width)]
        + [held_whole(*a.shape) for a in (slots, gates, shared)]
        + [
            pl.BlockSpec((1, units, width), lambda j: (j, 0, 0)),
            held_whole(*s_down.shape),
        ],
        outs,
        [growing(k, rows, width)] + [held_whole(*shape) for shape, _ in outs[1:]],
        kept,
        after,
        [pltpu.VMEM((owners, rows, width), bf16)],
        2 * owners * rows * width * (units + GROUP * BLOCK) + 4 * half * width * s_down.shape[0],
        2 * owners * width * (units + 2 * rows) + 4 * half * width,
    )
    return list(made[:1]), made[1:]


def rows_grad(left, right, owner, count, kept, after):
    owners, amount, wide = left.shape
    narrow = right.shape[2]
    depth = pl.Buffered(2 if count > 1 else 1)
    at = lambda j: (owner + j, 0, 0)
    return pl.pallas_call(
        rows_kernel,
        grid=(count,),
        in_specs=[
            pl.BlockSpec((1, amount, wide), at, pipeline_mode=depth),
            pl.BlockSpec((1, amount, narrow), at, pipeline_mode=depth),
        ]
        + [pl.BlockSpec(memory_space=pl.ANY)] * (len(kept) + 1),
        out_specs=pl.BlockSpec((1, wide, narrow), at, pipeline_mode=depth),
        out_shape=jax.ShapeDtypeStruct((owners, wide, narrow), jnp.float32),
        input_output_aliases={2: 0} if kept else {},
        compiler_params=pltpu.CompilerParams(vmem_limit_bytes=VMEM),
        cost_estimate=pl.CostEstimate(
            flops=2 * count * amount * wide * narrow,
            bytes_accessed=4 * count * wide * narrow,
            transcendentals=0,
        ),
    )(left, right, *kept, after)


def rows_of_columns_kernel(came_ref, weights_ref, rows_ref, sum_ref):
    blocks, _, three = came_ref.shape
    part, width = three // 3, rows_ref.shape[1] // 3
    total = 0.0
    for block in range(blocks):
        for i in range(3):
            into = slice(i * width + block * part, i * width + (block + 1) * part)
            values = came_ref[block, :, i * part : (i + 1) * part].astype(jnp.float32)
            rows_ref[:, into] = values
            weighted = values * weights_ref[:, into].astype(jnp.float32)
            total = total + jnp.sum(weighted, axis=1, keepdims=True)
    sum_ref[...] = total


def rows_of_columns(came, weights):
    return pl.pallas_call(
        rows_of_columns_kernel,
        out_shape=[
            jax.ShapeDtypeStruct(weights.shape, jnp.float32),
            jax.ShapeDtypeStruct((weights.shape[0], 1), jnp.float32),
        ],
        compiler_params=pltpu.CompilerParams(vmem_limit_bytes=VMEM),
    )(came, weights)


def shared_grads(rows_x, rows_g, hidden, joined, after):
    count, width = len(rows_x), rows_x[0].shape[1]
    bf16, f32 = jnp.bfloat16, jnp.float32
    far, near = pl.BlockSpec(memory_space=pltpu.HBM), pl.BlockSpec(memory_space=pltpu.VMEM)
    wide, size = joined.shape[1], GROUP * BLOCK
    return pl.pallas_call(
        functools.partial(shared_kernel, count=count),
        in_specs=[far] * (2 * count) + [near] * 2 + [far],
        out_specs=[near] * 2,
        out_shape=[
            jax.ShapeDtypeStruct((width, wide), bf16),
            jax.ShapeDtypeStruct((hidden.shape[1], width), f32),
        ],
        scratch_shapes=[
            pltpu.VMEM((2, size, width), bf16),
            pltpu.VMEM((2, size, width), bf16),
            pltpu.VMEM((wide, width), f32),
            pltpu.SemaphoreType.DMA((2, 1 + GROUP)),
        ],
        compiler_params=pltpu.CompilerParams(vmem_limit_bytes=VMEM),
        cost_estimate=pl.CostEstimate(
            flops=2 * hidden.shape[0] * width * (wide + hidden.shape[1]),
            bytes_accessed=4 * hidden.shape[0] * width,
            transcendentals=0,
        ),
    )(*rows_x, *rows_g, hidden, joined, after)


def local(
    tokens,
    gain_attn,
    w_qkv,
    w_out,
    gain_ffn,
    w_router,
    w_shared_in,
    w_shared_down,
    w_expert_in,
    w_expert_down,
    routes,
    plan,
    cotangent,
):
    n_ctx, planes = lax.axis_size("ctx"), lax.axis_size("fsdp")
    devices = n_ctx * planes
    ctx, plane = lax.axis_index("ctx"), lax.axis_index("fsdp")
    device = ctx * planes + plane
    amount, width = tokens.shape[1:]
    head_size = width // HEADS
    heads = HEADS // n_ctx
    part = heads * head_size
    rows = width // devices
    per_owner = w_expert_in.shape[0]
    units = w_shared_down.shape[0]
    bf16, f32 = jnp.bfloat16, jnp.float32
    order = jnp.array(plane_order(), jnp.int32)
    places = order ^ ctx

    clock = Clock()

    expert_ids = jnp.arange(EXPERTS, dtype=jnp.int32)
    own_mask = jnp.sum((expert_ids[:, None, None] == routes[0].T[None]).astype(f32), axis=1)
    before = (jnp.arange(amount)[:, None] < jnp.arange(amount)[None, :]).astype(bf16)
    ranking = jnp.where(own_mask > 0, dot(own_mask.astype(bf16), before), -1.0)

    qkv_part = w_qkv.reshape(rows, 3, n_ctx, part).transpose(2, 0, 1, 3).reshape(n_ctx, rows, 3 * part)
    qkv_part = lax.all_to_all(qkv_part, "ctx", split_axis=0, concat_axis=0, tiled=True)
    sequence = Transfer(gather_plane(tokens[0], False))
    small = jnp.concatenate([ranking.astype(bf16), jnp.pad(w_router, ((0, 0), (0, amount - EXPERTS)))])
    small = small.reshape(-1, EXTRA, amount).transpose(1, 0, 2).reshape(EXTRA, -1)
    small = jnp.pad(small, ((0, 0), (0, width - small.shape[1])))
    own_grads = jnp.concatenate([cotangent[0], small], axis=0)
    grads = [Transfer(gather_plane(own_grads, False))]
    grad_blocks = [Transfer(turned(own_grads, k)) for k in range(1, min(3, planes))]
    (qkv_part,) = stage(clock, [sequence, *grads, *grad_blocks], [qkv_part])

    out_part = w_out.reshape(rows, n_ctx, part).transpose(1, 0, 2)
    ring_w = Transfer(ring(jnp.concatenate([qkv_part, out_part], axis=2)))
    gains = jnp.concatenate([gain_attn, gain_ffn])
    gains = Transfer(exchanged(clock.now(jnp.broadcast_to(gains[None], (devices, 2 * rows)))))
    shared_in = w_shared_in.reshape(rows, 2, devices, units).transpose(2, 0, 1, 3)
    shared_in = shared_in.reshape(devices, rows, 2 * units)

    half_block = amount // 2
    half_ids = (places[:, None] * 2 + jnp.arange(2, dtype=jnp.int32)[None, :]).reshape(-1)
    placed = jnp.sum(
        jnp.where(half_ids[:, None] == jnp.arange(plan.shape[0])[None, :], plan[None, :], 0), axis=1
    )
    pos = (placed[:, None] * half_block + jnp.arange(half_block)[None, :]).reshape(-1).astype(f32)
    frequency = ROPE_BASE ** (-2.0 * jnp.arange(head_size // 2, dtype=f32) / head_size)
    angles = pos[:, None] * frequency[None, :]
    cosine, sine = jnp.cos(angles), jnp.sin(angles)
    tables = [
        jnp.concatenate([cosine, cosine], axis=1),
        jnp.concatenate([-sine, sine], axis=1),
        pos[:, None],
        pos[None, :],
    ]
    shared_in, *tables = stage(clock, [ring_w, gains, sequence, *grads], [shared_in, *tables])
    if planes > 1:
        grads.append(Transfer(gather_plane(grad_blocks[0].result, False)))
    stage(clock, [ring_w, gains, sequence, *grads])
    gain_one, gain_two = (
        gains.result[:, at : at + rows].reshape(width).astype(f32) for at in (0, rows)
    )
    seq_rows = finish(clock, sequence)[0]

    first_expert = lax.rem(device * per_owner, EXPERTS)
    first = [first_expert, device * per_owner // EXPERTS, ctx]
    back = lax.rem(plane - jnp.arange(planes, dtype=jnp.int32) + planes, planes)
    first = [jnp.stack([*first, back[k]]).astype(jnp.int32) for k in range(planes)]
    ranks, slots = [], []

    lane = -(-units // BLOCK) * BLOCK
    s_down = jnp.pad(w_shared_down, ((0, lane - units), (0, 0)))
    early_kept, dhs = [], []

    def grads_stage(transfers, beside=(), work=True):
        nonlocal early_kept
        k, made = len(dhs), []
        if work and k < planes and k < len(grads) and grads[k].done:
            early_kept, made = early(
                k, planes, first[k], grads[k].result, rows, w_expert_down, s_down, early_kept, clock.token
            )
            for some, one in zip((ranks, slots), made[1:], strict=True):
                some.append(one)
        arrays = stage(clock, [*transfers, *grads, *grad_blocks], [*beside, *made[:1]])
        dhs.extend(arrays[len(beside) :])
        k = len(grads)
        if 2 <= k < planes and grad_blocks[k - 1].done and grads[-1].step is not grads[-1].opening:
            grads.append(Transfer(gather_plane(grad_blocks[k - 1].result, False)))
            grads[-1].opening = grads[-1].step
            if len(grad_blocks) < planes - 1:
                ahead = len(grad_blocks) + 1
                source = own_grads if ahead == 3 else grad_blocks[-1].result
                grad_blocks.append(Transfer(turned(source, ahead if ahead == 3 else 1)))
        return arrays[: len(beside)]

    grads[-1].opening = None
    while not ring_w.done:
        shared_in, own_grads = grads_stage([ring_w], [shared_in, own_grads])
    pieces = ring_w.result
    shared_in = Transfer(exchanged(shared_in))
    own_rows = tokens[0].astype(f32)
    plane_id = plane.reshape(1).astype(jnp.int32)
    *attended, normed, query, key, value, mixed, tops, totals = attend(
        plane_id, seq_rows, gain_one[None, :], tables, pieces, heads, clock.token
    )
    saved = [normed, query, key, value, mixed, tops, totals]
    attended = grads_stage([shared_in], attended)
    attended = Transfer(scatter_plane(*attended))
    shared_in = shared_in.result.reshape(width, 2, units)
    s_in = jnp.pad(shared_in, ((0, 0), (0, 0), (0, lane - units))).reshape(width, 2 * lane)
    (s_in,) = grads_stage([attended], [s_in])
    while not attended.done:
        grads_stage([attended])
    residual = own_rows + attended.result.astype(f32)
    ffn_own = rms_scale(residual, gain_two).astype(bf16)

    ffn, d_parts = [Transfer(gather_plane(ffn_own))], []
    block, d_sum = Transfer(turned(ffn_own)), None
    mid_kept, mids, late_kept, out_parts, out_sum, router_t = [], [], [], [], None, None

    def do_late():
        nonlocal late_kept
        if len(out_parts) == planes:
            return []
        k = (len(out_parts) + 1) % planes
        late_kept, pair = late(
            k, planes, first[k], mid_kept[1], early_kept[0], slots[k], mids[k][0], mids[k][2],
            w_expert_down, s_down, late_kept, clock.token,
        )
        return list(pair)

    def outs_stage(transfers, beside=(), moving=None, adding=True, opening=True):
        nonlocal out_sum
        pair = do_late() if not beside else []
        if out_sum is None and len(out_parts) == planes and out_parts[0].done:
            out_sum = Transfer(staged_sum(out_parts))
        going = [t for t in out_parts if not t.done]
        fresh = [t for t in going if t.step is t.opening]
        going = [t for t in going if t not in fresh]
        fresh = fresh if opening else []
        if moving is not None:
            going = going[:moving]
        sums = [out_sum] if out_sum and adding else []
        arrays = stage(clock, [*transfers, *going, *fresh, *sums], [*beside, *pair])
        if pair:
            out_parts.append(Transfer(scatter_plane(*arrays)))
            out_parts[-1].opening = out_parts[-1].step
            arrays = []
        return arrays

    while d_sum is None or not d_sum.done:
        going = [*ffn, *d_parts, block, *([d_sum] if d_sum else [])]
        k = len(mids)
        if router_t is None and len(ranks) == planes:
            router_full = early_kept[2].reshape(width, amount)[:, :EXPERTS]
            router_t = router_full.T
        if k < planes and ffn[k].done and len(dhs) > k and router_t is not None:
            mid_kept, pair, made = middle(
                k, planes, first[k], ffn[k].result, router_t, ranks[k], slots[k], w_expert_in, s_in,
                early_kept[1], dhs[k], mid_kept, clock.token,
            )
            mids.append(made)
            pair = grads_stage(going, list(pair), work=False)
            d_parts.append(Transfer(scatter_plane(*pair)))
        elif k == planes:
            outs_stage(going, moving=1 if d_parts[-1].done else 0)
        else:
            grads_stage(going)
        if len(ffn) < planes and block.done:
            ffn.append(Transfer(gather_plane(block.result)))
            if len(ffn) < planes:
                block = Transfer(turned(block.result))
        if d_sum is None and len(d_parts) == planes and d_parts[min(1, planes - 1)].done:
            d_sum = Transfer(staged_sum(d_parts[1:] + d_parts[:1]))
    rows_in, hidden, d_joined = mid_kept
    gates = mids[0][0]

    dgate = d_sum.result[amount:].astype(f32).reshape(4, EXPERTS, amount)
    dgate = jnp.sum(dgate, axis=0)
    gates_own = gates[:, :amount]
    dlogits = gates_own * (dgate - jnp.sum(gates_own * dgate, axis=0, keepdims=True))
    dlogits_b = dlogits.astype(bf16).T
    d_ffn = d_sum.result[:amount].astype(f32) + contract_cols(dlogits_b, router_full)
    second_back = jax.vjp(rms_scale, residual, gain_two)[1](d_ffn)
    d_residual = cotangent[0].astype(f32) + second_back[0]

    d_attn = Transfer(gather_plane(d_residual.astype(bf16)))
    outs_stage([d_attn], moving=0)
    while len(out_parts) < planes:
        outs_stage([], moving=1)
    shared = None
    while not d_attn.done or shared is None:
        if shared is not None:
            outs_stage([d_attn], moving=1)
            continue
        into, shared_down_grad = shared_grads(
            [side for t in ffn for side in t.result],
            [side for t in grads for side in t.result],
            jnp.concatenate([made[2] for made in mids]),
            jnp.concatenate([made[3] for made in mids]),
            clock.token,
        )
        small = contract_rows(ffn_own, clock.now(dlogits_b)).astype(bf16)
        gain = second_back[1][:, None].astype(bf16)
        shared = jnp.concatenate([into[:, :units], into[:, lane : lane + units], small, gain], axis=1)
        shared = jnp.pad(shared, ((0, 0), (0, -shared.shape[1] % BLOCK)))
        shared = shared.reshape(devices, rows, -1)
        shared, shared_down_grad = outs_stage(
            [d_attn], [shared, shared_down_grad], moving=1, opening=False
        )
    shared = Transfer(exchanged(shared))

    d_normed, ring_grad = attend_back(
        plane_id, d_attn.result, saved, tables, pieces, heads, clock.token
    )
    d_normed = outs_stage([shared], list(d_normed), moving=1)
    ring_grad = Transfer(ring_sum([piece.reshape(-1, 4 * part) for piece in ring_grad]))
    d_normed = Transfer(scatter_plane(*d_normed))

    first_half = -(-per_owner // 2)
    (dy,) = late_kept
    work = [lambda kept: rows_grad(rows_in, d_joined, 0, first_half, kept, clock.token)]
    if first_half < per_owner:
        work.append(
            lambda kept: rows_grad(
                rows_in, d_joined, first_half, per_owner - first_half, kept, clock.token
            )
        )
    work.append(lambda kept: rows_grad(hidden, dy, 0, per_owner, [], clock.token))
    made = []
    while work or not (ring_grad.done and d_normed.done):
        if work:
            one = work.pop(0)(made)
            (one,) = outs_stage([ring_grad, d_normed], [one], 1, False)
            if work:
                made = [one]
            else:
                (expert_in_grad,), expert_down_grad = made, one
        else:
            outs_stage([ring_grad, d_normed], [], 1, False)
    ring_grad = ring_grad.result.reshape(n_ctx, rows, 4 * part)
    qkv_grad = lax.all_to_all(ring_grad[:, :, : 3 * part], "ctx", split_axis=0, concat_axis=0, tiled=True)
    out_grad = ring_grad[:, :, 3 * part :].transpose(1, 0, 2).reshape(rows, width).astype(f32)
    first_back = jax.vjp(lambda x: rms_scale(x, gain_one), own_rows)[1](d_normed.result.astype(f32))
    tokens_grad = d_residual + first_back[0]
    shared = clock.now(shared.result)
    shared_in_grad = shared[:, :, : 2 * units].reshape(devices, rows, 2, units)
    shared_in_grad = shared_in_grad.transpose(1, 2, 0, 3).reshape(rows, 2 * devices * units).astype(f32)
    small = jnp.sum(shared[:, :, 2 * units :].astype(f32), axis=0)
    router_grad, gain_ffn_grad = small[:, :EXPERTS], small[:, EXPERTS]
    shared_down_grad = shared_down_grad[:units]
    while out_sum is None or not out_sum.done:
        if out_sum is None and out_parts[0].done:
            out_sum = Transfer(staged_sum(out_parts))
        stage(clock, [*out_parts, *([out_sum] if out_sum else [])])
    result = (residual + out_sum.result.astype(f32)).astype(bf16)
    qkv_grad, weighted = rows_of_columns(qkv_grad, w_qkv)
    gain_attn_grad = weighted[:, 0] / gain_attn.astype(f32)
    return (
        result[None],
        tokens_grad[None],
        gain_attn_grad,
        qkv_grad,
        out_grad,
        gain_ffn_grad,
        router_grad,
        shared_in_grad,
        shared_down_grad,
        expert_in_grad,
        expert_down_grad,
    )


def solution(mesh):
    split = P(BOTH)
    matrix = P(BOTH, None)
    cube = P(BOTH, None, None)
    batch = P("fsdp", "ctx", None)
    return jax.shard_map(
        local,
        mesh=mesh,
        in_specs=(
            batch,
            split,
            matrix,
            matrix,
            split,
            matrix,
            matrix,
            matrix,
            cube,
            cube,
            batch,
            P(),
            batch,
        ),
        out_specs=(
            batch,
            batch,
            split,
            matrix,
            matrix,
            split,
            matrix,
            matrix,
            matrix,
            cube,
            cube,
        ),
        check_vma=False,
    )
```

```python
import functools

import jax
import jax.numpy as jnp
from jax import lax
from jax.experimental import pallas as pl
from jax.experimental.pallas import tpu as pltpu
from jax.sharding import PartitionSpec as P

HEADS = 16
EXPERTS = 64
CAP = 20
BLOCK = 128
EXTRA = 16
GROUP = 4
VMEM = 64 * 1024 * 1024

EPSILON = 1e-06
ROPE_BASE = 10000.0
NEGATIVE = -1e30
BOTH = ("ctx", "fsdp")


def rms_scale(values, gain):
    inverse = lax.rsqrt(jnp.mean(values * values, axis=-1, keepdims=True) + EPSILON)
    return values * inverse * gain


def dot(left, right):
    return jnp.dot(left, right, preferred_element_type=jnp.float32)


def contract_rows(left, right):
    return lax.dot_general(
        left, right, (((0,), (0,)), ((), ())), preferred_element_type=jnp.float32
    )


def contract_cols(left, right):
    return lax.dot_general(
        left, right, (((1,), (1,)), ((), ())), preferred_element_type=jnp.float32
    )


def plane_order():
    count = lax.axis_size("ctx")
    return list(range(0, count, 2)) + list(range(1, count, 2))


def ctx_bits():
    count = lax.axis_size("ctx")
    return [1 << i for i in range(1, count.bit_length() - 1)]


def swap(values, bit):
    count = lax.axis_size("ctx")
    return lax.ppermute(values, "ctx", [(i, i ^ bit) for i in range(count)])


def turn(values, step=1):
    count = lax.axis_size("fsdp")
    return lax.ppermute(values, "fsdp", [(i, (i + step) % count) for i in range(count)])


def add(left, right):
    return (left.astype(jnp.float32) + right.astype(jnp.float32)).astype(left.dtype)


class Step:
    def __init__(self, sent, outs=(), beside=()):
        self.sent, self.outs, self.beside = list(sent), list(outs), list(beside)


class Transfer:
    def __init__(self, steps):
        self.steps, self.step, self.done, self.result = steps, None, False, None
        self.advance(None)

    def advance(self, arrived):
        try:
            self.step = self.steps.send(arrived)
        except StopIteration as stop:
            self.step, self.done, self.result = None, True, stop.value


class Clock:
    def __init__(self):
        self.token = jnp.zeros((8, 128), jnp.float32)

    def now(self, values):
        return values + self.token[0, 0].astype(values.dtype)


CHUNK = 16


def add_rows(target, at, sources, rows):
    @pl.loop(0, rows // CHUNK)
    def _(i):
        row = pl.multiple_of(i * CHUNK, CHUNK)
        total = sum(ref[pl.ds(row, CHUNK), :].astype(jnp.float32) for ref in sources)
        target[pl.ds(at + row, CHUNK), :] = total.astype(target.dtype)


def make_outs(inputs, outs, plans, scratch):
    held, terms, (in_sems, out_sems) = scratch[: len(outs)], scratch[len(outs) : -2], scratch[-2:]
    parts, copies, used = [], 0, 0
    for buffer, out, plan in zip(held, outs, plans, strict=True):
        at = 0
        for rows, sources in plan:
            place = buffer.at[pl.ds(at, rows)]
            into = [place] if len(sources) == 1 else list(terms[used : used + len(sources)])
            used += 0 if len(sources) == 1 else len(sources)
            arriving = []
            for (i, start), target in zip(sources, into, strict=True):
                source = inputs[i].at[pl.ds(start, rows)]
                arriving.append(pltpu.make_async_copy(source, target, in_sems.at[copies]))
                arriving[-1].start()
                copies += 1
            leaving = pltpu.make_async_copy(place, out.at[pl.ds(at, rows)], out_sems.at[len(parts)])
            parts.append((arriving, buffer, at, into, rows, leaving))
            at += rows
    for arriving, buffer, at, into, rows, leaving in parts:
        for copy in arriving:
            copy.wait()
        if len(arriving) > 1:
            add_rows(buffer, at, into, rows)
        leaving.start()
    for *_, leaving in parts:
        leaving.wait()


def stage(clock, transfers, beside=()):
    active = [t for t in transfers if not t.done]
    making = [t for t in active if t.step.outs]
    waited = [a for t in active if not t.step.outs for a in t.step.sent]
    passed = [clock.token, *beside]
    taken, plans, kinds = [], [], []
    for t in making:
        base = len(taken)
        taken += t.step.sent + t.step.beside
        for plan in t.step.outs:
            plans.append([(rows, [(base + i, start) for i, start in terms]) for rows, terms in plan])
            like = t.step.sent[0]
            kinds.append((sum(rows for rows, _ in plan), like.shape[1], like.dtype))
    scratch = [pltpu.VMEM((rows, width), kind) for rows, width, kind in kinds]
    count = 0
    for (_, width, kind), plan in zip(kinds, plans, strict=True):
        for rows, terms in plan:
            count += len(terms)
            if len(terms) > 1:
                scratch += [pltpu.VMEM((rows, width), kind)] * len(terms)
    if making:
        scratch += [pltpu.SemaphoreType.DMA((count,)), pltpu.SemaphoreType.DMA((sum(map(len, plans)),))]
    first = len(passed) + len(waited)

    def kernel(*refs):
        outs = first + len(taken) + len(passed)
        if making:
            make_outs(
                refs[first : first + len(taken)],
                refs[outs : outs + len(kinds)],
                plans,
                refs[outs + len(kinds) :],
            )

    far = pl.BlockSpec(memory_space=pl.ANY)
    arrays = pl.pallas_call(
        kernel,
        in_specs=[far] * (first + len(taken)),
        out_specs=[far] * (len(passed) + len(kinds)),
        out_shape=[jax.ShapeDtypeStruct(a.shape, a.dtype) for a in passed]
        + [jax.ShapeDtypeStruct((rows, width), kind) for rows, width, kind in kinds],
        scratch_shapes=scratch,
        input_output_aliases={i: i for i in range(len(passed))},
        compiler_params=pltpu.CompilerParams(vmem_limit_bytes=VMEM),
    )(*passed, *waited, *taken)
    clock.token, given, arrays = arrays[0], arrays[1 : len(passed)], arrays[len(passed) :]
    results = {}
    for t in making:
        results[id(t)], arrays = arrays[: len(t.step.outs)], arrays[len(t.step.outs) :]
    for t in active:
        t.advance(results[id(t)] if id(t) in results else t.step.sent)
    return given


def finish(clock, *transfers):
    while not all(t.done for t in transfers):
        stage(clock, transfers)
    return [t.result for t in transfers]


def turned(block, step=1):
    (block,) = yield Step([turn(block, step)])
    return block


def ring(block):
    held = [block]
    for _ in range(lax.axis_size("fsdp") - 1):
        (block,) = yield Step([turn(block)])
        held.append(block)
    return held


def ring_sum(pieces):
    total = pieces[1]
    for piece in pieces[2:]:
        rows = total.shape[0]
        (total,) = yield Step([turn(total)], [[(rows, [(0, 0), (1, 0)])]], [piece])
    (total,) = yield Step([turn(total)])
    return pieces[0], total


def staged_sum(parts):
    total = parts[0].result
    for part in parts[1:]:
        (total,) = yield Step([turn(total)])
        while not part.done:
            (total,) = yield Step([total])
        total = add(part.result, total)
    return total


def to_all(values):
    return lax.all_to_all(values, BOTH, split_axis=0, concat_axis=0, tiled=True)


def exchanged(values):
    (values,) = yield Step([to_all(values)])
    return values


def gather_plane(block, direct=True):
    bits = ctx_bits()
    amount = block.shape[0]
    half = -(-amount // 2 // CHUNK) * CHUNK
    rest = amount - half
    if len(bits) == 2 and direct:
        others = [swap(block, place) for place in (bits[0], bits[1], bits[0] | bits[1])]
        (near,) = yield Step(others, [[(amount, [(i, 0)]) for i in (3, 0, 1, 2)]], [block])
    elif len(bits) == 2:
        x_bit, y_bit = bits
        over = [swap(block, x_bit), swap(block, y_bit)]
        first, second = yield Step(over, [[(half, [(0, 0)])], [(rest, [(1, half)])]])
        corner = [swap(first, y_bit), swap(second, x_bit)]
        parts = [(amount, [(i, 0)]) for i in (2, 3, 4)] + [(half, [(0, 0)]), (rest, [(1, 0)])]
        (near,) = yield Step(corner, [parts], [block, *over])
    else:
        near = block
        for bit in bits:
            rows = near.shape[0]
            (near,) = yield Step([swap(near, bit)], [[(rows, [(1, 0)]), (rows, [(0, 0)])]], [near])
    (far,) = yield Step([swap(near, 1)])
    return near, far


def scatter_plane(near, far):
    bits = ctx_bits()
    size = near.shape[0] >> len(bits)
    if len(bits) == 2:
        parts = [[(size, [(0, i * size), (1, i * size)])] for i in range(4)]
        own, part_x, part_y, corner = yield Step([swap(far, 1)], parts, [near])
        back = [swap(part_x, bits[0]), swap(part_y, bits[1]), swap(corner, bits[0] | bits[1])]
        (total,) = yield Step(back, [[(size, [(i, 0) for i in range(4)])]], [own])
        return total
    rows = near.shape[0]
    (held,) = yield Step([swap(far, 1)], [[(rows, [(0, 0), (1, 0)])]], [near])
    for bit in reversed(bits):
        rows //= 2
        (held,) = yield Step([swap(held[rows:], bit)], [[(rows, [(0, 0), (1, 0)])]], [held])
    return held


def gate_parts(first, second):
    sigmoid = 1.0 / (1.0 + jnp.exp(-first))
    return sigmoid, first * sigmoid * second


def gate_back(first, second, sigmoid, upstream):
    silu = first * sigmoid
    return upstream * second * (sigmoid + silu * (1.0 - sigmoid)), upstream * silu


def pick(slot_ref, owner, span):
    tokens = GROUP * BLOCK
    slots = slot_ref[pl.ds(owner, 1), span * tokens : (span + 1) * tokens]
    ids = lax.broadcasted_iota(jnp.int32, (GROUP * CAP, tokens), 0).astype(jnp.float32)
    return ids == slots


def pick_all(slot_ref, span):
    chosen = [pick(slot_ref, owner, span).astype(jnp.bfloat16) for owner in range(slot_ref.shape[0])]
    return jnp.concatenate(chosen, axis=0)


def spans_of(first_ref, second_ref, stride=BLOCK):
    per_side = first_ref.shape[0] // (GROUP * stride)
    return [
        (ref, [(n * GROUP + i) * stride for i in range(GROUP)])
        for ref in (first_ref, second_ref)
        for n in range(per_side)
    ]


def read_span(ref, starts):
    if starts[1] == starts[0] + BLOCK:
        return ref[starts[0] : starts[0] + GROUP * BLOCK, :]
    return jnp.concatenate([ref[at : at + BLOCK, :] for at in starts], axis=0)


def write_span(ref, starts, values):
    for i, at in enumerate(starts):
        ref[at : at + BLOCK, :] = values[i * BLOCK : (i + 1) * BLOCK].astype(ref.dtype)


def slots_at(span):
    return slice(span * GROUP * CAP, (span + 1) * GROUP * CAP)


def tokens_at(span):
    return slice(span * GROUP * BLOCK, (span + 1) * GROUP * BLOCK)


def streamed(source, buffers, sems, step, count):
    def copy(owner):
        return pltpu.make_async_copy(source.at[owner], buffers.at[owner % 2], sems.at[owner % 2])

    @pl.when(step == 0)
    def _():
        copy(0).start()

    @pl.when(step + 1 < count)
    def _():
        copy(step + 1).start()

    def arrived():
        copy(step).wait()
        return buffers[step % 2]

    return arrived


def early_kernel(*refs, carried):
    first_ref, ga_ref, gb_ref, down_ref, s_down_ref = refs[:5]
    (rows_ref, dh_ref, router_out, dhs_ref, ranks_ref, slot_ref, kept_ref, router_ref, w_ref, w_sems, sem) = refs[
        5 + carried :
    ]
    owners = slot_ref.shape[0]
    step = pl.program_id(0)
    weights = streamed(down_ref, w_ref, w_sems, step, owners)

    @pl.when(step == 0)
    def _():
        places = spans_of(ga_ref, gb_ref, BLOCK + EXTRA)
        blocks, count = router_ref.shape[:2]
        for block, (ref, at) in enumerate((ref, at) for ref, starts in places for at in starts):
            place = 2 * block if 2 * block < blocks else 2 * block - blocks + 1
            came = ref[at + BLOCK : at + BLOCK + EXTRA, :]
            lanes = slice(block * BLOCK, (block + 1) * BLOCK)
            for i in range((EXPERTS + count) // EXTRA):
                tile, row = came[:, i * BLOCK : (i + 1) * BLOCK], i * EXTRA
                if row < EXPERTS:
                    ranks_ref[row : row + EXTRA, lanes] = tile.astype(jnp.float32)
                else:
                    router_ref[first_ref[2] ^ place, row - EXPERTS : row - EXPERTS + EXTRA, :] = tile
        router_copy = pltpu.make_async_copy(router_ref, router_out.at[:, first_ref[3]], sem)
        router_copy.start()
        lane = lax.broadcasted_iota(jnp.int32, (1, slot_ref.shape[1]), 1)
        offset = (CAP * (lane // BLOCK % GROUP)).astype(jnp.float32)
        for owner in range(owners):
            ranks = ranks_ref[pl.ds(first_ref[0] + owner, 1), :]
            slot_ref[owner : owner + 1, :] = jnp.where(ranks >= 0, ranks + offset, -1.0)
        for span, place in enumerate(places):
            values = read_span(*place)
            taken = dot(pick_all(slot_ref, span), values).astype(jnp.bfloat16)
            for owner in range(owners):
                kept_ref[owner, slots_at(span), :] = taken[slots_at(owner)]
            dhs_ref[tokens_at(span), :] = contract_cols(values, s_down_ref[...])
        router_copy.wait()

    rows = kept_ref[step]
    rows_ref[0] = rows
    dh_ref[0] = contract_cols(rows, weights())


def gate_rows(first_ref, values, width):
    per_row = width // BLOCK
    rows = lax.broadcasted_iota(jnp.int32, (EXTRA, width), 0)
    groups = lax.broadcasted_iota(jnp.int32, (EXTRA, width), 1) // BLOCK
    leading = values.astype(jnp.bfloat16).astype(jnp.float32)
    total = jnp.zeros((EXTRA, width), jnp.float32)
    for owner in range(values.shape[0]):
        expert = first_ref[0] + owner
        for i, one in enumerate((leading, values - leading)):
            wide = jnp.concatenate([one[owner : owner + 1]] * per_row, axis=1)
            row = (2 * first_ref[1] + i) * (EXPERTS // per_row) + expert // per_row
            here = (rows == row) & (groups == expert % per_row)
            total = total + jnp.where(here, wide, 0.0)
    return total.astype(jnp.bfloat16)


def middle_kernel(*refs, carried):
    (first_ref, xa_ref, xb_ref, router_ref, mask_ref, slot_ref, in_ref, s_in_ref, dh_ref, dhs_ref) = refs[:10]
    (rows_ref, hidden_ref, dj_ref, da_ref, db_ref, gates_ref, dgate_ref, sh_ref, ds_ref, r_ref, z_ref, gate_ref, w_ref, w_sems) = refs[10 + carried :]
    bf16 = jnp.bfloat16
    owners = slot_ref.shape[0]
    step = pl.program_id(0)
    spans = spans_of(xa_ref, xb_ref)
    weights = streamed(in_ref, w_ref, w_sems, step, owners)

    @pl.when(step == 0)
    def _():
        for span, place in enumerate(spans):
            x = read_span(*place)
            lanes = tokens_at(span)
            mask = mask_ref[:, lanes] >= 0
            logits = jnp.where(mask, contract_cols(router_ref[...], x), NEGATIVE)
            gates = jnp.where(mask, jnp.exp(logits - jnp.max(logits, axis=0, keepdims=True)), 0.0)
            gates = gates / jnp.sum(gates, axis=0, keepdims=True)
            gates_ref[:, lanes] = gates
            expert = lax.broadcasted_iota(jnp.int32, gates.shape, 0)
            for owner in range(owners):
                own = jnp.sum(jnp.where(expert == first_ref[0] + owner, gates, 0.0), axis=0, keepdims=True)
                gate_ref[owner, slots_at(span), :] = jnp.sum(
                    jnp.where(pick(slot_ref, owner, span), own, 0.0), axis=1, keepdims=True
                )
            taken = dot(pick_all(slot_ref, span), x).astype(bf16)
            for owner in range(owners):
                r_ref[owner, slots_at(span), :] = taken[slots_at(owner)]
            joined = dot(x, s_in_ref[...])
            units = joined.shape[1] // 2
            first, second = joined[:, :units], joined[:, units:]
            sigmoid, hidden = gate_parts(first, second)
            sh_ref[lanes, :] = hidden.astype(bf16)
            back = gate_back(first, second, sigmoid, dhs_ref[lanes, :])
            ds_ref[lanes, :] = jnp.concatenate(back, axis=1).astype(bf16)

    rows = r_ref[step]
    weights_in = weights()
    joined = dot(rows, weights_in)
    units = joined.shape[1] // 2
    first, second = joined[:, :units], joined[:, units:]
    sigmoid, hidden = gate_parts(first, second)
    back = gate_back(first, second, sigmoid, gate_ref[step] * dh_ref[0])
    d_gate = jnp.sum(hidden * dh_ref[0], axis=1, keepdims=True)
    for span in range(len(spans)):
        spread = jnp.where(pick(slot_ref, step, span), d_gate[slots_at(span)], 0.0)
        dgate_ref[pl.ds(step, 1), tokens_at(span)] = jnp.sum(spread, axis=0, keepdims=True)
    d_joined = jnp.concatenate(back, axis=1).astype(bf16)
    z_ref[step] = contract_cols(d_joined, weights_in).astype(bf16)
    rows_ref[0] = rows
    hidden_ref[0] = hidden.astype(bf16)
    dj_ref[0] = d_joined

    @pl.when(step == owners - 1)
    def _():
        for span, place in enumerate(spans_of(da_ref, db_ref, BLOCK + EXTRA)):
            made = jnp.concatenate([z_ref[owner, slots_at(span), :] for owner in range(owners)], axis=0)
            total = contract_rows(pick_all(slot_ref, span), made)
            total = total + contract_cols(ds_ref[tokens_at(span), :], s_in_ref[...])
            write_span(*place, total)
            for i, at in enumerate(place[1]):
                block = span * GROUP + i
                place[0][at + BLOCK : at + BLOCK + EXTRA, :] = gate_rows(
                    first_ref, dgate_ref[:, block * BLOCK : (block + 1) * BLOCK], made.shape[1]
                )


def late_kernel(*refs, carried):
    (first_ref, hidden_ref, rows_ref, slot_ref, gates_ref, sh_ref, down_ref, s_down_ref) = refs[:8]
    (dy_ref, oa_ref, ob_ref, y_ref) = refs[8 + carried :]
    bf16 = jnp.bfloat16
    owners = slot_ref.shape[0]
    step = pl.program_id(0)
    spans = spans_of(oa_ref, ob_ref)
    partial = dot(hidden_ref[0], down_ref[0])
    rows = rows_ref[0].astype(jnp.float32)
    gates = []
    for span in range(len(spans)):
        chosen = pick(slot_ref, step, span)
        lanes = tokens_at(span)
        own = gates_ref[pl.ds(first_ref[0] + step, 1), lanes]
        gates.append(jnp.sum(jnp.where(chosen, own, 0.0), axis=1, keepdims=True))
    gate = jnp.concatenate(gates, axis=0)
    y_ref[step] = (gate * partial).astype(bf16)
    dy_ref[0] = (gate * rows).astype(bf16)

    @pl.when(step == owners - 1)
    def _():
        for span, place in enumerate(spans):
            made = jnp.concatenate([y_ref[owner, slots_at(span), :] for owner in range(owners)], axis=0)
            total = contract_rows(pick_all(slot_ref, span), made)
            total = total + dot(sh_ref[tokens_at(span), :], s_down_ref[...])
            write_span(*place, total)


ROWS = 256


def row_chunks(amount, body):
    @pl.loop(0, amount // ROWS)
    def _(i):
        body(pl.multiple_of(i * ROWS, ROWS))


def plane_copies(plane, pieces, target, sems):
    count = len(pieces)
    return [
        pltpu.make_async_copy(
            piece, target(lax.rem(plane - k + count, count)), sems.at[k]
        )
        for k, piece in enumerate(pieces)
    ]


def turn_head(values, cosine, sine):
    return values * cosine + pltpu.roll(values, values.shape[1] // 2, 1) * sine


def attend_kernel(*refs, planes, heads):
    (plane_ref, gain_ref, cos_ref, sin_ref, column_ref, row_ref) = refs[:6]
    near_out, far_out, w_pieces = refs[6], refs[7], refs[8 : 8 + planes]
    outs = refs[9 + planes : 18 + planes]
    (w_ref, x_ref, o_ref, *kept, sems) = refs[18 + planes :]
    (normed_ref, q_ref, k_ref, v_ref, mixed_ref, top_ref, total_ref) = kept
    bf16, f32 = jnp.bfloat16, jnp.float32
    plane = plane_ref[0]
    width = near_out.shape[1]
    blocks, part = w_ref.shape[0], w_ref.shape[3] // 4
    size = part // heads
    half = near_out.shape[0]
    amount = 2 * half
    copies = plane_copies(plane, w_pieces, lambda at: w_ref.at[:, at], sems.at[0])
    sides = [
        pltpu.make_async_copy(ref, x_ref.at[side], sems.at[1, side])
        for side, ref in enumerate((near_out, far_out))
    ]
    leaving = [pltpu.make_async_copy(o_ref.at[side], outs[side], sems.at[2, side]) for side in range(2)]
    leaving += [
        pltpu.make_async_copy(ref, out, sems.at[3, i])
        for i, (ref, out) in enumerate(zip(kept, outs[2:], strict=True))
    ]
    for copy in copies + sides:
        copy.start()
    for copy in copies:
        copy.wait()

    for side, base in enumerate((0, half)):
        sides[side].wait()

        def project(row, base=base, side=side):
            at = pl.ds(base + row, ROWS)
            x = x_ref[side, pl.ds(row, ROWS), :].astype(f32)
            normed = rms_scale(x, gain_ref[...]).astype(bf16)
            normed_ref[at, :] = normed
            projected = dot(normed, w_ref[:, :, :, : 3 * part].reshape(width, 3 * part))
            cosine, sine = cos_ref[at, :], sin_ref[at, :]
            for head in range(heads):
                mine = slice(head * size, (head + 1) * size)
                for target, start in ((q_ref, 0), (k_ref, part)):
                    values = projected[:, start + head * size : start + (head + 1) * size]
                    target[at, mine] = turn_head(values, cosine, sine).astype(bf16)
            v_ref[at, :] = projected[:, 2 * part :].astype(bf16)

        row_chunks(half, project)
    for copy in leaving[2:6]:
        copy.start()

    for head in range(heads):
        mine = slice(head * size, (head + 1) * size)

        def attend(row, mine=mine, head=head):
            at = pl.ds(row, ROWS)
            scores = contract_cols(q_ref[at, mine], k_ref[:, mine]) * size**-0.5
            visible = row_ref[...] <= column_ref[at, :]
            scores = jnp.where(visible, scores, NEGATIVE)
            top = jnp.max(scores, axis=1, keepdims=True)
            expo = jnp.where(visible, jnp.exp(scores - top), 0.0)
            total = jnp.sum(expo, axis=1, keepdims=True)
            top_ref[head, at, :] = top
            total_ref[head, at, :] = total
            mixed_ref[at, mine] = dot(expo.astype(bf16), v_ref[:, mine]) / total

        row_chunks(amount, attend)
    for copy in leaving[6:]:
        copy.start()

    for side, base in enumerate((0, half)):

        def project_out(row, base=base, side=side):
            mixed = mixed_ref[pl.ds(base + row, ROWS), :].astype(bf16)
            for i in range(blocks):
                weights = w_ref[i, :, :, 3 * part :].reshape(part, width // blocks)
                into = slice(i * width // blocks, (i + 1) * width // blocks)
                o_ref[side, pl.ds(row, ROWS), into] = dot(mixed, weights).astype(bf16)

        row_chunks(half, project_out)
        leaving[side].start()
    for copy in leaving:
        copy.wait()


def attend_back_kernel(*refs, planes, heads):
    (plane_ref, cos_ref, sin_ref, column_ref, row_ref) = refs[:5]
    arriving, w_pieces = refs[5:14], refs[14 : 14 + planes]
    rest = refs[15 + planes :]
    d_outs, w_grads = rest[:2], rest[2 : 2 + planes]
    (w_ref, gw_ref, dm_ref, dp_ref, dk_ref, dv_ref, o_ref, *came, sems) = rest[2 + planes :]
    (near_ref, far_ref, normed_ref, q_ref, k_ref, v_ref, mixed_ref, top_ref, total_ref) = came
    bf16, f32 = jnp.bfloat16, jnp.float32
    plane = plane_ref[0]
    width = near_ref.shape[1]
    blocks, part = w_ref.shape[0], w_ref.shape[3] // 4
    size = part // heads
    half = near_ref.shape[0]
    amount = 2 * half
    w_copies = plane_copies(plane, w_pieces, lambda at: w_ref.at[:, at], sems.at[0])
    copies = [
        pltpu.make_async_copy(source, ref, sems.at[2, i])
        for i, (source, ref) in enumerate(zip(arriving, came, strict=True))
    ]
    d_copies = [pltpu.make_async_copy(o_ref.at[side], d_outs[side], sems.at[3, side]) for side in range(2)]
    for copy in w_copies + copies[:2] + copies[3:] + copies[2:3]:
        copy.start()
    for copy in w_copies:
        copy.wait()

    for side, (base, ref) in enumerate(((0, near_ref), (half, far_ref))):
        copies[side].wait()

        def back_out(row, base=base, ref=ref):
            values = 0.0
            for i in range(blocks):
                weights = w_ref[i, :, :, 3 * part :].reshape(part, width // blocks)
                into = slice(i * width // blocks, (i + 1) * width // blocks)
                values = values + contract_cols(ref[pl.ds(row, ROWS), into], weights)
            dm_ref[pl.ds(base + row, ROWS), :] = values.astype(bf16).astype(f32)

        row_chunks(half, back_out)
    for copy in copies[3:]:
        copy.wait()
    sides = [(mixed_ref[:half, :].astype(bf16), near_ref), (mixed_ref[half:, :].astype(bf16), far_ref)]
    for i in range(blocks):
        into = slice(i * width // blocks, (i + 1) * width // blocks)
        grad = sum(contract_rows(mixed, ref[:, into]) for mixed, ref in sides)
        grad = grad.astype(bf16).reshape(planes, part // planes, width // blocks)
        gw_ref[i, :, :, 3 * part :] = grad

    for head in range(heads):
        mine = slice(head * size, (head + 1) * size)
        dk_ref[...] = jnp.zeros_like(dk_ref)
        dv_ref[...] = jnp.zeros_like(dv_ref)

        def attend_back(row, mine=mine, head=head):
            at = pl.ds(row, ROWS)
            query, key, value = q_ref[at, mine], k_ref[:, mine], v_ref[:, mine]
            d_mixed, total = dm_ref[at, mine], total_ref[head, at, :]
            grad_num = (d_mixed / total).astype(bf16)
            shift = jnp.sum(d_mixed * mixed_ref[at, mine], axis=1, keepdims=True) / total
            scores = contract_cols(query, key) * size**-0.5
            visible = row_ref[...] <= column_ref[at, :]
            scores = jnp.where(visible, scores, NEGATIVE)
            expo = jnp.where(visible, jnp.exp(scores - top_ref[head, at, :]), 0.0)
            d_score = (expo * (contract_cols(grad_num, value) - shift)).astype(bf16)
            d_query = dot(d_score, key) * size**-0.5
            dp_ref[at, mine] = turn_head(d_query, cos_ref[at, :], -sin_ref[at, :]).astype(bf16)
            dk_ref[...] += contract_rows(d_score, query)
            dv_ref[...] += contract_rows(expo.astype(bf16), grad_num)

        row_chunks(amount, attend_back)
        d_key = turn_head(dk_ref[...] * size**-0.5, cos_ref[...], -sin_ref[...])
        dp_ref[:, part + head * size : part + (head + 1) * size] = d_key.astype(bf16)
        dp_ref[:, 2 * part + head * size : 2 * part + (head + 1) * size] = dv_ref[...].astype(bf16)

    copies[2].wait()
    pieces = 4
    step, count = width // pieces, blocks // pieces
    for i in range(pieces):
        grad = contract_rows(normed_ref[:, i * step : (i + 1) * step], dp_ref[...]).astype(bf16)
        grad = grad.reshape(count, *gw_ref.shape[1:3], 3 * part)
        gw_ref[i * count : (i + 1) * count, :, :, : 3 * part] = grad
    w_back = [
        pltpu.make_async_copy(
            gw_ref.at[:, lax.rem(plane - k + planes, planes)], w_grads[k], sems.at[1, k]
        )
        for k in range(planes)
    ]
    for copy in w_back:
        copy.start()
    for side, base in enumerate((0, half)):

        def back_project(row, base=base, side=side):
            values = contract_cols(
                dp_ref[pl.ds(base + row, ROWS), :], w_ref[:, :, :, : 3 * part].reshape(width, 3 * part)
            )
            o_ref[side, pl.ds(row, ROWS), :] = values.astype(bf16)

        row_chunks(half, back_project)
        d_copies[side].start()
    for copy in w_back + d_copies:
        copy.wait()


def attend_call(kernel, small, blocks, arrays, outs, scratch, after, flops):
    far, near = pl.BlockSpec(memory_space=pltpu.HBM), pl.BlockSpec(memory_space=pltpu.VMEM)
    return pl.pallas_call(
        kernel,
        in_specs=[pl.BlockSpec(memory_space=pltpu.SMEM)]
        + [near] * len(blocks)
        + [far] * (len(arrays) + 1),
        out_specs=[far] * len(outs),
        out_shape=[jax.ShapeDtypeStruct(shape, kind) for shape, kind in outs],
        scratch_shapes=scratch,
        compiler_params=pltpu.CompilerParams(vmem_limit_bytes=VMEM),
        cost_estimate=pl.CostEstimate(flops=flops, bytes_accessed=30_000_000, transcendentals=0),
    )(small, *blocks, *arrays, after)


def attend(plane, rows, gain, tables, pieces, heads, after):
    bf16, f32 = jnp.bfloat16, jnp.float32
    half, width = rows[0].shape
    planes = len(pieces)
    n_ctx, depth, four = pieces[0].shape
    part = four // 4
    kept = [((2 * half, width), bf16)] + [((2 * half, part), bf16)] * 3
    kept += [((2 * half, part), f32)] + [((heads, 2 * half, 1), f32)] * 2
    return attend_call(
        functools.partial(attend_kernel, planes=planes, heads=heads),
        plane,
        [gain, *tables],
        [*rows, *pieces],
        [((half, width), bf16)] * 2 + kept,
        [pltpu.VMEM((n_ctx, planes, depth, four), bf16)]
        + [pltpu.VMEM((2, half, width), bf16)] * 2
        + [pltpu.VMEM(shape, kind) for shape, kind in kept]
        + [pltpu.SemaphoreType.DMA((4, max(planes, 7)))],
        after,
        4 * half * width * 4 * part + 16 * half * half * part,
    )


def attend_back(plane, rows, saved, tables, pieces, heads, after):
    bf16, f32 = jnp.bfloat16, jnp.float32
    half, width = rows[0].shape
    planes = len(pieces)
    n_ctx, depth, four = pieces[0].shape
    part = four // 4
    made = attend_call(
        functools.partial(attend_back_kernel, planes=planes, heads=heads),
        plane,
        tables,
        [*rows, *saved, *pieces],
        [((half, width), bf16)] * 2 + [(pieces[0].shape, bf16)] * planes,
        [
            pltpu.VMEM((n_ctx, planes, depth, four), bf16),
            pltpu.VMEM((n_ctx, planes, depth, four), bf16),
            pltpu.VMEM((2 * half, part), f32),
            pltpu.VMEM((2 * half, 3 * part), bf16),
            pltpu.VMEM((2 * half, part // heads), f32),
            pltpu.VMEM((2 * half, part // heads), f32),
            pltpu.VMEM((2, half, width), bf16),
            *(pltpu.VMEM(a.shape, a.dtype) for a in (*rows, *saved)),
            pltpu.SemaphoreType.DMA((4, max(planes, 9))),
        ],
        after,
        4 * half * width * 8 * part + 40 * half * half * part,
    )
    return made[:2], list(made[2:])


def rows_kernel(left_ref, right_ref, *refs):
    refs[-1][0] = contract_rows(left_ref[0], right_ref[0])


def shared_kernel(*refs, count):
    xs, gs = refs[:count], refs[count : 2 * count]
    hidden_ref, joined_ref, _, into_ref, down_ref, x_ref, g_ref, sum_ref, sems = refs[2 * count :]
    size = GROUP * BLOCK
    places = []
    for x, g in zip(xs, gs, strict=True):
        for at, (_, starts) in enumerate(spans_of(g, g, BLOCK + EXTRA)[: x.shape[0] // size]):
            places.append((x, at * size, g, starts))

    def copies(i):
        x, at, g, starts = places[i]
        slot = i % 2
        made = [pltpu.make_async_copy(x.at[pl.ds(at, size)], x_ref.at[slot], sems.at[slot, 0])]
        for n, start in enumerate(starts):
            source, target = g.at[pl.ds(start, BLOCK)], g_ref.at[slot, pl.ds(n * BLOCK, BLOCK)]
            made.append(pltpu.make_async_copy(source, target, sems.at[slot, 1 + n]))
        return made

    for copy in copies(0):
        copy.start()
    for i in range(len(places)):
        if i + 1 < len(places):
            for copy in copies(i + 1):
                copy.start()
        for copy in copies(i):
            copy.wait()
        at = slice(i * size, (i + 1) * size)
        into = contract_rows(joined_ref[at, :], x_ref[i % 2])
        down = contract_rows(hidden_ref[at, :], g_ref[i % 2])
        sum_ref[...] = into if i == 0 else sum_ref[...] + into
        down_ref[...] = down if i == 0 else down_ref[...] + down
    for at in range(0, into_ref.shape[0], size):
        into_ref[at : at + size, :] = sum_ref[:, at : at + size].T.astype(into_ref.dtype)


def held_whole(*shape):
    return pl.BlockSpec(shape, lambda j: (0,) * len(shape), pipeline_mode=pl.Buffered(1))


def expert_call(
    kernel, owners, operands, specs, outs, out_specs, kept, after, scratch, flops, moved
):
    return pl.pallas_call(
        functools.partial(kernel, carried=len(kept) + 1),
        grid=(owners,),
        in_specs=specs + [pl.BlockSpec(memory_space=pl.ANY)] * (len(kept) + 1),
        out_specs=out_specs,
        out_shape=[jax.ShapeDtypeStruct(shape, kind) for shape, kind in outs],
        scratch_shapes=scratch,
        input_output_aliases={len(operands) + i: i for i in range(len(kept))},
        compiler_params=pltpu.CompilerParams(vmem_limit_bytes=VMEM),
        cost_estimate=pl.CostEstimate(flops=flops, bytes_accessed=moved, transcendentals=0),
    )(*operands, *kept, after)


def growing(k, rows, columns):
    return pl.BlockSpec((1, rows, columns), lambda j: (j, k, 0))


def weight_buffers(array):
    depth = min(2, array.shape[0])
    return [pltpu.VMEM((depth,) + array.shape[1:], array.dtype), pltpu.SemaphoreType.DMA((depth,))]


def first_kernel(grads_ref, routes_ref, router_ref, qkv_ref, out_ref, parts_ref):
    bf16, f32 = jnp.bfloat16, jnp.float32
    amount, width = grads_ref.shape
    blocks, _, three = parts_ref.shape
    part = three // 3
    for block in range(blocks):
        for i in range(3):
            start = i * (qkv_ref.shape[1] // 3) + block * part
            parts_ref[block, :, i * part : (i + 1) * part] = qkv_ref[:, start : start + part]
    out_ref[:amount, :] = grads_ref[...]
    experts = lax.broadcasted_iota(jnp.int32, (EXPERTS, amount), 0)
    named = jnp.zeros((EXPERTS, amount), f32)
    for i in range(routes_ref.shape[0]):
        named = named + (experts == routes_ref[i : i + 1, :]).astype(f32)
    tokens = (amount, amount)
    before = lax.broadcasted_iota(jnp.int32, tokens, 0) < lax.broadcasted_iota(jnp.int32, tokens, 1)
    ranks = jnp.where(named > 0, dot(named.astype(bf16), before.astype(bf16)), -1.0).astype(bf16)
    router = jnp.concatenate(
        [router_ref[...], jnp.zeros((router_ref.shape[0], amount - EXPERTS), bf16)], axis=1
    )
    tiles = [ranks[at : at + EXTRA] for at in range(0, EXPERTS, EXTRA)]
    tiles += [router[at : at + EXTRA] for at in range(0, router.shape[0], EXTRA)]
    tiles.append(jnp.zeros((EXTRA, width - len(tiles) * amount), bf16))
    out_ref[amount:, :] = jnp.concatenate(tiles, axis=1)


def first_arrays(grads, routes, router, w_qkv, blocks):
    rows, columns = w_qkv.shape
    return pl.pallas_call(
        first_kernel,
        out_shape=[
            jax.ShapeDtypeStruct((grads.shape[0] + EXTRA, grads.shape[1]), grads.dtype),
            jax.ShapeDtypeStruct((blocks, rows, columns // blocks), w_qkv.dtype),
        ],
        compiler_params=pltpu.CompilerParams(vmem_limit_bytes=VMEM),
    )(grads, routes, router, w_qkv)


def early(k, planes, first, grads, count, w_down, s_down, kept, after):
    bf16, f32 = jnp.bfloat16, jnp.float32
    owners, units, width = w_down.shape
    half = grads[0].shape[0] * BLOCK // (BLOCK + EXTRA)
    rows, lane = 2 * half // BLOCK * CAP, s_down.shape[0]
    outs = [
        ((owners, planes * rows, width), bf16),
        ((owners, planes * rows, units), f32),
        ((2 * half // BLOCK, planes, count, BLOCK), bf16),
        ((2 * half, lane), f32),
        ((EXPERTS, 2 * half), f32),
        ((owners, 2 * half), f32),
    ]
    made = expert_call(
        early_kernel,
        owners,
        [first, *grads, w_down, s_down],
        [pl.BlockSpec(memory_space=pltpu.SMEM)]
        + [held_whole(*grads[0].shape)] * 2
        + [pl.BlockSpec(memory_space=pltpu.HBM), held_whole(*s_down.shape)],
        outs,
        [growing(k, rows, width), growing(k, rows, units), pl.BlockSpec(memory_space=pltpu.HBM)]
        + [held_whole(*shape) for shape, _ in outs[3:]],
        kept,
        after,
        [
            pltpu.VMEM((owners, rows, width), bf16),
            pltpu.VMEM((2 * half // BLOCK, count, BLOCK), bf16),
            *weight_buffers(w_down),
            pltpu.SemaphoreType.DMA(()),
        ],
        2 * owners * rows * width * (units + GROUP * BLOCK) + 4 * half * width * lane,
        2 * owners * width * (units + 2 * rows) + 4 * half * width,
    )
    return list(made[:3]), made[3:]


def middle(
    k, planes, first, rows_x, router_t, mask, slots, w_in, s_in, dh, dhs, kept, after
):
    bf16, f32 = jnp.bfloat16, jnp.float32
    owners, width, joined = w_in.shape
    half = rows_x[0].shape[0]
    rows, lane = 2 * half // BLOCK * CAP, dhs.shape[1]
    outs = [
        ((owners, planes * rows, width), bf16),
        ((owners, planes * rows, joined // 2), bf16),
        ((owners, planes * rows, joined), bf16),
        ((half // BLOCK * (BLOCK + EXTRA), width), bf16),
        ((half // BLOCK * (BLOCK + EXTRA), width), bf16),
        ((EXPERTS, 2 * half), f32),
        ((owners, 2 * half), f32),
        ((2 * half, lane), bf16),
        ((2 * half, 2 * lane), bf16),
    ]
    made = expert_call(
        middle_kernel,
        owners,
        [first, *rows_x, router_t, mask, slots, w_in, s_in, dh, dhs],
        [pl.BlockSpec(memory_space=pltpu.SMEM)]
        + [held_whole(half, width)] * 2
        + [held_whole(*a.shape) for a in (router_t, mask, slots)]
        + [pl.BlockSpec(memory_space=pltpu.HBM), held_whole(*s_in.shape), growing(k, rows, joined // 2)]
        + [held_whole(*dhs.shape)],
        outs,
        [growing(k, rows, width), growing(k, rows, joined // 2), growing(k, rows, joined)]
        + [held_whole(*shape) for shape, _ in outs[3:]],
        kept,
        after,
        [
            pltpu.VMEM((owners, rows, width), bf16),
            pltpu.VMEM((owners, rows, width), bf16),
            pltpu.VMEM((owners, rows, 1), f32),
            *weight_buffers(w_in),
        ],
        4 * owners * rows * width * (joined + GROUP * BLOCK) + 16 * half * width * lane,
        2 * owners * width * (joined + 2 * rows) + 8 * half * width,
    )
    return list(made[:3]), made[3:5], made[5:]


def late(k, planes, first, hidden, taken, slots, gates, shared, w_down, s_down, kept, after):
    bf16, f32 = jnp.bfloat16, jnp.float32
    owners, units, width = w_down.shape
    half = shared.shape[0] // 2
    rows = 2 * half // BLOCK * CAP
    outs = [
        ((owners, hidden.shape[1], width), bf16),
        ((half, width), bf16),
        ((half, width), bf16),
    ]
    made = expert_call(
        late_kernel,
        owners,
        [first, hidden, taken, slots, gates, shared, w_down, s_down],
        [pl.BlockSpec(memory_space=pltpu.SMEM), growing(k, rows, units), growing(k, rows, width)]
        + [held_whole(*a.shape) for a in (slots, gates, shared)]
        + [
            pl.BlockSpec((1, units, width), lambda j: (j, 0, 0)),
            held_whole(*s_down.shape),
        ],
        outs,
        [growing(k, rows, width)] + [held_whole(*shape) for shape, _ in outs[1:]],
        kept,
        after,
        [pltpu.VMEM((owners, rows, width), bf16)],
        2 * owners * rows * width * (units + GROUP * BLOCK) + 4 * half * width * s_down.shape[0],
        2 * owners * width * (units + 2 * rows) + 4 * half * width,
    )
    return list(made[:1]), made[1:]


def rows_grad(left, right, owner, count, kept, after):
    owners, amount, wide = left.shape
    narrow = right.shape[2]
    depth = pl.Buffered(2 if count > 1 else 1)
    at = lambda j: (owner + j, 0, 0)
    return pl.pallas_call(
        rows_kernel,
        grid=(count,),
        in_specs=[
            pl.BlockSpec((1, amount, wide), at, pipeline_mode=depth),
            pl.BlockSpec((1, amount, narrow), at, pipeline_mode=depth),
        ]
        + [pl.BlockSpec(memory_space=pl.ANY)] * (len(kept) + 1),
        out_specs=pl.BlockSpec((1, wide, narrow), at, pipeline_mode=depth),
        out_shape=jax.ShapeDtypeStruct((owners, wide, narrow), jnp.float32),
        input_output_aliases={2: 0} if kept else {},
        compiler_params=pltpu.CompilerParams(vmem_limit_bytes=VMEM),
        cost_estimate=pl.CostEstimate(
            flops=2 * count * amount * wide * narrow,
            bytes_accessed=4 * count * wide * narrow,
            transcendentals=0,
        ),
    )(left, right, *kept, after)


def last_kernel(came_ref, weights_ref, gain_ref, residual_ref, own_ref, moved_ref, rows_ref, sum_ref, out_ref):
    f32 = jnp.float32
    blocks, _, three = came_ref.shape
    part, width = three // 3, rows_ref.shape[1] // 3
    total = 0.0
    for block in range(blocks):
        for i in range(3):
            into = slice(i * width + block * part, i * width + (block + 1) * part)
            values = came_ref[block, :, i * part : (i + 1) * part].astype(f32)
            rows_ref[:, into] = values
            weighted = values * weights_ref[:, into].astype(f32)
            total = total + jnp.sum(weighted, axis=1, keepdims=True)
    sum_ref[...] = total / gain_ref[...]
    for at in range(0, out_ref.shape[0], EXTRA):
        rows = slice(at, at + EXTRA)
        added = own_ref[rows, :].astype(f32) + moved_ref[rows, :].astype(f32)
        out_ref[rows, :] = (residual_ref[rows, :] + added).astype(out_ref.dtype)


def last_outputs(came, weights, gain, residual, own, moved):
    return pl.pallas_call(
        last_kernel,
        out_shape=[
            jax.ShapeDtypeStruct(weights.shape, jnp.float32),
            jax.ShapeDtypeStruct((weights.shape[0], 1), jnp.float32),
            jax.ShapeDtypeStruct(residual.shape, jnp.bfloat16),
        ],
        compiler_params=pltpu.CompilerParams(vmem_limit_bytes=VMEM),
    )(came, weights, gain, residual, own, moved)


def shared_grads(rows_x, rows_g, hidden, joined, after):
    count, width = len(rows_x), rows_x[0].shape[1]
    bf16, f32 = jnp.bfloat16, jnp.float32
    far, near = pl.BlockSpec(memory_space=pltpu.HBM), pl.BlockSpec(memory_space=pltpu.VMEM)
    wide, size = joined.shape[1], GROUP * BLOCK
    return pl.pallas_call(
        functools.partial(shared_kernel, count=count),
        in_specs=[far] * (2 * count) + [near] * 2 + [far],
        out_specs=[near] * 2,
        out_shape=[
            jax.ShapeDtypeStruct((width, wide), bf16),
            jax.ShapeDtypeStruct((hidden.shape[1], width), f32),
        ],
        scratch_shapes=[
            pltpu.VMEM((2, size, width), bf16),
            pltpu.VMEM((2, size, width), bf16),
            pltpu.VMEM((wide, width), f32),
            pltpu.SemaphoreType.DMA((2, 1 + GROUP)),
        ],
        compiler_params=pltpu.CompilerParams(vmem_limit_bytes=VMEM),
        cost_estimate=pl.CostEstimate(
            flops=2 * hidden.shape[0] * width * (wide + hidden.shape[1]),
            bytes_accessed=4 * hidden.shape[0] * width,
            transcendentals=0,
        ),
    )(*rows_x, *rows_g, hidden, joined, after)


def local(
    tokens,
    gain_attn,
    w_qkv,
    w_out,
    gain_ffn,
    w_router,
    w_shared_in,
    w_shared_down,
    w_expert_in,
    w_expert_down,
    routes,
    plan,
    cotangent,
):
    n_ctx, planes = lax.axis_size("ctx"), lax.axis_size("fsdp")
    devices = n_ctx * planes
    ctx, plane = lax.axis_index("ctx"), lax.axis_index("fsdp")
    device = ctx * planes + plane
    amount, width = tokens.shape[1:]
    head_size = width // HEADS
    heads = HEADS // n_ctx
    part = heads * head_size
    rows = width // devices
    per_owner = w_expert_in.shape[0]
    units = w_shared_down.shape[0]
    bf16, f32 = jnp.bfloat16, jnp.float32
    order = jnp.array(plane_order(), jnp.int32)
    places = order ^ ctx

    clock = Clock()

    own_grads, qkv_part = first_arrays(cotangent[0], routes[0].T, w_router, w_qkv, n_ctx)
    qkv_part = lax.all_to_all(qkv_part, "ctx", split_axis=0, concat_axis=0, tiled=True)
    sequence = Transfer(gather_plane(tokens[0], False))
    grads = [Transfer(gather_plane(own_grads, False))]
    arrival = [0, 1, planes - 1, *range(2, planes - 1)][:planes]
    grad_blocks = [Transfer(turned(own_grads, k)) for k in arrival[1:3]]
    (qkv_part,) = stage(clock, [sequence, *grads, *grad_blocks], [qkv_part])

    out_part = w_out.reshape(rows, n_ctx, part).transpose(1, 0, 2)
    ring_w = Transfer(ring(jnp.concatenate([qkv_part, out_part], axis=2)))
    gains = jnp.concatenate([gain_attn, gain_ffn])
    gains = Transfer(exchanged(clock.now(jnp.broadcast_to(gains[None], (devices, 2 * rows)))))
    shared_in = w_shared_in.reshape(rows, 2, devices, units).transpose(2, 0, 1, 3)
    shared_in = shared_in.reshape(devices, rows, 2 * units)

    half_block = amount // 2
    half_ids = (places[:, None] * 2 + jnp.arange(2, dtype=jnp.int32)[None, :]).reshape(-1)
    placed = jnp.sum(
        jnp.where(half_ids[:, None] == jnp.arange(plan.shape[0])[None, :], plan[None, :], 0), axis=1
    )
    pos = (placed[:, None] * half_block + jnp.arange(half_block)[None, :]).reshape(-1).astype(f32)
    frequency = ROPE_BASE ** (-2.0 * jnp.arange(head_size // 2, dtype=f32) / head_size)
    angles = pos[:, None] * frequency[None, :]
    cosine, sine = jnp.cos(angles), jnp.sin(angles)
    tables = [
        jnp.concatenate([cosine, cosine], axis=1),
        jnp.concatenate([-sine, sine], axis=1),
        pos[:, None],
        pos[None, :],
    ]
    shared_in, *tables = stage(clock, [ring_w, gains, sequence, *grads], [shared_in, *tables])
    if planes > 1:
        grads.append(Transfer(gather_plane(grad_blocks[0].result, False)))
    stage(clock, [ring_w, gains, sequence, *grads])
    gain_one, gain_two = (
        gains.result[:, at : at + rows].reshape(width).astype(f32) for at in (0, rows)
    )
    seq_rows = finish(clock, sequence)[0]

    first_expert = lax.rem(device * per_owner, EXPERTS)
    first = [first_expert, device * per_owner // EXPERTS, ctx]
    back = lax.rem(plane - jnp.arange(planes, dtype=jnp.int32) + planes, planes)
    first = [jnp.stack([*first, back[k]]).astype(jnp.int32) for k in range(planes)]
    ranks, slots, dhs = {}, {}, {}

    lane = -(-units // BLOCK) * BLOCK
    s_down = jnp.pad(w_shared_down, ((0, lane - units), (0, 0)))
    early_kept = []

    def grads_stage(transfers, beside=(), work=True):
        nonlocal early_kept
        i, made = len(dhs), []
        if work and i < planes and i < len(grads) and grads[i].done:
            k = arrival[i]
            early_kept, made = early(
                k, planes, first[k], grads[i].result, rows, w_expert_down, s_down, early_kept, clock.token
            )
            ranks[k], slots[k] = made[1:]
        arrays = stage(clock, [*transfers, *grads, *grad_blocks], [*beside, *made[:1]])
        if made:
            dhs[k] = arrays[-1]
        i = len(grads)
        if 2 <= i < planes and grad_blocks[i - 1].done and grads[-1].step is not grads[-1].opening:
            grads.append(Transfer(gather_plane(grad_blocks[i - 1].result, False)))
            grads[-1].opening = grads[-1].step
            if len(grad_blocks) < planes - 1:
                source = neighbour if len(grad_blocks) == 2 else grad_blocks[-1].result
                grad_blocks.append(Transfer(turned(source)))
        return arrays[: len(beside)]

    grads[-1].opening = None
    neighbour = grad_blocks[0].result
    while not ring_w.done:
        shared_in, neighbour = grads_stage([ring_w], [shared_in, neighbour])
    pieces = ring_w.result
    shared_in = Transfer(exchanged(shared_in))
    own_rows = tokens[0].astype(f32)
    plane_id = plane.reshape(1).astype(jnp.int32)
    *attended, normed, query, key, value, mixed, tops, totals = attend(
        plane_id, seq_rows, gain_one[None, :], tables, pieces, heads, clock.token
    )
    saved = [normed, query, key, value, mixed, tops, totals]
    attended = grads_stage([], attended)
    attended = Transfer(scatter_plane(*attended))
    grads_stage([attended])
    while not (attended.done and shared_in.done):
        grads_stage([attended, shared_in])
    shared_in = shared_in.result.reshape(width, 2, units)
    s_in = jnp.pad(shared_in, ((0, 0), (0, 0), (0, lane - units))).reshape(width, 2 * lane)
    residual = own_rows + attended.result.astype(f32)
    ffn_own = rms_scale(residual, gain_two).astype(bf16)

    ffn, d_parts = [Transfer(gather_plane(ffn_own))], []
    block, d_sum = Transfer(turned(ffn_own)), None
    mid_kept, mids, late_kept, out_parts, out_sum, router_t = [], [], [], [], None, None

    def do_late():
        nonlocal late_kept
        if len(out_parts) == planes:
            return []
        k = (len(out_parts) + 1) % planes
        late_kept, pair = late(
            k, planes, first[k], mid_kept[1], early_kept[0], slots[k], mids[k][0], mids[k][2],
            w_expert_down, s_down, late_kept, clock.token,
        )
        return list(pair)

    def outs_stage(transfers, beside=(), moving=None, opening=True):
        nonlocal out_sum
        pair = do_late() if not beside else []
        if out_sum is None and len(out_parts) == planes and out_parts[0].done:
            out_sum = Transfer(staged_sum(out_parts[:-1]))
        going = [t for t in out_parts if not t.done]
        fresh = [t for t in going if t.step is t.opening]
        going = [t for t in going if t not in fresh]
        fresh = fresh if opening else []
        if moving is not None:
            going = going[:moving]
        sums = [out_sum] if out_sum else []
        arrays = stage(clock, [*transfers, *going, *fresh, *sums], [*beside, *pair])
        if pair:
            out_parts.append(Transfer(scatter_plane(*arrays)))
            out_parts[-1].opening = out_parts[-1].step
            arrays = []
        return arrays

    while d_sum is None or not d_sum.done:
        going = [*ffn, *d_parts, block, *([d_sum] if d_sum else [])]
        k = len(mids)
        if router_t is None and len(ranks) == planes:
            router_full = early_kept[2].reshape(width, amount)[:, :EXPERTS]
            router_t = router_full.T
        if k < planes and ffn[k].done and k in dhs and router_t is not None:
            mid_kept, pair, made = middle(
                k, planes, first[k], ffn[k].result, router_t, ranks[k], slots[k], w_expert_in, s_in,
                early_kept[1], dhs[k], mid_kept, clock.token,
            )
            mids.append(made)
            pair = grads_stage(going, list(pair), work=False)
            d_parts.append(Transfer(scatter_plane(*pair)))
        elif k == planes:
            outs_stage(going, moving=1 if d_parts[-1].done else 0)
        else:
            (s_in,) = grads_stage(going, [s_in])
        if len(ffn) < planes and block.done:
            ffn.append(Transfer(gather_plane(block.result)))
            if len(ffn) < planes:
                block = Transfer(turned(block.result))
        if d_sum is None and len(d_parts) == planes and d_parts[min(1, planes - 1)].done:
            d_sum = Transfer(staged_sum(d_parts[1:] + d_parts[:1]))
    rows_in, hidden, d_joined = mid_kept
    gates = mids[0][0]

    dgate = d_sum.result[amount:].astype(f32).reshape(4, EXPERTS, amount)
    dgate = jnp.sum(dgate, axis=0)
    gates_own = gates[:, :amount]
    dlogits = gates_own * (dgate - jnp.sum(gates_own * dgate, axis=0, keepdims=True))
    dlogits_b = dlogits.astype(bf16).T
    d_ffn = d_sum.result[:amount].astype(f32) + contract_cols(dlogits_b, router_full)
    second_back = jax.vjp(rms_scale, residual, gain_two)[1](d_ffn)
    d_residual = cotangent[0].astype(f32) + second_back[0]

    d_attn = Transfer(gather_plane(d_residual.astype(bf16)))
    outs_stage([d_attn], moving=0)
    while len(out_parts) < planes:
        outs_stage([], moving=1)
    shared = None
    while not d_attn.done or shared is None:
        if shared is not None:
            outs_stage([d_attn], moving=1)
            continue
        into, shared_down_grad = shared_grads(
            [side for t in ffn for side in t.result],
            [side for k in range(planes) for side in grads[arrival.index(k)].result],
            jnp.concatenate([made[2] for made in mids]),
            jnp.concatenate([made[3] for made in mids]),
            clock.token,
        )
        small = contract_rows(ffn_own, clock.now(dlogits_b)).astype(bf16)
        gain = second_back[1][:, None].astype(bf16)
        shared = jnp.concatenate([into[:, :units], into[:, lane : lane + units], small, gain], axis=1)
        shared = jnp.pad(shared, ((0, 0), (0, -shared.shape[1] % BLOCK)))
        shared = shared.reshape(devices, rows, -1)
        shared, shared_down_grad = outs_stage(
            [d_attn], [shared, shared_down_grad], moving=1, opening=False
        )
    shared = Transfer(exchanged(shared))

    d_normed, ring_grad = attend_back(
        plane_id, d_attn.result, saved, tables, pieces, heads, clock.token
    )
    d_normed = outs_stage([shared], list(d_normed), moving=1)
    ring_grad = Transfer(ring_sum([piece.reshape(-1, 4 * part) for piece in ring_grad]))
    d_normed = Transfer(scatter_plane(*d_normed))

    first_half = -(-per_owner // 2)
    (dy,) = late_kept
    work = [lambda kept: [rows_grad(rows_in, d_joined, 0, first_half, kept, clock.token)]]
    if first_half < per_owner:
        work.append(
            lambda kept: [
                rows_grad(rows_in, d_joined, first_half, per_owner - first_half, kept, clock.token)
            ]
        )
    work.append(lambda kept: [rows_grad(hidden, dy, 0, per_owner, [], clock.token)])
    made, last = [], None
    while work or not (ring_grad.done and d_normed.done):
        one = work.pop(0)(made) if work else []
        last = [out_sum.result] if not work and out_sum.done else []
        *one, last = outs_stage([ring_grad, d_normed], [*one, *last], 1) if last else [
            *outs_stage([ring_grad, d_normed], one, 1),
            None,
        ]
        if work:
            made = one
        elif one:
            (expert_in_grad,), (expert_down_grad,) = made, one
    ring_grad = add(*ring_grad.result).reshape(n_ctx, rows, 4 * part)
    qkv_grad = lax.all_to_all(ring_grad[:, :, : 3 * part], "ctx", split_axis=0, concat_axis=0, tiled=True)
    out_grad = ring_grad[:, :, 3 * part :].transpose(1, 0, 2).reshape(rows, width).astype(f32)
    first_back = jax.vjp(lambda x: rms_scale(x, gain_one), own_rows)[1](d_normed.result.astype(f32))
    tokens_grad = d_residual + first_back[0]
    shared = clock.now(shared.result)
    shared_in_grad = shared[:, :, : 2 * units].reshape(devices, rows, 2, units)
    shared_in_grad = shared_in_grad.transpose(1, 2, 0, 3).reshape(rows, 2 * devices * units).astype(f32)
    small = jnp.sum(shared[:, :, 2 * units :].astype(f32), axis=0)
    router_grad, gain_ffn_grad = small[:, :EXPERTS], small[:, EXPERTS]
    shared_down_grad = shared_down_grad[:units]
    while not (out_sum.done and out_parts[-1].done):
        stage(clock, [*out_parts, out_sum])
        last = out_sum.result
    qkv_grad, gain_attn_grad, result = last_outputs(
        qkv_grad, w_qkv, gain_attn.astype(f32)[:, None], residual, out_parts[-1].result, turn(last)
    )
    gain_attn_grad = gain_attn_grad[:, 0]
    return (
        result[None],
        tokens_grad[None],
        gain_attn_grad,
        qkv_grad,
        out_grad,
        gain_ffn_grad,
        router_grad,
        shared_in_grad,
        shared_down_grad,
        expert_in_grad,
        expert_down_grad,
    )


def solution(mesh):
    split = P(BOTH)
    matrix = P(BOTH, None)
    cube = P(BOTH, None, None)
    batch = P("fsdp", "ctx", None)
    return jax.shard_map(
        local,
        mesh=mesh,
        in_specs=(
            batch,
            split,
            matrix,
            matrix,
            split,
            matrix,
            matrix,
            matrix,
            cube,
            cube,
            batch,
            P(),
            batch,
        ),
        out_specs=(
            batch,
            batch,
            split,
            matrix,
            matrix,
            split,
            matrix,
            matrix,
            matrix,
            cube,
            cube,
        ),
        check_vma=False,
    )
```
